32 devices in a mesh: user: 16 (over z, y, core), item: 2 (over x).
Axes of the slice: x: 2, y: 2, z: 4, core: 2. Of those that a mesh axis runs over, the one named last changes fastest.
Arguments:
- user_feat: bfloat16 [32768, 512], P('user'), may hold values from -6 to 6
- cotangent: bfloat16 [32768, 512], P('user'), may hold values from -6 to 6
- gain: float32 [512], replicated, may hold values from 0.25 to 1.75
- item_feat: bfloat16 [2, 2048, 512], P('item', 'user'), may hold values from -6 to 6
- categories: int32 [2, 2048], P('item', 'user'), may hold values from 0 to 7, as said below
- expert_w: bfloat16 [8, 512, 512], P('item'), may hold values from -0.25 to 0.25
- tile_place: int32 [16, 2, 80], P('user', 'item'), may hold values from 0 to 255, as said below
- tile_level: int32 [16, 2, 80, 128, 128], P('user', 'item'), may hold values from 0 to 15
- tile_count: int32 [16, 2], P('user', 'item'), may hold values from 1 to 80, as said below
Outputs:
- user_grad: bfloat16 [32768, 512], P('user', 'item')
- item_grad: bfloat16 [2, 2048, 512], P('item', 'user')
- expert_grad: float32 [8, 512, 512], P('item', 'user')
- gain_grad: float32 [512], P('item')
The draws below stay inside these ranges and needn't reach their ends.
Inputs may be any that keep to these rules, and one draw needn't show every extreme that they name: The categories of items of item shard j lie in j * 4 to (j + 1) * 4 - 1. `tile_place`: within one device the 80 slots name distinct positions. `tile_count`: slots at or past the count are unused; some device has all 80 slots live.
All inputs are finite; a program needn't handle non-finite values.
Results may differ from the reference program's by a relative error of at most 0.0065.
Values may be sent and summed in bfloat16 or wider, within the bound.
No kernel may reach another device: no remote copies, remote signals or barrier semaphores. Data moves between devices by JAX's collectives and lax.ppermute only.
A program may use at most 128 MiB of HBM per device.

```python
import jax
import jax.numpy as jnp
from jax import lax

D = 512
TILE = 128
EXP_SHARD = 4
UT = 16
IT = 16
NT = 80
USHARDS = 16
ISHARDS = 2
EXPERTS = 8
ITEMS_SH = 2048
NU = 32768


def draw_categories(key, part):
    picks = jax.random.randint(key, (ISHARDS, ITEMS_SH), 0, EXP_SHARD)
    return (picks + jnp.arange(ISHARDS, dtype=jnp.int32)[:, None] * EXP_SHARD).astype(jnp.int32)


def draw_tile_place(key, part):
    keys = jax.random.split(key, USHARDS * ISHARDS)
    chosen = jax.vmap(lambda one_key: jax.random.permutation(one_key, UT * IT)[:NT])(keys)
    return chosen.reshape(USHARDS, ISHARDS, NT).astype(jnp.int32)


def draw_tile_count(key, part):
    first_key, second_key = jax.random.split(key)
    devices_all = USHARDS * ISHARDS
    counts = jax.random.randint(first_key, (devices_all,), max(1, NT // 8), NT // 2 + 1)
    full_one = jax.random.randint(second_key, (), 0, devices_all)
    counts = jnp.where(jnp.arange(devices_all, dtype=jnp.int32) == full_one, NT, counts)
    return counts.reshape(USHARDS, ISHARDS).astype(jnp.int32)


def set_ends(drawn, rng, least, largest):
    longest = drawn.shape.index(max(drawn.shape))
    spots = []
    for shift in (0, 1):
        where = [jax.random.randint(jax.random.fold_in(rng, axis), (), 0, length) for axis, length in enumerate(drawn.shape)]
        where[longest] = (where[longest] + shift) % drawn.shape[longest]
        spots.append(tuple(where))
    return drawn.at[spots[0]].set(least).at[spots[1]].set(largest)


def shard_levels(key, shape, cuts, low, high):
    level, own = 1.0, jax.random.fold_in(key, 6)
    for dim, shards_of in cuts:
        steps = jnp.exp(jax.random.uniform(jax.random.fold_in(own, dim), (shards_of,), jnp.float32, low / len(cuts), high / len(cuts)))
        level = level * jnp.repeat(steps, shape[dim] // shards_of).reshape([-1 if axis == dim else 1 for axis in range(len(shape))])
    return level


def gaussian(key, shape, width, limit, cuts=(), held_as=jnp.bfloat16):
    level = shard_levels(key, shape, cuts, -0.22, 0.18) if cuts else 1.0
    result = jax.random.normal(key, shape, jnp.float32) * width * level
    return jnp.minimum(jnp.maximum(result, -limit), limit).astype(held_as)


def setup_inputs(seed: int = 0) -> dict:
    key_list = jax.random.split(jax.random.key(seed), 10)
    user_feat = gaussian(key_list[0], (NU, D), 1.0, 6.0, ((0, 16),))
    cotangent = gaussian(key_list[1], (NU, D), 1.0, 6.0, ((0, 16),))
    gain = jnp.clip(1.0 + 0.15 * jax.random.normal(key_list[2], (D,), jnp.float32), 0.25, 1.75)
    item_feat = gaussian(key_list[3], (ISHARDS, ITEMS_SH, D), 1.0, 6.0, ((0, 2), (1, 16)))
    categories = draw_categories(jax.random.fold_in(key_list[9], 71), 0)
    expert_w = gaussian(key_list[5], (EXPERTS, D, D), D ** -0.5, 0.25, ((0, 2),))
    tile_place = draw_tile_place(jax.random.fold_in(key_list[9], 71), 0)
    tile_level = set_ends(jax.random.randint(key_list[7], (USHARDS, ISHARDS, NT, TILE, TILE), 0, 16), jax.random.fold_in(key_list[7], 1), 0, 15).astype(jnp.int32)
    tile_count = draw_tile_count(jax.random.fold_in(key_list[9], 71), 0)
    return dict(user_feat=user_feat, cotangent=cotangent, gain=gain, item_feat=item_feat, categories=categories, expert_w=expert_w, tile_place=tile_place, tile_level=tile_level, tile_count=tile_count)


def tile_setup(places, levels, counts):
    live_mask = (jnp.arange(NT, dtype=jnp.int32) < counts).astype(jnp.float32)
    tile_weights = levels.astype(jnp.float32) * (1.0 / (2.0 * TILE)) * live_mask[:, None, None]
    return (tile_weights, places // IT, places % IT)

def spread_items(tile_weights, row_block, col_block, queries):
    picked = jnp.take(queries.reshape(IT, TILE, D), col_block, axis=0)
    products = jnp.einsum('sij,sjd->sid', tile_weights, picked, precision=lax.Precision.HIGHEST)
    onehot = (row_block[:, None] == jnp.arange(UT, dtype=jnp.int32)[None, :]).astype(jnp.float32)
    return jnp.einsum('su,sid->uid', onehot, products, precision=lax.Precision.HIGHEST).reshape(UT * TILE, D)

def spread_users(tile_weights, row_block, col_block, grads):
    picked = jnp.take(grads.reshape(UT, TILE, D), row_block, axis=0)
    products = jnp.einsum('sij,sid->sjd', tile_weights, picked, precision=lax.Precision.HIGHEST)
    onehot = (col_block[:, None] == jnp.arange(IT, dtype=jnp.int32)[None, :]).astype(jnp.float32)
    return jnp.einsum('sc,sjd->cjd', onehot, products, precision=lax.Precision.HIGHEST).reshape(IT * TILE, D)

def reference(user_feat, cotangent, gain, item_feat, categories, expert_w, tile_place, tile_level, tile_count):
    by_shard = expert_w.reshape(ISHARDS, EXP_SHARD, D, D)
    shard_ids = jnp.arange(ISHARDS, dtype=jnp.int32)

    def project(inputs):
        item_rows, item_cats, matrices, shard_id = inputs
        acc_total = jnp.zeros((ITEMS_SH, D), jnp.float32)
        for expert in range(EXP_SHARD):
            chosen = item_cats == shard_id * EXP_SHARD + expert
            acc_total = acc_total + jnp.where(chosen[:, None], jnp.dot(item_rows, matrices[expert], preferred_element_type=jnp.float32), 0.0)
        return acc_total.astype(jnp.bfloat16)
    queries = lax.map(project, (item_feat, categories, by_shard, shard_ids)).astype(jnp.float32)
    users = user_feat.reshape(USHARDS, UT * TILE, D)
    grads = cotangent.reshape(USHARDS, UT * TILE, D)

    def per_user(running, inputs):
        item_acc, gain_acc = running
        user_rows, grad_rows, places, levels, counts = inputs

        def add_items(acc_total, pieces):
            one_place, one_level, one_count, one_query = pieces
            tile_weights, row_block, col_block = tile_setup(one_place, one_level, one_count)
            return (acc_total + spread_items(tile_weights, row_block, col_block, one_query), None)
        summed, _ = lax.scan(add_items, jnp.zeros((UT * TILE, D), jnp.float32), (places, levels, counts, queries))
        pre_norm = user_rows.astype(jnp.float32) + summed
        inv_rms = lax.rsqrt(lax.optimization_barrier(jnp.mean(pre_norm * pre_norm, axis=-1, keepdims=True)) + 1e-05)
        grad_float = grad_rows.astype(jnp.float32)
        scaled_grad = gain[None, :] * grad_float
        cross_mean = lax.optimization_barrier(jnp.mean(scaled_grad * pre_norm, axis=-1, keepdims=True))
        state_grad = (inv_rms * scaled_grad - inv_rms ** 3 * pre_norm * cross_mean).astype(jnp.bfloat16)
        gain_acc = gain_acc + lax.optimization_barrier(jnp.sum(grad_float * pre_norm * inv_rms, axis=0))
        grad_wide = state_grad.astype(jnp.float32)

        def item_terms(pieces):
            one_place, one_level, one_count = pieces
            tile_weights, row_block, col_block = tile_setup(one_place, one_level, one_count)
            return spread_users(tile_weights, row_block, col_block, grad_wide)
        item_acc = item_acc + lax.map(item_terms, (places, levels, counts))
        return ((item_acc, gain_acc), state_grad)
    initial = (jnp.zeros((ISHARDS, ITEMS_SH, D), jnp.float32), jnp.zeros((D,), jnp.float32))
    (item_acc, gain_grad), user_blocks = lax.scan(per_user, initial, (users, grads, tile_place, tile_level, tile_count))
    user_grad = user_blocks.reshape(NU, D)
    rounded = item_acc.astype(jnp.bfloat16)

    def finish(inputs):
        item_rows, item_cats, matrices, shard_id, sums_rows = inputs
        acc_total = jnp.zeros((ITEMS_SH, D), jnp.float32)
        grad_list = []
        for expert in range(EXP_SHARD):
            chosen = item_cats == shard_id * EXP_SHARD + expert
            acc_total = acc_total + jnp.where(chosen[:, None], jnp.dot(sums_rows, matrices[expert].T, preferred_element_type=jnp.float32), 0.0)
            masked = jnp.where(chosen[:, None], item_rows, jnp.zeros_like(item_rows))
            grad_list.append(jnp.dot(masked.T, sums_rows, preferred_element_type=jnp.float32))
        return (acc_total.astype(jnp.bfloat16), jnp.stack(grad_list))
    item_grad, expert_grad = lax.map(finish, (item_feat, categories, by_shard, shard_ids, rounded))
    return (user_grad, item_grad, expert_grad.reshape(EXPERTS, D, D), gain_grad)
```

```python
import functools

import jax
import jax.numpy as jnp
from jax import lax
from jax.experimental import pallas as pl
from jax.experimental.pallas import tpu as pltpu
from jax.sharding import PartitionSpec as P

TILE = 128
SLOTS_PER_STEP = 8
ROW_CHUNKS = 4


def place_tiles(item_blocks, place_ref, count_ref, level_ref, dense_ref):
    step = pl.program_id(0)

    @pl.when(step == 0)
    def _():
        dense_ref[...] = jnp.zeros_like(dense_ref)

    for offset in range(level_ref.shape[0]):
        slot = step * level_ref.shape[0] + offset

        @pl.when(slot < count_ref[0])
        def _():
            place = place_ref[slot]
            row = pl.multiple_of((place // item_blocks) * TILE, TILE)
            col = pl.multiple_of((place % item_blocks) * TILE, TILE)
            weights = level_ref[offset].astype(jnp.float32) * (1.0 / (2.0 * TILE))
            dense_ref[pl.ds(row, TILE), pl.ds(col, TILE)] = weights.astype(jnp.bfloat16)


def dense_tiles(place, count, level, users, items):
    slots = level.shape[0]
    per_step = SLOTS_PER_STEP if slots % SLOTS_PER_STEP == 0 else 1
    return pl.pallas_call(
        functools.partial(place_tiles, items // TILE),
        out_shape=jax.ShapeDtypeStruct((users, items), jnp.bfloat16),
        grid_spec=pltpu.PrefetchScalarGridSpec(
            num_scalar_prefetch=2,
            grid=(slots // per_step,),
            in_specs=[
                pl.BlockSpec((per_step, TILE, TILE), lambda step, place_ref, count_ref: (step, 0, 0))
            ],
            out_specs=pl.BlockSpec((users, items), lambda step, place_ref, count_ref: (0, 0)),
        ),
        compiler_params=pltpu.CompilerParams(
            dimension_semantics=("arbitrary",), vmem_limit_bytes=40 * 1024 * 1024
        ),
        cost_estimate=pl.CostEstimate(
            flops=slots * TILE * TILE,
            bytes_accessed=slots * TILE * TILE * 4 + users * items * 2,
            transcendentals=0,
        ),
        name="place_tiles",
    )(place, count, level)


def over_items(partial, size):
    total = None
    for shift in range(1, size):
        pairs = [(source, (source + shift) % size) for source in range(size)]
        arrived = lax.ppermute(partial, "item", pairs).astype(jnp.float32)
        total = arrived if total is None else total + arrived
    return total


def scatter_sum(terms, size):
    cores, sides = 2, 2
    layers = size // (cores * sides)
    index = lax.axis_index("user")
    core, side, layer = index % cores, (index // cores) % sides, index // (cores * sides)
    rest = terms.shape[1:]
    terms = terms.reshape((layers, sides, cores) + rest)

    def flip(value, bit):
        return lax.ppermute(value, "user", [(source, source ^ bit) for source in range(size)])

    own = lax.dynamic_index_in_dim(terms, core, 2, keepdims=False)
    away = lax.dynamic_index_in_dim(terms, 1 - core, 2, keepdims=False).astype(jnp.bfloat16)
    terms = own + flip(away, 1).astype(jnp.float32)
    own = lax.dynamic_index_in_dim(terms, side, 1, keepdims=False)
    away = lax.dynamic_index_in_dim(terms, 1 - side, 1, keepdims=False).astype(jnp.bfloat16)
    terms = own + flip(away, 2).astype(jnp.float32)
    total = lax.dynamic_index_in_dim(terms, layer, 0, keepdims=False)
    step = cores * sides
    for shift in range(1, layers):
        away = lax.dynamic_index_in_dim(terms, (layer + shift) % layers, 0, keepdims=False)
        pairs = [(source, (source + shift * step) % size) for source in range(size)]
        total = total + lax.ppermute(away.astype(jnp.bfloat16), "user", pairs).astype(jnp.float32)
    return total


def on_device(
    user_feat, cotangent, gain, item_feat, categories, expert_w, tile_place, tile_level, tile_count
):
    users, width = user_feat.shape
    user_size, item_size = lax.axis_size("user"), lax.axis_size("item")
    item_index = lax.axis_index("item")
    own_items = item_feat.shape[1]
    items = own_items * user_size
    experts_here = expert_w.shape[0]
    first_expert = item_index * experts_here
    own_cats = categories[0]

    feats = lax.all_gather(item_feat[0], "user", axis=0, tiled=True)
    all_cats = lax.all_gather(own_cats, "user", axis=0, tiled=True)
    dense = dense_tiles(tile_place[0, 0], tile_count[0], tile_level[0, 0], users, items)

    queries = jnp.zeros((items, width), jnp.float32)
    for expert in range(experts_here):
        queries = queries + jnp.where(
            (all_cats == first_expert + expert)[:, None],
            jnp.dot(feats, expert_w[expert], preferred_element_type=jnp.float32),
            0.0,
        )
    queries = queries.astype(jnp.bfloat16)

    rows = users // ROW_CHUNKS
    grads, gain_term = [], jnp.zeros((width,), jnp.float32)
    for chunk in range(ROW_CHUNKS):
        part = slice(chunk * rows, (chunk + 1) * rows)
        partial = jnp.dot(dense[part], queries, preferred_element_type=jnp.float32)
        partial = partial.astype(jnp.bfloat16)
        pre_norm = user_feat[part].astype(jnp.float32) + partial.astype(jnp.float32)
        pre_norm = pre_norm + over_items(partial, item_size)
        grad_float = cotangent[part].astype(jnp.float32)
        scaled_grad = gain[None, :] * grad_float
        inv_rms = lax.rsqrt(jnp.mean(pre_norm * pre_norm, axis=-1, keepdims=True) + 1e-05)
        cross_mean = jnp.mean(scaled_grad * pre_norm, axis=-1, keepdims=True)
        grads.append(
            (inv_rms * scaled_grad - inv_rms**3 * pre_norm * cross_mean).astype(jnp.bfloat16)
        )
        gain_term = gain_term + jnp.sum(grad_float * pre_norm * inv_rms, axis=0)
    state_grad = jnp.concatenate(grads, axis=0)
    col_width = width // item_size
    user_grad = lax.dynamic_slice_in_dim(state_grad, item_index * col_width, col_width, 1)
    gain_own = lax.dynamic_slice_in_dim(gain_term, item_index * col_width, col_width, 0)
    gain_grad = jnp.sum(lax.all_gather(gain_own, "user", axis=0), axis=0)

    item_terms = lax.dot_general(
        state_grad, dense, (((0,), (0,)), ((), ())), preferred_element_type=jnp.float32
    )
    own_width = width // user_size
    sums = scatter_sum(item_terms.reshape(user_size, own_width, items), user_size)
    sums = sums.astype(jnp.bfloat16)

    chosen = all_cats[None, :] == first_expert + jnp.arange(experts_here, dtype=jnp.int32)[:, None]
    masked = jnp.where(chosen[:, None, :], sums[None], jnp.zeros_like(sums)[None])
    expert_cols = lax.dot_general(
        feats,
        masked.reshape(experts_here * own_width, items),
        (((0,), (1,)), ((), ())),
        preferred_element_type=jnp.float32,
    )
    swapped = lax.all_to_all(
        expert_cols.reshape(user_size, own_width, experts_here * own_width), "user", 0, 0
    )
    expert_grad = (
        swapped.reshape(user_size, own_width, experts_here, own_width)
        .transpose(2, 1, 0, 3)
        .reshape(experts_here, own_width, width)
    )

    by_item = sums.reshape(own_width, user_size, own_items).transpose(1, 0, 2)
    own_sums = lax.all_to_all(by_item, "user", 0, 0).reshape(width, own_items)
    item_total = jnp.zeros((own_items, width), jnp.float32)
    for expert in range(experts_here):
        item_total = item_total + jnp.where(
            (own_cats == first_expert + expert)[:, None],
            lax.dot_general(
                own_sums,
                expert_w[expert],
                (((0,), (1,)), ((), ())),
                preferred_element_type=jnp.float32,
            ),
            0.0,
        )
    return (user_grad, item_total.astype(jnp.bfloat16)[None], expert_grad, gain_grad)


def solution(mesh):
    placed = (
        P("user", None),
        P("user", None),
        P(),
        P("item", "user", None),
        P("item", "user"),
        P("item", None, None),
        P("user", "item", None),
        P("user", "item", None, None, None),
        P("user", "item"),
    )
    return jax.shard_map(
        on_device,
        mesh=mesh,
        in_specs=placed,
        out_specs=(P("user", "item"), P("item", "user", None), P("item", "user", None), P("item")),
        check_vma=False,
    )
```

```python
import functools

import jax
import jax.numpy as jnp
from jax import lax
from jax.experimental import pallas as pl
from jax.experimental.pallas import tpu as pltpu
from jax.sharding import PartitionSpec as P

TILE = 128
SLOTS_PER_STEP = 8
HALVES = 2
ROW_CHUNKS = 4
BLOCK_ROWS = 256
MIB = 1024 * 1024


def place_tiles(item_blocks, place_ref, count_ref, level_ref, dense_ref):
    step = pl.program_id(0)

    @pl.when(step == 0)
    def _():
        dense_ref[...] = jnp.zeros_like(dense_ref)

    for offset in range(level_ref.shape[0]):
        slot = step * level_ref.shape[0] + offset

        @pl.when(slot < count_ref[0])
        def _():
            place = place_ref[slot]
            row = pl.multiple_of((place // item_blocks) * TILE, TILE)
            col = pl.multiple_of((place % item_blocks) * TILE, TILE)
            weights = level_ref[offset].astype(jnp.float32) * (1.0 / (2.0 * TILE))
            dense_ref[pl.ds(row, TILE), pl.ds(col, TILE)] = weights.astype(jnp.bfloat16)


def dense_tiles(place, count, level, users, items):
    slots = level.shape[0]
    per_step = SLOTS_PER_STEP if slots % SLOTS_PER_STEP == 0 else 1
    return pl.pallas_call(
        functools.partial(place_tiles, items // TILE),
        out_shape=jax.ShapeDtypeStruct((users, items), jnp.bfloat16),
        grid_spec=pltpu.PrefetchScalarGridSpec(
            num_scalar_prefetch=2,
            grid=(slots // per_step,),
            in_specs=[
                pl.BlockSpec((per_step, TILE, TILE), lambda step, place_ref, count_ref: (step, 0, 0))
            ],
            out_specs=pl.BlockSpec((users, items), lambda step, place_ref, count_ref: (0, 0)),
        ),
        compiler_params=pltpu.CompilerParams(
            dimension_semantics=("arbitrary",), vmem_limit_bytes=40 * MIB
        ),
        cost_estimate=pl.CostEstimate(
            flops=slots * TILE * TILE,
            bytes_accessed=slots * TILE * TILE * 4 + users * items * 2,
            transcendentals=0,
        ),
        name="place_tiles",
    )(place, count, level)


def project_own(first_ref, cats_ref, feat_ref, weight_ref, *rest):
    out_refs, total_ref = rest[:-1], rest[-1]
    expert = pl.program_id(0)
    own = feat_ref.shape[0]
    on_diagonal = lax.broadcasted_iota(jnp.int32, (own, own), 0) == lax.broadcasted_iota(
        jnp.int32, (own, own), 1
    )
    cats = jnp.sum(
        jnp.where(on_diagonal, cats_ref[...].astype(jnp.float32), 0.0), axis=1, keepdims=True
    )
    chosen = cats == (first_ref[0] + expert).astype(jnp.float32)
    part = jnp.dot(feat_ref[...], weight_ref[0], preferred_element_type=jnp.float32)
    part = jnp.where(chosen, part, 0.0)

    @pl.when(expert == 0)
    def _():
        total_ref[...] = part

    @pl.when(expert > 0)
    def _():
        total_ref[...] += part

    @pl.when(expert == pl.num_programs(0) - 1)
    def _():
        cols = out_refs[0].shape[1]
        for half, out_ref in enumerate(out_refs):
            out_ref[...] = total_ref[:, half * cols : (half + 1) * cols].astype(out_ref.dtype)


def own_queries(first_expert, cats, feat, weights):
    own, width = feat.shape
    experts = weights.shape[0]
    half = jax.ShapeDtypeStruct((own, width // HALVES), jnp.bfloat16)
    half_spec = pl.BlockSpec((own, width // HALVES), lambda expert, first_ref: (0, 0))
    return pl.pallas_call(
        project_own,
        out_shape=[half] * HALVES,
        grid_spec=pltpu.PrefetchScalarGridSpec(
            num_scalar_prefetch=1,
            grid=(experts,),
            in_specs=[
                pl.BlockSpec((1, own), lambda expert, first_ref: (0, 0)),
                pl.BlockSpec((own, width), lambda expert, first_ref: (0, 0)),
                pl.BlockSpec((1, width, width), lambda expert, first_ref: (expert, 0, 0)),
            ],
            out_specs=[half_spec] * HALVES,
            scratch_shapes=[pltpu.VMEM((own, width), jnp.float32)],
        ),
        compiler_params=pltpu.CompilerParams(dimension_semantics=("arbitrary",)),
        cost_estimate=pl.CostEstimate(
            flops=2 * own * width * width * experts,
            bytes_accessed=weights.size * 2 + own * width * 4,
            transcendentals=0,
        ),
        name="own_queries",
    )(first_expert.reshape(1), cats.reshape(1, own), feat, weights)


def spread(blocks, order_ref, *rest):
    query_refs, dense_ref, out_ref = rest[:blocks], rest[blocks], rest[blocks + 1]
    all_ref, sems = rest[blocks + 2 :]
    own = query_refs[0].shape[0]

    @pl.when(pl.program_id(0) == 0)
    def _():
        copies = []
        for place, query_ref in enumerate(query_refs):
            start = pl.multiple_of(order_ref[place] * own, own)
            copy = pltpu.make_async_copy(query_ref, all_ref.at[pl.ds(start, own)], sems.at[place])
            copy.start()
            copies.append(copy)
        for copy in copies:
            copy.wait()

    out_ref[...] = jnp.dot(
        dense_ref[...], all_ref[...], preferred_element_type=jnp.float32
    ).astype(out_ref.dtype)


def spread_items(order, queries, dense, first, rows):
    items = dense.shape[1]
    own, cols = queries[0].shape
    blocks = len(queries)
    block_rows = min(BLOCK_ROWS, rows)
    first_block = first // block_rows
    return pl.pallas_call(
        functools.partial(spread, blocks),
        out_shape=jax.ShapeDtypeStruct((rows, cols), jnp.bfloat16),
        grid_spec=pltpu.PrefetchScalarGridSpec(
            num_scalar_prefetch=1,
            grid=(rows // block_rows,),
            in_specs=[pl.BlockSpec(memory_space=pl.ANY)] * blocks
            + [pl.BlockSpec((block_rows, items), lambda step, order_ref: (first_block + step, 0))],
            out_specs=pl.BlockSpec((block_rows, cols), lambda step, order_ref: (step, 0)),
            scratch_shapes=[
                pltpu.VMEM((items, cols), jnp.bfloat16),
                pltpu.SemaphoreType.DMA((blocks,)),
            ],
        ),
        compiler_params=pltpu.CompilerParams(
            dimension_semantics=("arbitrary",), vmem_limit_bytes=24 * MIB
        ),
        cost_estimate=pl.CostEstimate(
            flops=2 * rows * items * cols,
            bytes_accessed=rows * items * 2 + items * cols * 2 + rows * cols * 2,
            transcendentals=0,
        ),
        name="spread_items",
    )(order, *queries, dense)


def norm_backward(pieces, user_ref, grad_ref, gain_ref, *rest):
    piece_refs, out_ref, term_ref = rest[: pieces * HALVES], rest[-2], rest[-1]
    summed = []
    for half in range(HALVES):
        total = piece_refs[half * pieces][...].astype(jnp.float32)
        for piece in range(1, pieces):
            total = total + piece_refs[half * pieces + piece][...].astype(jnp.float32)
        summed.append(total)
    width = out_ref.shape[1]
    pre_norm = user_ref[...].astype(jnp.float32) + jnp.concatenate(summed, axis=1)
    grad = grad_ref[...].astype(jnp.float32)
    scaled_grad = gain_ref[...] * grad
    inv_rms = lax.rsqrt(jnp.sum(pre_norm * pre_norm, axis=1, keepdims=True) / width + 1e-05)
    cross_mean = jnp.sum(scaled_grad * pre_norm, axis=1, keepdims=True) / width
    out_ref[...] = (
        inv_rms * scaled_grad - pre_norm * (inv_rms * inv_rms * inv_rms * cross_mean)
    ).astype(out_ref.dtype)
    term = jnp.sum(grad * pre_norm * inv_rms, axis=0, keepdims=True)

    @pl.when(pl.program_id(0) == 0)
    def _():
        term_ref[...] = term

    @pl.when(pl.program_id(0) > 0)
    def _():
        term_ref[...] += term


def user_gradient(user_feat, cotangent, gain, pieces, first, rows):
    width = user_feat.shape[1]
    block_rows = min(BLOCK_ROWS, rows)
    first_block = first // block_rows
    flat = [piece for half in pieces for piece in half]
    whole = pl.BlockSpec((block_rows, width), lambda step: (first_block + step, 0))
    part = pl.BlockSpec((block_rows, width // HALVES), lambda step: (step, 0))
    return pl.pallas_call(
        functools.partial(norm_backward, len(pieces[0])),
        out_shape=[
            jax.ShapeDtypeStruct((rows, width), jnp.bfloat16),
            jax.ShapeDtypeStruct((1, width), jnp.float32),
        ],
        grid=(rows // block_rows,),
        in_specs=[whole, whole, pl.BlockSpec((1, width), lambda step: (0, 0))] + [part] * len(flat),
        out_specs=[
            pl.BlockSpec((block_rows, width), lambda step: (step, 0)),
            pl.BlockSpec((1, width), lambda step: (0, 0)),
        ],
        compiler_params=pltpu.CompilerParams(
            dimension_semantics=("arbitrary",), vmem_limit_bytes=24 * MIB
        ),
        cost_estimate=pl.CostEstimate(
            flops=16 * rows * width,
            bytes_accessed=rows * width * 2 * (3 + len(pieces[0])),
            transcendentals=rows,
        ),
        name="user_gradient",
    )(user_feat, cotangent, gain.reshape(1, width), *flat)


def flip(value, size, bits):
    return lax.ppermute(value, "user", [(source, source ^ bits) for source in range(size)])


def gather_parts(own, size):
    same_core = [own] + [flip(own, size, 2 * chip) for chip in range(1, size // 2)]
    parts = [None] * size
    for chip, part in enumerate(same_core):
        parts[2 * chip] = part
        parts[2 * chip + 1] = flip(part, size, 1)
    return parts


def scatter_sum(terms, size):
    cores, sides = 2, 2
    layers = size // (cores * sides)
    index = lax.axis_index("user")
    core, side, layer = index % cores, (index // cores) % sides, index // (cores * sides)
    rest = terms.shape[1:]
    terms = terms.reshape((layers, sides, cores) + rest)
    own = lax.dynamic_index_in_dim(terms, core, 2, keepdims=False)
    away = lax.dynamic_index_in_dim(terms, 1 - core, 2, keepdims=False).astype(jnp.bfloat16)
    terms = own + flip(away, size, 1).astype(jnp.float32)
    own = lax.dynamic_index_in_dim(terms, side, 1, keepdims=False)
    away = lax.dynamic_index_in_dim(terms, 1 - side, 1, keepdims=False).astype(jnp.bfloat16)
    terms = own + flip(away, size, 2).astype(jnp.float32)
    total = lax.dynamic_index_in_dim(terms, layer, 0, keepdims=False)
    for other in range(1, layers):
        away = lax.dynamic_index_in_dim(terms, layer ^ other, 0, keepdims=False)
        arrived = flip(away.astype(jnp.bfloat16), size, other * cores * sides)
        total = total + arrived.astype(jnp.float32)
    return total


def as_rows(value, size):
    count = value.shape[1]
    padded = -(-count // TILE) * TILE
    return jnp.pad(value, ((0, 0), (0, padded - count))).reshape(size, padded // TILE, TILE)


def on_device(
    user_feat, cotangent, gain, item_feat, categories, expert_w, tile_place, tile_level, tile_count
):
    users, width = user_feat.shape
    user_size, item_size = lax.axis_size("user"), lax.axis_size("item")
    user_index, item_index = lax.axis_index("user"), lax.axis_index("item")
    own_items = item_feat.shape[1]
    items = own_items * user_size
    experts_here = expert_w.shape[0]
    first_expert = item_index * experts_here
    own_cats, own_feat = categories[0], item_feat[0]
    rows, half_width = users // ROW_CHUNKS, width // HALVES

    own_halves = own_queries(first_expert, own_cats, own_feat, expert_w)
    order = user_index ^ jnp.arange(user_size, dtype=jnp.int32)
    queries = [gather_parts(own, user_size) for own in own_halves]
    dense = dense_tiles(tile_place[0, 0], tile_count[0], tile_level[0, 0], users, items)

    local_cats = (own_cats - first_expert).astype(jnp.bfloat16)
    packed = jnp.concatenate(
        [own_feat, jnp.broadcast_to(local_cats[:, None], (own_items, TILE))], axis=1
    )
    packed, _ = lax.optimization_barrier((packed, queries[-1][-1]))
    packed = lax.all_gather(packed, "user", axis=0, tiled=True)
    feats, all_cats = packed[:, :width], packed[:, width].astype(jnp.int32)

    partials = [[None] * ROW_CHUNKS for _ in range(HALVES)]
    for half in range(HALVES):
        for chunk in range(ROW_CHUNKS):
            partial = spread_items(order, queries[half], dense, chunk * rows, rows)
            pieces = [partial]
            for shift in range(1, item_size):
                pairs = [(source, (source + shift) % item_size) for source in range(item_size)]
                pieces.append(lax.ppermute(partial, "item", pairs))
            partials[half][chunk] = pieces

    grads, gain_term, item_terms = [], 0.0, 0.0
    for chunk in range(ROW_CHUNKS):
        grad, term = user_gradient(
            user_feat,
            cotangent,
            gain,
            [partials[half][chunk] for half in range(HALVES)],
            chunk * rows,
            rows,
        )
        grads.append(grad)
        gain_term = gain_term + term[0]
        if chunk < ROW_CHUNKS - 1:
            item_terms = item_terms + lax.dot_general(
                grad,
                dense[chunk * rows : (chunk + 1) * rows],
                (((0,), (0,)), ((), ())),
                preferred_element_type=jnp.float32,
            )
    own_width = width // user_size
    part_width = own_width // HALVES
    sums = []
    for half in range(HALVES):
        part = slice(half * half_width, (half + 1) * half_width)
        terms = item_terms[part] + lax.dot_general(
            grads[-1][:, part],
            dense[users - rows :],
            (((0,), (0,)), ((), ())),
            preferred_element_type=jnp.float32,
        )
        terms = terms.reshape(user_size, part_width, items)
        sums.append(scatter_sum(terms, user_size).astype(jnp.bfloat16))
    sums = jnp.concatenate(sums, axis=0)

    col_width = width // item_size
    user_grad = jnp.concatenate(
        [lax.dynamic_slice_in_dim(grad, item_index * col_width, col_width, 1) for grad in grads],
        axis=0,
    )
    gain_own = lax.dynamic_slice_in_dim(gain_term, item_index * col_width, col_width, 0)

    chosen = all_cats[None, :] == jnp.arange(experts_here, dtype=jnp.int32)[:, None]
    masked = jnp.where(chosen[:, None, :], sums[None], jnp.zeros_like(sums)[None])
    expert_cols = lax.dot_general(
        feats,
        masked.reshape(experts_here * own_width, items),
        (((0,), (1,)), ((), ())),
        preferred_element_type=jnp.float32,
    ).astype(jnp.bfloat16)
    by_item = sums.reshape(own_width, user_size, own_items).transpose(1, 0, 2)
    gain_sent = jnp.broadcast_to(gain_own.astype(jnp.bfloat16)[None], (user_size, col_width))
    pieces = [
        as_rows(by_item.reshape(user_size, -1), user_size),
        as_rows(expert_cols.reshape(user_size, -1), user_size),
        as_rows(gain_sent, user_size),
    ]
    swapped = lax.all_to_all(jnp.concatenate(pieces, axis=1), "user", 0, 0)
    ends = [pieces[0].shape[1], pieces[0].shape[1] + pieces[1].shape[1]]

    own_sums = (
        swapped[:, : ends[0]]
        .reshape(user_size, HALVES, part_width, own_items)
        .transpose(1, 0, 2, 3)
        .reshape(width, own_items)
    )
    expert_grad = (
        swapped[:, ends[0] : ends[1]]
        .reshape(user_size, own_width, experts_here, HALVES, part_width)
        .transpose(2, 1, 3, 0, 4)
        .reshape(experts_here, own_width, width)
        .astype(jnp.float32)
    )
    gain_grad = jnp.sum(
        swapped[:, ends[1] :].reshape(user_size, -1)[:, :col_width].astype(jnp.float32), axis=0
    )
    item_total = jnp.zeros((own_items, width), jnp.float32)
    for expert in range(experts_here):
        item_total = item_total + jnp.where(
            (own_cats == first_expert + expert)[:, None],
            lax.dot_general(
                own_sums,
                expert_w[expert],
                (((0,), (1,)), ((), ())),
                preferred_element_type=jnp.float32,
            ),
            0.0,
        )
    return (user_grad, item_total.astype(jnp.bfloat16)[None], expert_grad, gain_grad)


def solution(mesh):
    placed = (
        P("user", None),
        P("user", None),
        P(),
        P("item", "user", None),
        P("item", "user"),
        P("item", None, None),
        P("user", "item", None),
        P("user", "item", None, None, None),
        P("user", "item"),
    )
    return jax.shard_map(
        on_device,
        mesh=mesh,
        in_specs=placed,
        out_specs=(P("user", "item"), P("item", "user", None), P("item", "user", None), P("item")),
        check_vma=False,
    )
```

```python
import functools

import jax
import jax.numpy as jnp
from jax import lax
from jax.experimental import pallas as pl
from jax.experimental.pallas import tpu as pltpu
from jax.sharding import PartitionSpec as P

TILE = 128
SLOTS_PER_STEP = 8
HALVES = 2
ROW_CHUNKS = 4
BLOCK_ROWS = 256
MIB = 1024 * 1024


def place_tiles(item_blocks, place_ref, count_ref, level_ref, dense_ref):
    step = pl.program_id(0)

    @pl.when(step == 0)
    def _():
        dense_ref[...] = jnp.zeros_like(dense_ref)

    for offset in range(level_ref.shape[0]):
        slot = step * level_ref.shape[0] + offset

        @pl.when(slot < count_ref[0])
        def _():
            place = place_ref[slot]
            row = pl.multiple_of((place // item_blocks) * TILE, TILE)
            col = pl.multiple_of((place % item_blocks) * TILE, TILE)
            weights = level_ref[offset].astype(jnp.float32) * (1.0 / (2.0 * TILE))
            dense_ref[pl.ds(row, TILE), pl.ds(col, TILE)] = weights.astype(jnp.bfloat16)


def dense_tiles(place, count, level, users, items):
    slots = level.shape[0]
    per_step = SLOTS_PER_STEP if slots % SLOTS_PER_STEP == 0 else 1
    return pl.pallas_call(
        functools.partial(place_tiles, items // TILE),
        out_shape=jax.ShapeDtypeStruct((users, items), jnp.bfloat16),
        grid_spec=pltpu.PrefetchScalarGridSpec(
            num_scalar_prefetch=2,
            grid=(slots // per_step,),
            in_specs=[
                pl.BlockSpec((per_step, TILE, TILE), lambda step, place_ref, count_ref: (step, 0, 0))
            ],
            out_specs=pl.BlockSpec((users, items), lambda step, place_ref, count_ref: (0, 0)),
        ),
        compiler_params=pltpu.CompilerParams(
            dimension_semantics=("arbitrary",), vmem_limit_bytes=40 * MIB
        ),
        cost_estimate=pl.CostEstimate(
            flops=slots * TILE * TILE,
            bytes_accessed=slots * TILE * TILE * 4 + users * items * 2,
            transcendentals=0,
        ),
        name="place_tiles",
    )(place, count, level)


def project_own(first_ref, cats_ref, feat_ref, weight_ref, *rest):
    out_refs, total_ref = rest[:-1], rest[-1]
    expert = pl.program_id(0)
    own = feat_ref.shape[0]
    on_diagonal = lax.broadcasted_iota(jnp.int32, (own, own), 0) == lax.broadcasted_iota(
        jnp.int32, (own, own), 1
    )
    cats = jnp.sum(
        jnp.where(on_diagonal, cats_ref[...].astype(jnp.float32), 0.0), axis=1, keepdims=True
    )
    chosen = cats == (first_ref[0] + expert).astype(jnp.float32)
    part = jnp.dot(feat_ref[...], weight_ref[0], preferred_element_type=jnp.float32)
    part = jnp.where(chosen, part, 0.0)

    @pl.when(expert == 0)
    def _():
        total_ref[...] = part

    @pl.when(expert > 0)
    def _():
        total_ref[...] += part

    @pl.when(expert == pl.num_programs(0) - 1)
    def _():
        cols = out_refs[0].shape[1]
        for half, out_ref in enumerate(out_refs):
            out_ref[...] = total_ref[:, half * cols : (half + 1) * cols].astype(out_ref.dtype)


def own_queries(first_expert, cats, feat, weights):
    own, width = feat.shape
    experts = weights.shape[0]
    half = jax.ShapeDtypeStruct((own, width // HALVES), jnp.bfloat16)
    half_spec = pl.BlockSpec((own, width // HALVES), lambda expert, first_ref: (0, 0))
    return pl.pallas_call(
        project_own,
        out_shape=[half] * HALVES,
        grid_spec=pltpu.PrefetchScalarGridSpec(
            num_scalar_prefetch=1,
            grid=(experts,),
            in_specs=[
                pl.BlockSpec((1, own), lambda expert, first_ref: (0, 0)),
                pl.BlockSpec((own, width), lambda expert, first_ref: (0, 0)),
                pl.BlockSpec((1, width, width), lambda expert, first_ref: (expert, 0, 0)),
            ],
            out_specs=[half_spec] * HALVES,
            scratch_shapes=[pltpu.VMEM((own, width), jnp.float32)],
        ),
        compiler_params=pltpu.CompilerParams(dimension_semantics=("arbitrary",)),
        cost_estimate=pl.CostEstimate(
            flops=2 * own * width * width * experts,
            bytes_accessed=weights.size * 2 + own * width * 4,
            transcendentals=0,
        ),
        name="own_queries",
    )(first_expert.reshape(1), cats.reshape(1, own), feat, weights)


def fetch_in_order(order_ref, sources, all_ref, sems):
    per_source = len(sems) // len(sources)
    own = sources[0].shape[0] // per_source
    copies = []
    for place in range(len(sems)):
        source = sources[place // per_source].at[pl.ds((place % per_source) * own, own)]
        start = pl.multiple_of(order_ref[place] * own, own)
        copy = pltpu.make_async_copy(source, all_ref.at[pl.ds(start, own)], sems[place])
        copy.start()
        copies.append(copy)
    for copy in copies:
        copy.wait()


def spread(blocks, order_ref, same_ref, other_ref, dense_ref, *rest):
    out_refs, all_ref, sems = rest[:-2], rest[-2], rest[-1]
    step = pl.program_id(0)

    @pl.when(step == 0)
    def _():
        fetch_in_order(
            order_ref, (same_ref, other_ref), all_ref, [sems.at[place] for place in range(blocks)]
        )

    product = jnp.dot(dense_ref[...], all_ref[...], preferred_element_type=jnp.float32)
    for chunk, out_ref in enumerate(out_refs):

        @pl.when(step == chunk)
        def _():
            out_ref[...] = product.astype(out_ref.dtype)


def spread_items(order, queries, dense, first, chunks, rows):
    items = dense.shape[1]
    cols = queries[0].shape[1]
    blocks = order.shape[0]
    return pl.pallas_call(
        functools.partial(spread, blocks),
        out_shape=[jax.ShapeDtypeStruct((rows, cols), jnp.bfloat16)] * chunks,
        grid_spec=pltpu.PrefetchScalarGridSpec(
            num_scalar_prefetch=1,
            grid=(chunks,),
            in_specs=[pl.BlockSpec(memory_space=pl.ANY)] * 2
            + [pl.BlockSpec((rows, items), lambda step, order_ref: (first + step, 0))],
            out_specs=[pl.BlockSpec((rows, cols), lambda step, order_ref: (0, 0))] * chunks,
            scratch_shapes=[
                pltpu.VMEM((items, cols), jnp.bfloat16),
                pltpu.SemaphoreType.DMA((blocks,)),
            ],
        ),
        compiler_params=pltpu.CompilerParams(
            dimension_semantics=("arbitrary",), vmem_limit_bytes=24 * MIB
        ),
        cost_estimate=pl.CostEstimate(
            flops=2 * chunks * rows * items * cols,
            bytes_accessed=chunks * rows * (items + cols) * 2 + items * cols * 2,
            transcendentals=0,
        ),
        name="spread_items",
    )(order, *queries, dense)


def order_items(blocks, order_ref, same_ref, other_ref, feat_ref, mask_ref, all_ref, sems):
    fetch_in_order(
        order_ref, (same_ref, other_ref), all_ref, [sems.at[place] for place in range(blocks)]
    )
    width = feat_ref.shape[1]
    experts, own_width = mask_ref.shape[0], mask_ref.shape[1]
    feat_ref[...] = all_ref[:, :width]
    for start in range(0, feat_ref.shape[0], TILE):
        cats = all_ref[pl.ds(start, TILE), pl.ds(width, TILE)].astype(jnp.float32)
        cats = jnp.transpose(cats)[:own_width]
        for expert in range(experts):
            mask_ref[expert, :, pl.ds(start, TILE)] = (cats == expert).astype(mask_ref.dtype)


def ordered_items(order, packed, experts, own_width, width):
    items, blocks = 2 * packed[0].shape[0], order.shape[0]
    return pl.pallas_call(
        functools.partial(order_items, blocks),
        out_shape=[
            jax.ShapeDtypeStruct((items, width), jnp.bfloat16),
            jax.ShapeDtypeStruct((experts, own_width, items), jnp.bfloat16),
        ],
        grid_spec=pltpu.PrefetchScalarGridSpec(
            num_scalar_prefetch=1,
            grid=(1,),
            in_specs=[pl.BlockSpec(memory_space=pl.ANY)] * 2,
            out_specs=[
                pl.BlockSpec((items, width), lambda step, order_ref: (0, 0)),
                pl.BlockSpec((experts, own_width, items), lambda step, order_ref: (0, 0, 0)),
            ],
            scratch_shapes=[
                pltpu.VMEM((items, packed[0].shape[1]), jnp.bfloat16),
                pltpu.SemaphoreType.DMA((blocks,)),
            ],
        ),
        compiler_params=pltpu.CompilerParams(
            dimension_semantics=("arbitrary",), vmem_limit_bytes=24 * MIB
        ),
        cost_estimate=pl.CostEstimate(
            flops=0, bytes_accessed=items * width * 6, transcendentals=0
        ),
        name="order_items",
    )(order, *packed)


def norm_backward(pieces, user_ref, grad_ref, gain_ref, *rest):
    piece_refs, out_ref, term_ref = rest[: pieces * HALVES], rest[-2], rest[-1]
    summed = []
    for half in range(HALVES):
        total = piece_refs[half * pieces][...].astype(jnp.float32)
        for piece in range(1, pieces):
            total = total + piece_refs[half * pieces + piece][...].astype(jnp.float32)
        summed.append(total)
    width = out_ref.shape[1]
    pre_norm = user_ref[...].astype(jnp.float32) + jnp.concatenate(summed, axis=1)
    grad = grad_ref[...].astype(jnp.float32)
    scaled_grad = gain_ref[...] * grad
    inv_rms = lax.rsqrt(jnp.sum(pre_norm * pre_norm, axis=1, keepdims=True) / width + 1e-05)
    cross_mean = jnp.sum(scaled_grad * pre_norm, axis=1, keepdims=True) / width
    out_ref[...] = (
        inv_rms * scaled_grad - pre_norm * (inv_rms * inv_rms * inv_rms * cross_mean)
    ).astype(out_ref.dtype)
    term = jnp.sum(grad * pre_norm * inv_rms, axis=0, keepdims=True)

    @pl.when(pl.program_id(0) == 0)
    def _():
        term_ref[...] = term

    @pl.when(pl.program_id(0) > 0)
    def _():
        term_ref[...] += term


def user_gradient(user_feat, cotangent, gain, pieces, first, rows):
    width = user_feat.shape[1]
    block_rows = min(BLOCK_ROWS, rows)
    first_block = first // block_rows
    flat = [piece for half in pieces for piece in half]
    whole = pl.BlockSpec((block_rows, width), lambda step: (first_block + step, 0))
    part = pl.BlockSpec((block_rows, width // HALVES), lambda step: (step, 0))
    return pl.pallas_call(
        functools.partial(norm_backward, len(pieces[0])),
        out_shape=[
            jax.ShapeDtypeStruct((rows, width), jnp.bfloat16),
            jax.ShapeDtypeStruct((1, width), jnp.float32),
        ],
        grid=(rows // block_rows,),
        in_specs=[whole, whole, pl.BlockSpec((1, width), lambda step: (0, 0))] + [part] * len(flat),
        out_specs=[
            pl.BlockSpec((block_rows, width), lambda step: (step, 0)),
            pl.BlockSpec((1, width), lambda step: (0, 0)),
        ],
        compiler_params=pltpu.CompilerParams(
            dimension_semantics=("arbitrary",), vmem_limit_bytes=24 * MIB
        ),
        cost_estimate=pl.CostEstimate(
            flops=16 * rows * width,
            bytes_accessed=rows * width * 2 * (3 + len(pieces[0])),
            transcendentals=rows,
        ),
        name="user_gradient",
    )(user_feat, cotangent, gain.reshape(1, width), *flat)


def flip(value, size, bits):
    return lax.ppermute(value, "user", [(source, source ^ bits) for source in range(size)])


def gather_layers(own, size):
    return jnp.concatenate(
        [own] + [flip(own, size, 4 * layer) for layer in range(1, size // 4)], axis=0
    )


def gather_sides(own, size):
    own = jnp.concatenate([own, flip(own, size, 2)], axis=0)
    return own, flip(own, size, 1)


def gather_order(size):
    layers = size // 4
    place = jnp.arange(size, dtype=jnp.int32)
    core, side, layer = place // (size // 2), (place // layers) % 2, place % layers
    return lax.axis_index("user") ^ (layer * 4 + side * 2 + core)


def scatter_sum(terms, size):
    cores, sides = 2, 2
    layers = size // (cores * sides)
    index = lax.axis_index("user")
    core, side, layer = index % cores, (index // cores) % sides, index // (cores * sides)
    rest = terms.shape[1:]
    terms = terms.reshape((layers, sides, cores) + rest)
    own = lax.dynamic_index_in_dim(terms, core, 2, keepdims=False)
    away = lax.dynamic_index_in_dim(terms, 1 - core, 2, keepdims=False).astype(jnp.bfloat16)
    terms = own + flip(away, size, 1).astype(jnp.float32)
    own = lax.dynamic_index_in_dim(terms, side, 1, keepdims=False)
    away = lax.dynamic_index_in_dim(terms, 1 - side, 1, keepdims=False).astype(jnp.bfloat16)
    terms = own + flip(away, size, 2).astype(jnp.float32)
    total = lax.dynamic_index_in_dim(terms, layer, 0, keepdims=False)
    for other in range(1, layers):
        away = lax.dynamic_index_in_dim(terms, layer ^ other, 0, keepdims=False)
        arrived = flip(away.astype(jnp.bfloat16), size, other * cores * sides)
        total = total + arrived.astype(jnp.float32)
    return total


def as_rows(value, size):
    count = value.shape[1]
    padded = -(-count // TILE) * TILE
    return jnp.pad(value, ((0, 0), (0, padded - count))).reshape(size, padded // TILE, TILE)


def on_device(
    user_feat, cotangent, gain, item_feat, categories, expert_w, tile_place, tile_level, tile_count
):
    users, width = user_feat.shape
    user_size, item_size = lax.axis_size("user"), lax.axis_size("item")
    item_index = lax.axis_index("item")
    own_items = item_feat.shape[1]
    items = own_items * user_size
    experts_here = expert_w.shape[0]
    first_expert = item_index * experts_here
    own_cats, own_feat = categories[0], item_feat[0]
    rows, half_width = users // ROW_CHUNKS, width // HALVES

    own_halves = own_queries(first_expert, own_cats, own_feat, expert_w)
    order = gather_order(user_size)
    dense = dense_tiles(tile_place[0, 0], tile_count[0], tile_level[0, 0], users, items)
    layers = [gather_layers(own, user_size) for own in own_halves]
    layers[0], dense = lax.optimization_barrier((layers[0], dense))
    queries = [gather_sides(part, user_size) for part in layers]

    local_cats = (own_cats - first_expert).astype(jnp.bfloat16)
    packed = jnp.concatenate(
        [own_feat, jnp.broadcast_to(local_cats[:, None], (own_items, TILE))], axis=1
    )
    packed, _ = lax.optimization_barrier((packed, queries[-1][1]))
    packed = gather_sides(gather_layers(packed, user_size), user_size)
    own_width = width // user_size
    feats, mask = ordered_items(order, packed, experts_here, own_width, width)

    partials = []
    for half in range(HALVES):
        first = [0, 1] if half == 0 else [0]
        partials.append([])
        for start, end in zip(first, first[1:] + [ROW_CHUNKS]):
            for partial in spread_items(order, queries[half], dense, start, end - start, rows):
                pieces = [partial]
                for shift in range(1, item_size):
                    pairs = [(source, (source + shift) % item_size) for source in range(item_size)]
                    pieces.append(lax.ppermute(partial, "item", pairs))
                partials[half].append(pieces)

    grads, gain_term, item_terms = [], 0.0, 0.0
    for chunk in range(ROW_CHUNKS):
        grad, term = user_gradient(
            user_feat,
            cotangent,
            gain,
            [partials[half][chunk] for half in range(HALVES)],
            chunk * rows,
            rows,
        )
        grads.append(grad)
        gain_term = gain_term + term[0]
        if chunk < ROW_CHUNKS - 1:
            item_terms = item_terms + lax.dot_general(
                grad,
                dense[chunk * rows : (chunk + 1) * rows],
                (((0,), (0,)), ((), ())),
                preferred_element_type=jnp.float32,
            )
    part_width = own_width // HALVES
    sums = []
    for half in range(HALVES):
        part = slice(half * half_width, (half + 1) * half_width)
        terms = item_terms[part] + lax.dot_general(
            grads[-1][:, part],
            dense[users - rows :],
            (((0,), (0,)), ((), ())),
            preferred_element_type=jnp.float32,
        )
        terms = terms.reshape(user_size, part_width, items)
        sums.append(scatter_sum(terms, user_size).astype(jnp.bfloat16))
    sums = jnp.concatenate(sums, axis=0)

    col_width = width // item_size
    user_grad = jnp.concatenate(
        [lax.dynamic_slice_in_dim(grad, item_index * col_width, col_width, 1) for grad in grads],
        axis=0,
    )
    gain_own = lax.dynamic_slice_in_dim(gain_term, item_index * col_width, col_width, 0)

    masked = mask * sums[None]
    expert_cols = lax.dot_general(
        feats,
        masked.reshape(experts_here * own_width, items),
        (((0,), (1,)), ((), ())),
        preferred_element_type=jnp.float32,
    ).astype(jnp.bfloat16)
    by_item = sums.reshape(own_width, user_size, own_items).transpose(1, 0, 2)
    gain_sent = jnp.broadcast_to(gain_own.astype(jnp.bfloat16)[None], (user_size, col_width))
    pieces = [
        as_rows(by_item.reshape(user_size, -1), user_size),
        as_rows(expert_cols.reshape(user_size, -1), user_size),
        as_rows(gain_sent, user_size),
    ]
    swapped = lax.all_to_all(jnp.concatenate(pieces, axis=1), "user", 0, 0)
    ends = [pieces[0].shape[1], pieces[0].shape[1] + pieces[1].shape[1]]

    own_sums = (
        swapped[:, : ends[0]]
        .reshape(user_size, HALVES, part_width, own_items)
        .transpose(1, 0, 2, 3)
        .reshape(width, own_items)
    )
    expert_grad = (
        swapped[:, ends[0] : ends[1]]
        .reshape(user_size, own_width, experts_here, HALVES, part_width)
        .transpose(2, 1, 3, 0, 4)
        .reshape(experts_here, own_width, width)
        .astype(jnp.float32)
    )
    gain_grad = jnp.sum(
        swapped[:, ends[1] :].reshape(user_size, -1)[:, :col_width].astype(jnp.float32), axis=0
    )
    item_total = jnp.zeros((own_items, width), jnp.float32)
    for expert in range(experts_here):
        item_total = item_total + jnp.where(
            (own_cats == first_expert + expert)[:, None],
            lax.dot_general(
                own_sums,
                expert_w[expert],
                (((0,), (1,)), ((), ())),
                preferred_element_type=jnp.float32,
            ),
            0.0,
        )
    return (user_grad, item_total.astype(jnp.bfloat16)[None], expert_grad, gain_grad)


def solution(mesh):
    placed = (
        P("user", None),
        P("user", None),
        P(),
        P("item", "user", None),
        P("item", "user"),
        P("item", None, None),
        P("user", "item", None),
        P("user", "item", None, None, None),
        P("user", "item"),
    )
    return jax.shard_map(
        on_device,
        mesh=mesh,
        in_specs=placed,
        out_specs=(P("user", "item"), P("item", "user", None), P("item", "user", None), P("item")),
        check_vma=False,
    )
```

```python
import functools

import jax
import jax.numpy as jnp
from jax import lax
from jax.experimental import pallas as pl
from jax.experimental.pallas import tpu as pltpu
from jax.sharding import PartitionSpec as P

TILE = 128
SLOTS_PER_STEP = 8
HALVES = 2
ROW_CHUNKS = 4
BLOCK_ROWS = 256
MIB = 1024 * 1024


def place_tiles(item_blocks, place_ref, count_ref, level_ref, dense_ref):
    step = pl.program_id(0)

    @pl.when(step == 0)
    def _():
        dense_ref[...] = jnp.zeros_like(dense_ref)

    for offset in range(level_ref.shape[0]):
        slot = step * level_ref.shape[0] + offset

        @pl.when(slot < count_ref[0])
        def _():
            place = place_ref[slot]
            row = pl.multiple_of((place // item_blocks) * TILE, TILE)
            col = pl.multiple_of((place % item_blocks) * TILE, TILE)
            weights = level_ref[offset].astype(jnp.float32) * (1.0 / (2.0 * TILE))
            dense_ref[pl.ds(row, TILE), pl.ds(col, TILE)] = weights.astype(jnp.bfloat16)


def dense_tiles(place, count, level, users, items):
    slots = level.shape[0]
    per_step = SLOTS_PER_STEP if slots % SLOTS_PER_STEP == 0 else 1
    return pl.pallas_call(
        functools.partial(place_tiles, items // TILE),
        out_shape=jax.ShapeDtypeStruct((users, items), jnp.bfloat16),
        grid_spec=pltpu.PrefetchScalarGridSpec(
            num_scalar_prefetch=2,
            grid=(slots // per_step,),
            in_specs=[
                pl.BlockSpec((per_step, TILE, TILE), lambda step, place_ref, count_ref: (step, 0, 0))
            ],
            out_specs=pl.BlockSpec((users, items), lambda step, place_ref, count_ref: (0, 0)),
        ),
        compiler_params=pltpu.CompilerParams(
            dimension_semantics=("arbitrary",), vmem_limit_bytes=40 * MIB
        ),
        cost_estimate=pl.CostEstimate(
            flops=slots * TILE * TILE,
            bytes_accessed=slots * TILE * TILE * 4 + users * items * 2,
            transcendentals=0,
        ),
        name="place_tiles",
    )(place, count, level)


def project_own(first_ref, cats_ref, feat_ref, weight_ref, *rest):
    out_refs, fetched_ref, sems = rest[:-2], rest[-2], rest[-1]
    experts, width = weight_ref.shape[:2]
    copies = [
        pltpu.make_async_copy(weight_ref.at[expert], fetched_ref.at[expert], sems.at[expert])
        for expert in range(experts)
    ]
    for copy in copies:
        copy.start()
    own = feat_ref.shape[0]
    on_diagonal = lax.broadcasted_iota(jnp.int32, (own, own), 0) == lax.broadcasted_iota(
        jnp.int32, (own, own), 1
    )
    cats = jnp.sum(
        jnp.where(on_diagonal, cats_ref[...].astype(jnp.float32), 0.0), axis=1, keepdims=True
    )
    total = jnp.zeros((own, width), jnp.float32)
    for expert in range(experts):
        copies[expert].wait()
        part = jnp.dot(feat_ref[...], fetched_ref[expert], preferred_element_type=jnp.float32)
        chosen = cats == (first_ref[0] + expert).astype(jnp.float32)
        total = total + jnp.where(chosen, part, 0.0)
    cols = out_refs[0].shape[1]
    for half, out_ref in enumerate(out_refs):
        out_ref[...] = total[:, half * cols : (half + 1) * cols].astype(out_ref.dtype)


def own_queries(first_expert, cats, feat, weights):
    own, width = feat.shape
    experts = weights.shape[0]
    half = jax.ShapeDtypeStruct((own, width // HALVES), jnp.bfloat16)
    half_spec = pl.BlockSpec((own, width // HALVES), lambda step, first_ref: (0, 0))
    return pl.pallas_call(
        project_own,
        out_shape=[half] * HALVES,
        grid_spec=pltpu.PrefetchScalarGridSpec(
            num_scalar_prefetch=1,
            grid=(1,),
            in_specs=[
                pl.BlockSpec((1, own), lambda step, first_ref: (0, 0)),
                pl.BlockSpec((own, width), lambda step, first_ref: (0, 0)),
                pl.BlockSpec(memory_space=pl.ANY),
            ],
            out_specs=[half_spec] * HALVES,
            scratch_shapes=[
                pltpu.VMEM((experts, width, width), jnp.bfloat16),
                pltpu.SemaphoreType.DMA((experts,)),
            ],
        ),
        compiler_params=pltpu.CompilerParams(
            dimension_semantics=("arbitrary",), vmem_limit_bytes=16 * MIB
        ),
        cost_estimate=pl.CostEstimate(
            flops=2 * own * width * width * experts,
            bytes_accessed=weights.size * 2 + own * width * 4,
            transcendentals=0,
        ),
        name="own_queries",
    )(first_expert.reshape(1), cats.reshape(1, own), feat, weights)


def fetch_in_order(order_ref, sources, all_ref, sems):
    per_source = len(sems) // len(sources)
    own = sources[0].shape[0] // per_source
    copies = []
    for place in range(len(sems)):
        source = sources[place // per_source].at[pl.ds((place % per_source) * own, own)]
        start = pl.multiple_of(order_ref[place] * own, own)
        copy = pltpu.make_async_copy(source, all_ref.at[pl.ds(start, own)], sems[place])
        copy.start()
        copies.append(copy)
    for copy in copies:
        copy.wait()


def spread(blocks, order_ref, same_ref, other_ref, dense_ref, *rest):
    out_refs, all_ref = rest[:-1], rest[-1]
    step = pl.program_id(0)

    @pl.when(step == 0)
    def _():
        own = all_ref.shape[0] // blocks
        for place in range(blocks):
            source = (same_ref, other_ref)[2 * place // blocks]
            start = pl.multiple_of(order_ref[place] * own, own)
            all_ref[pl.ds(start, own)] = source[pl.ds((place % (blocks // 2)) * own, own)]

    product = jnp.dot(dense_ref[...], all_ref[...], preferred_element_type=jnp.float32)
    for chunk, out_ref in enumerate(out_refs):

        @pl.when(step == chunk)
        def _():
            out_ref[...] = product.astype(out_ref.dtype)


def spread_items(order, queries, dense, first, chunks, rows):
    items = dense.shape[1]
    cols = queries[0].shape[1]
    blocks = order.shape[0]
    return pl.pallas_call(
        functools.partial(spread, blocks),
        out_shape=[jax.ShapeDtypeStruct((rows, cols), jnp.bfloat16)] * chunks,
        grid_spec=pltpu.PrefetchScalarGridSpec(
            num_scalar_prefetch=1,
            grid=(chunks,),
            in_specs=[pl.BlockSpec(queries[0].shape, lambda step, order_ref: (0, 0))] * 2
            + [pl.BlockSpec((rows, items), lambda step, order_ref: (first + step, 0))],
            out_specs=[pl.BlockSpec((rows, cols), lambda step, order_ref: (0, 0))] * chunks,
            scratch_shapes=[pltpu.VMEM((items, cols), jnp.bfloat16)],
        ),
        compiler_params=pltpu.CompilerParams(
            dimension_semantics=("arbitrary",), vmem_limit_bytes=24 * MIB
        ),
        cost_estimate=pl.CostEstimate(
            flops=2 * chunks * rows * items * cols,
            bytes_accessed=chunks * rows * (items + cols) * 2 + items * cols * 2,
            transcendentals=0,
        ),
        name="spread_items",
    )(order, *queries, dense)


def order_items(blocks, order_ref, same_ref, other_ref, feat_ref, mask_ref, all_ref, sems):
    fetch_in_order(
        order_ref, (same_ref, other_ref), all_ref, [sems.at[place] for place in range(blocks)]
    )
    width = feat_ref.shape[1]
    experts, own_width = mask_ref.shape[0], mask_ref.shape[1]
    feat_ref[...] = all_ref[:, :width]
    for start in range(0, feat_ref.shape[0], TILE):
        cats = all_ref[pl.ds(start, TILE), pl.ds(width, TILE)].astype(jnp.float32)
        cats = jnp.transpose(cats)[:own_width]
        for expert in range(experts):
            mask_ref[expert, :, pl.ds(start, TILE)] = (cats == expert).astype(mask_ref.dtype)


def ordered_items(order, packed, experts, own_width, width):
    items, blocks = 2 * packed[0].shape[0], order.shape[0]
    return pl.pallas_call(
        functools.partial(order_items, blocks),
        out_shape=[
            jax.ShapeDtypeStruct((items, width), jnp.bfloat16),
            jax.ShapeDtypeStruct((experts, own_width, items), jnp.bfloat16),
        ],
        grid_spec=pltpu.PrefetchScalarGridSpec(
            num_scalar_prefetch=1,
            grid=(1,),
            in_specs=[pl.BlockSpec(memory_space=pl.ANY)] * 2,
            out_specs=[
                pl.BlockSpec((items, width), lambda step, order_ref: (0, 0)),
                pl.BlockSpec((experts, own_width, items), lambda step, order_ref: (0, 0, 0)),
            ],
            scratch_shapes=[
                pltpu.VMEM((items, packed[0].shape[1]), jnp.bfloat16),
                pltpu.SemaphoreType.DMA((blocks,)),
            ],
        ),
        compiler_params=pltpu.CompilerParams(
            dimension_semantics=("arbitrary",), vmem_limit_bytes=24 * MIB
        ),
        cost_estimate=pl.CostEstimate(
            flops=0, bytes_accessed=items * width * 6, transcendentals=0
        ),
        name="order_items",
    )(order, *packed)


def norm_backward(pieces, user_ref, grad_ref, gain_ref, *rest):
    piece_refs, out_ref, term_ref = rest[: pieces * HALVES], rest[-2], rest[-1]
    summed = []
    for half in range(HALVES):
        total = piece_refs[half * pieces][...].astype(jnp.float32)
        for piece in range(1, pieces):
            total = total + piece_refs[half * pieces + piece][...].astype(jnp.float32)
        summed.append(total)
    width = out_ref.shape[1]
    pre_norm = user_ref[...].astype(jnp.float32) + jnp.concatenate(summed, axis=1)
    grad = grad_ref[...].astype(jnp.float32)
    scaled_grad = gain_ref[...] * grad
    inv_rms = lax.rsqrt(jnp.sum(pre_norm * pre_norm, axis=1, keepdims=True) / width + 1e-05)
    cross_mean = jnp.sum(scaled_grad * pre_norm, axis=1, keepdims=True) / width
    out_ref[...] = (
        inv_rms * scaled_grad - pre_norm * (inv_rms * inv_rms * inv_rms * cross_mean)
    ).astype(out_ref.dtype)
    term = jnp.sum(grad * pre_norm * inv_rms, axis=0, keepdims=True)

    @pl.when(pl.program_id(0) == 0)
    def _():
        term_ref[...] = term

    @pl.when(pl.program_id(0) > 0)
    def _():
        term_ref[...] += term


def user_gradient(user_feat, cotangent, gain, pieces, first, rows):
    width = user_feat.shape[1]
    block_rows = min(BLOCK_ROWS, rows)
    first_block = first // block_rows
    flat = [piece for half in pieces for piece in half]
    whole = pl.BlockSpec((block_rows, width), lambda step: (first_block + step, 0))
    part = pl.BlockSpec((block_rows, width // HALVES), lambda step: (step, 0))
    return pl.pallas_call(
        functools.partial(norm_backward, len(pieces[0])),
        out_shape=[
            jax.ShapeDtypeStruct((rows, width), jnp.bfloat16),
            jax.ShapeDtypeStruct((1, width), jnp.float32),
        ],
        grid=(rows // block_rows,),
        in_specs=[whole, whole, pl.BlockSpec((1, width), lambda step: (0, 0))] + [part] * len(flat),
        out_specs=[
            pl.BlockSpec((block_rows, width), lambda step: (step, 0)),
            pl.BlockSpec((1, width), lambda step: (0, 0)),
        ],
        compiler_params=pltpu.CompilerParams(
            dimension_semantics=("arbitrary",), vmem_limit_bytes=24 * MIB
        ),
        cost_estimate=pl.CostEstimate(
            flops=16 * rows * width,
            bytes_accessed=rows * width * 2 * (3 + len(pieces[0])),
            transcendentals=rows,
        ),
        name="user_gradient",
    )(user_feat, cotangent, gain.reshape(1, width), *flat)


def flip(value, size, bits):
    return lax.ppermute(value, "user", [(source, source ^ bits) for source in range(size)])


def gather_layers(own, size):
    return jnp.concatenate(
        [own] + [flip(own, size, 4 * layer) for layer in range(1, size // 4)], axis=0
    )


def gather_sides(own, size):
    return jnp.concatenate([own, flip(own, size, 2)], axis=0)


def gather_order(size):
    layers = size // 4
    place = jnp.arange(size, dtype=jnp.int32)
    core, side, layer = place // (size // 2), (place // layers) % 2, place % layers
    return lax.axis_index("user") ^ (layer * 4 + side * 2 + core)


def sum_flipped(terms, size, bit, axis, index):
    own = lax.dynamic_index_in_dim(terms, index, axis, keepdims=False)
    away = lax.dynamic_index_in_dim(terms, 1 - index, axis, keepdims=False)
    return own + flip(away.astype(jnp.bfloat16), size, bit).astype(jnp.float32)


def sum_layers(terms, size, layer):
    total = lax.dynamic_index_in_dim(terms, layer, 0, keepdims=False)
    for other in range(1, terms.shape[0]):
        away = lax.dynamic_index_in_dim(terms, layer ^ other, 0, keepdims=False)
        total = total + flip(away.astype(jnp.bfloat16), size, other * 4).astype(jnp.float32)
    return total


def scatter_sum(terms, size, sides_first):
    index = lax.axis_index("user")
    core, side, layer = index % 2, (index // 2) % 2, index // 4
    terms = terms.reshape((size // 4, 2, 2) + terms.shape[1:])
    terms = sum_flipped(terms, size, 1, 2, core)
    if sides_first:
        return sum_layers(sum_flipped(terms, size, 2, 1, side), size, layer)
    return sum_flipped(sum_layers(terms, size, layer), size, 2, 0, side)


def as_rows(value, size):
    count = value.shape[1]
    padded = -(-count // TILE) * TILE
    return jnp.pad(value, ((0, 0), (0, padded - count))).reshape(size, padded // TILE, TILE)


def on_device(
    user_feat, cotangent, gain, item_feat, categories, expert_w, tile_place, tile_level, tile_count
):
    users, width = user_feat.shape
    user_size, item_size = lax.axis_size("user"), lax.axis_size("item")
    item_index = lax.axis_index("item")
    own_items = item_feat.shape[1]
    items = own_items * user_size
    experts_here = expert_w.shape[0]
    first_expert = item_index * experts_here
    own_cats, own_feat = categories[0], item_feat[0]
    rows, half_width = users // ROW_CHUNKS, width // HALVES

    own_halves = own_queries(first_expert, own_cats, own_feat, expert_w)
    order = gather_order(user_size)
    tile_index = tile_place[0, 0]
    layers = gather_layers(own_halves[0], user_size)
    layers, tile_index = lax.optimization_barrier((layers, tile_index))
    dense = dense_tiles(tile_index, tile_count[0], tile_level[0, 0], users, items)
    same = gather_sides(layers, user_size)
    same, dense, own_second = lax.optimization_barrier((same, dense, own_halves[1]))
    queries = [(same, flip(same, user_size, 1))]
    same = gather_sides(gather_layers(own_second, user_size), user_size)
    queries.append((same, flip(same, user_size, 1)))

    partials = []
    for half in range(HALVES):
        partials.append([])
        first = [0, 1, ROW_CHUNKS] if half == 0 else [0, ROW_CHUNKS]
        for start, end in zip(first, first[1:]):
            here = spread_items(order, queries[half], dense, start, end - start, rows)
            order, *here = lax.optimization_barrier((order, *here))
            for partial in here:
                pieces = [partial]
                for shift in range(1, item_size):
                    pairs = [(source, (source + shift) % item_size) for source in range(item_size)]
                    pieces.append(lax.ppermute(partial, "item", pairs))
                partials[half].append(pieces)

    local_cats = (own_cats - first_expert).astype(jnp.bfloat16)
    local_cats, order = lax.optimization_barrier((local_cats, order))
    packed = jnp.concatenate(
        [own_feat, jnp.broadcast_to(local_cats[:, None], (own_items, TILE))], axis=1
    )
    packed = gather_sides(gather_layers(packed, user_size), user_size)
    own_width = width // user_size
    feats, mask = ordered_items(
        order, (packed, flip(packed, user_size, 1)), experts_here, own_width, width
    )
    partials[-1][-2][1], feats, mask = lax.optimization_barrier((partials[-1][-2][1], feats, mask))

    grads, gain_term, item_terms = [], 0.0, 0.0
    for chunk in range(ROW_CHUNKS):
        grad, term = user_gradient(
            user_feat,
            cotangent,
            gain,
            [partials[half][chunk] for half in range(HALVES)],
            chunk * rows,
            rows,
        )
        grads.append(grad)
        gain_term = gain_term + term[0]
        if chunk < ROW_CHUNKS - 1:
            item_terms = item_terms + lax.dot_general(
                grad,
                dense[chunk * rows : (chunk + 1) * rows],
                (((0,), (0,)), ((), ())),
                preferred_element_type=jnp.float32,
            )
    part_width = own_width // HALVES
    sums = []
    for half in range(HALVES):
        part = slice(half * half_width, (half + 1) * half_width)
        terms = item_terms[part] + lax.dot_general(
            grads[-1][:, part],
            dense[users - rows :],
            (((0,), (0,)), ((), ())),
            preferred_element_type=jnp.float32,
        )
        terms = terms.reshape(user_size, part_width, items)
        sums.append(scatter_sum(terms, user_size, half == 0).astype(jnp.bfloat16))
    sums = jnp.concatenate(sums, axis=0)

    col_width = width // item_size
    user_grad = jnp.concatenate(
        [lax.dynamic_slice_in_dim(grad, item_index * col_width, col_width, 1) for grad in grads],
        axis=0,
    )
    gain_own = lax.dynamic_slice_in_dim(gain_term, item_index * col_width, col_width, 0)

    masked = mask * sums[None]
    expert_cols = lax.dot_general(
        feats,
        masked.reshape(experts_here * own_width, items),
        (((0,), (1,)), ((), ())),
        preferred_element_type=jnp.float32,
    ).astype(jnp.bfloat16)
    by_item = sums.reshape(own_width, user_size, own_items).transpose(1, 0, 2)
    gain_sent = jnp.broadcast_to(gain_own.astype(jnp.bfloat16)[None], (user_size, col_width))
    pieces = [
        as_rows(by_item.reshape(user_size, -1), user_size),
        as_rows(expert_cols.reshape(user_size, -1), user_size),
        as_rows(gain_sent, user_size),
    ]
    swapped = lax.all_to_all(jnp.concatenate(pieces, axis=1), "user", 0, 0)
    ends = [pieces[0].shape[1], pieces[0].shape[1] + pieces[1].shape[1]]

    own_sums = (
        swapped[:, : ends[0]]
        .reshape(user_size, HALVES, part_width, own_items)
        .transpose(1, 0, 2, 3)
        .reshape(width, own_items)
    )
    expert_grad = (
        swapped[:, ends[0] : ends[1]]
        .reshape(user_size, own_width, experts_here, HALVES, part_width)
        .transpose(2, 1, 3, 0, 4)
        .reshape(experts_here, own_width, width)
        .astype(jnp.float32)
    )
    gain_grad = jnp.sum(
        swapped[:, ends[1] :].reshape(user_size, -1)[:, :col_width].astype(jnp.float32), axis=0
    )
    item_total = jnp.zeros((own_items, width), jnp.float32)
    for expert in range(experts_here):
        item_total = item_total + jnp.where(
            (own_cats == first_expert + expert)[:, None],
            lax.dot_general(
                own_sums,
                expert_w[expert],
                (((0,), (1,)), ((), ())),
                preferred_element_type=jnp.float32,
            ),
            0.0,
        )
    return (user_grad, item_total.astype(jnp.bfloat16)[None], expert_grad, gain_grad)


def solution(mesh):
    placed = (
        P("user", None),
        P("user", None),
        P(),
        P("item", "user", None),
        P("item", "user"),
        P("item", None, None),
        P("user", "item", None),
        P("user", "item", None, None, None),
        P("user", "item"),
    )
    return jax.shard_map(
        on_device,
        mesh=mesh,
        in_specs=placed,
        out_specs=(P("user", "item"), P("item", "user", None), P("item", "user", None), P("item")),
        check_vma=False,
    )
```

```python
import functools

import jax
import jax.numpy as jnp
from jax import lax
from jax.experimental import pallas as pl
from jax.experimental.pallas import tpu as pltpu
from jax.sharding import PartitionSpec as P

TILE = 128
SLOTS_PER_STEP = 8
HALVES = 2
ROW_CHUNKS = 4
BLOCK_ROWS = 256
MIB = 1024 * 1024


def place_tiles(item_blocks, place_ref, count_ref, level_ref, _, dense_ref):
    step = pl.program_id(0)

    @pl.when(step == 0)
    def _():
        dense_ref[...] = jnp.zeros_like(dense_ref)

    for offset in range(level_ref.shape[0]):
        slot = step * level_ref.shape[0] + offset

        @pl.when(slot < count_ref[0])
        def _():
            place = place_ref[slot]
            row = pl.multiple_of((place // item_blocks) * TILE, TILE)
            col = pl.multiple_of((place % item_blocks) * TILE, TILE)
            weights = level_ref[offset].astype(jnp.float32) * (1.0 / (2.0 * TILE))
            dense_ref[pl.ds(row, TILE), pl.ds(col, TILE)] = weights.astype(jnp.bfloat16)


def dense_tiles(place, count, level, users, items, earlier):
    slots = level.shape[0]
    per_step = SLOTS_PER_STEP if slots % SLOTS_PER_STEP == 0 else 1
    return pl.pallas_call(
        functools.partial(place_tiles, items // TILE),
        out_shape=jax.ShapeDtypeStruct((users, items), jnp.bfloat16),
        grid_spec=pltpu.PrefetchScalarGridSpec(
            num_scalar_prefetch=2,
            grid=(slots // per_step,),
            in_specs=[
                pl.BlockSpec((per_step, TILE, TILE), lambda step, place_ref, count_ref: (step, 0, 0)),
                pl.BlockSpec(memory_space=pl.ANY),
            ],
            out_specs=pl.BlockSpec((users, items), lambda step, place_ref, count_ref: (0, 0)),
        ),
        compiler_params=pltpu.CompilerParams(
            dimension_semantics=("arbitrary",), vmem_limit_bytes=40 * MIB
        ),
        cost_estimate=pl.CostEstimate(
            flops=slots * TILE * TILE,
            bytes_accessed=slots * TILE * TILE * 4 + users * items * 2,
            transcendentals=0,
        ),
        name="place_tiles",
    )(place, count, level, earlier)


def project_own(first_ref, cats_ref, feat_ref, weight_ref, *rest):
    out_refs, fetched_ref, sems = rest[:-2], rest[-2], rest[-1]
    experts, width = weight_ref.shape[:2]
    copies = [
        pltpu.make_async_copy(weight_ref.at[expert], fetched_ref.at[expert], sems.at[expert])
        for expert in range(experts)
    ]
    for copy in copies:
        copy.start()
    own = feat_ref.shape[0]
    on_diagonal = lax.broadcasted_iota(jnp.int32, (own, own), 0) == lax.broadcasted_iota(
        jnp.int32, (own, own), 1
    )
    cats = jnp.sum(
        jnp.where(on_diagonal, cats_ref[...].astype(jnp.float32), 0.0), axis=1, keepdims=True
    )
    total = jnp.zeros((own, width), jnp.float32)
    for expert in range(experts):
        copies[expert].wait()
        part = jnp.dot(feat_ref[...], fetched_ref[expert], preferred_element_type=jnp.float32)
        chosen = cats == (first_ref[0] + expert).astype(jnp.float32)
        total = total + jnp.where(chosen, part, 0.0)
    cols = out_refs[0].shape[1]
    for half, out_ref in enumerate(out_refs):
        out_ref[...] = total[:, half * cols : (half + 1) * cols].astype(out_ref.dtype)


def own_queries(first_expert, cats, feat, weights):
    own, width = feat.shape
    experts = weights.shape[0]
    half = jax.ShapeDtypeStruct((own, width // HALVES), jnp.bfloat16)
    half_spec = pl.BlockSpec((own, width // HALVES), lambda step, first_ref: (0, 0))
    return pl.pallas_call(
        project_own,
        out_shape=[half] * HALVES,
        grid_spec=pltpu.PrefetchScalarGridSpec(
            num_scalar_prefetch=1,
            grid=(1,),
            in_specs=[
                pl.BlockSpec((1, own), lambda step, first_ref: (0, 0)),
                pl.BlockSpec((own, width), lambda step, first_ref: (0, 0)),
                pl.BlockSpec(memory_space=pl.ANY),
            ],
            out_specs=[half_spec] * HALVES,
            scratch_shapes=[
                pltpu.VMEM((experts, width, width), jnp.bfloat16),
                pltpu.SemaphoreType.DMA((experts,)),
            ],
        ),
        compiler_params=pltpu.CompilerParams(
            dimension_semantics=("arbitrary",), vmem_limit_bytes=56 * MIB
        ),
        cost_estimate=pl.CostEstimate(
            flops=2 * own * width * width * experts,
            bytes_accessed=weights.size * 2 + own * width * 4,
            transcendentals=0,
        ),
        name="own_queries",
    )(first_expert.reshape(1), cats.reshape(1, own), feat, weights)


def fetch_in_order(order_ref, sources, all_ref, sems):
    per_source = len(sems) // len(sources)
    own = sources[0].shape[0] // per_source
    copies = []
    for place in range(len(sems)):
        source = sources[place // per_source].at[pl.ds((place % per_source) * own, own)]
        start = pl.multiple_of(order_ref[place] * own, own)
        copy = pltpu.make_async_copy(source, all_ref.at[pl.ds(start, own)], sems[place])
        copy.start()
        copies.append(copy)
    for copy in copies:
        copy.wait()


def spread(blocks, order_ref, same_ref, other_ref, dense_ref, *rest):
    out_refs, next_ref, all_ref = rest[:-2], rest[-2], rest[-1]
    step = pl.program_id(0)

    @pl.when(step == 0)
    def _():
        for place in range(blocks):
            next_ref[place] = order_ref[place]
        own = all_ref.shape[0] // blocks
        for place in range(blocks):
            source = (same_ref, other_ref)[2 * place // blocks]
            start = pl.multiple_of(order_ref[place] * own, own)
            all_ref[pl.ds(start, own)] = source[pl.ds((place % (blocks // 2)) * own, own)]

    product = jnp.dot(dense_ref[...], all_ref[...], preferred_element_type=jnp.float32)
    rows, first = product.shape[0], 0
    for out_ref in out_refs:
        chunks = out_ref.shape[0] // rows

        @pl.when((step >= first) & (step < first + chunks))
        def _():
            start = pl.multiple_of((step - first) * rows, rows)
            out_ref[pl.ds(start, rows)] = product.astype(out_ref.dtype)

        first += chunks


def spread_items(order, queries, dense, first, counts, rows):
    items = dense.shape[1]
    cols = queries[0].shape[1]
    blocks, chunks = order.shape[0], sum(counts)
    whole = lambda step, order_ref: (0, 0)
    return pl.pallas_call(
        functools.partial(spread, blocks),
        out_shape=[jax.ShapeDtypeStruct((count * rows, cols), jnp.bfloat16) for count in counts]
        + [jax.ShapeDtypeStruct((blocks,), jnp.int32)],
        grid_spec=pltpu.PrefetchScalarGridSpec(
            num_scalar_prefetch=1,
            grid=(chunks,),
            in_specs=[pl.BlockSpec(queries[0].shape, whole)] * 2
            + [pl.BlockSpec((rows, items), lambda step, order_ref: (first + step, 0))],
            out_specs=[pl.BlockSpec((count * rows, cols), whole) for count in counts]
            + [pl.BlockSpec(memory_space=pltpu.SMEM)],
            scratch_shapes=[pltpu.VMEM((items, cols), jnp.bfloat16)],
        ),
        compiler_params=pltpu.CompilerParams(
            dimension_semantics=("arbitrary",), vmem_limit_bytes=24 * MIB
        ),
        cost_estimate=pl.CostEstimate(
            flops=2 * chunks * rows * items * cols,
            bytes_accessed=chunks * rows * (items + cols) * 2 + items * cols * 2,
            transcendentals=0,
        ),
        name="spread_items",
    )(order, *queries, dense)


def order_items(blocks, order_ref, same_ref, other_ref, feat_ref, mask_ref, all_ref, sems):
    fetch_in_order(
        order_ref, (same_ref, other_ref), all_ref, [sems.at[place] for place in range(blocks)]
    )
    width = feat_ref.shape[1]
    experts, own_width = mask_ref.shape[0], mask_ref.shape[1]
    feat_ref[...] = all_ref[:, :width]
    for start in range(0, feat_ref.shape[0], TILE):
        cats = all_ref[pl.ds(start, TILE), pl.ds(width, TILE)].astype(jnp.float32)
        cats = jnp.transpose(cats)[:own_width]
        for expert in range(experts):
            mask_ref[expert, :, pl.ds(start, TILE)] = (cats == expert).astype(mask_ref.dtype)


def ordered_items(order, packed, experts, own_width, width):
    items, blocks = 2 * packed[0].shape[0], order.shape[0]
    return pl.pallas_call(
        functools.partial(order_items, blocks),
        out_shape=[
            jax.ShapeDtypeStruct((items, width), jnp.bfloat16),
            jax.ShapeDtypeStruct((experts, own_width, items), jnp.bfloat16),
        ],
        grid_spec=pltpu.PrefetchScalarGridSpec(
            num_scalar_prefetch=1,
            grid=(1,),
            in_specs=[pl.BlockSpec(memory_space=pl.ANY)] * 2,
            out_specs=[
                pl.BlockSpec((items, width), lambda step, order_ref: (0, 0)),
                pl.BlockSpec((experts, own_width, items), lambda step, order_ref: (0, 0, 0)),
            ],
            scratch_shapes=[
                pltpu.VMEM((items, packed[0].shape[1]), jnp.bfloat16),
                pltpu.SemaphoreType.DMA((blocks,)),
            ],
        ),
        compiler_params=pltpu.CompilerParams(
            dimension_semantics=("arbitrary",), vmem_limit_bytes=24 * MIB
        ),
        cost_estimate=pl.CostEstimate(
            flops=0, bytes_accessed=items * width * 6, transcendentals=0
        ),
        name="order_items",
    )(order, *packed)


def norm_backward(pieces, user_ref, grad_ref, gain_ref, *rest):
    piece_refs, out_ref, term_ref = rest[: pieces * HALVES], rest[-2], rest[-1]
    summed = []
    for half in range(HALVES):
        total = piece_refs[half * pieces][...].astype(jnp.float32)
        for piece in range(1, pieces):
            total = total + piece_refs[half * pieces + piece][...].astype(jnp.float32)
        summed.append(total)
    width = out_ref.shape[1]
    pre_norm = user_ref[...].astype(jnp.float32) + jnp.concatenate(summed, axis=1)
    grad = grad_ref[...].astype(jnp.float32)
    scaled_grad = gain_ref[...] * grad
    inv_rms = lax.rsqrt(jnp.sum(pre_norm * pre_norm, axis=1, keepdims=True) / width + 1e-05)
    cross_mean = jnp.sum(scaled_grad * pre_norm, axis=1, keepdims=True) / width
    out_ref[...] = (
        inv_rms * scaled_grad - pre_norm * (inv_rms * inv_rms * inv_rms * cross_mean)
    ).astype(out_ref.dtype)
    term = jnp.sum(grad * pre_norm * inv_rms, axis=0, keepdims=True)

    @pl.when(pl.program_id(0) == 0)
    def _():
        term_ref[...] = term

    @pl.when(pl.program_id(0) > 0)
    def _():
        term_ref[...] += term


def user_gradient(user_feat, cotangent, gain, pieces, first, rows, earlier):
    width = user_feat.shape[1]
    block_rows = min(BLOCK_ROWS, rows)
    whole = pl.BlockSpec((block_rows, width), lambda step: (first // block_rows + step, 0))
    flat, specs = [], []
    for arrays, offset in pieces:
        index_map = lambda step, skipped=(first - offset) // block_rows: (skipped + step, 0)
        flat += arrays
        specs += [pl.BlockSpec((block_rows, width // HALVES), index_map)] * len(arrays)
    return pl.pallas_call(
        functools.partial(norm_backward, len(pieces[0][0])),
        out_shape=[
            jax.ShapeDtypeStruct((rows, width), jnp.bfloat16),
            jax.ShapeDtypeStruct((1, width), jnp.float32),
        ],
        grid=(rows // block_rows,),
        in_specs=[whole, whole, pl.BlockSpec((1, width), lambda step: (0, 0))]
        + specs
        + [pl.BlockSpec(memory_space=pl.ANY)] * len(earlier),
        out_specs=[
            pl.BlockSpec((block_rows, width), lambda step: (step, 0)),
            pl.BlockSpec((1, width), lambda step: (0, 0)),
        ],
        compiler_params=pltpu.CompilerParams(
            dimension_semantics=("arbitrary",), vmem_limit_bytes=24 * MIB
        ),
        cost_estimate=pl.CostEstimate(
            flops=16 * rows * width,
            bytes_accessed=rows * width * 2 * (3 + len(pieces[0][0])),
            transcendentals=rows,
        ),
        name="user_gradient",
    )(user_feat, cotangent, gain.reshape(1, width), *flat, *earlier)


def flip(value, size, bits):
    return lax.ppermute(value, "user", [(source, source ^ bits) for source in range(size)])


def gather_layers(own, size):
    return jnp.concatenate(
        [own] + [flip(own, size, 4 * layer) for layer in range(1, size // 4)], axis=0
    )


def gather_sides(own, size):
    return jnp.concatenate([own, flip(own, size, 2)], axis=0)


def gather_order(size):
    layers = size // 4
    place = jnp.arange(size, dtype=jnp.int32)
    core, side, layer = place // (size // 2), (place // layers) % 2, place % layers
    return lax.axis_index("user") ^ (layer * 4 + side * 2 + core)


def exchange(partial, size):
    pieces = [partial]
    for shift in range(1, size):
        pairs = [(source, (source + shift) % size) for source in range(size)]
        pieces.append(lax.ppermute(partial, "item", pairs))
    return pieces


def scatter_sums(halves, size):
    bits = size.bit_length() - 1
    index = lax.axis_index("user")
    orders = [list(range(bits)), [0, 2, 1] + list(range(3, bits))]
    halves = [terms.reshape((2,) * bits + terms.shape[1:]) for terms in halves]
    left = [list(reversed(range(bits))) for _ in halves]
    for stage in range(bits):
        for half, terms in enumerate(halves):
            bit = orders[half][stage]
            axis = left[half].index(bit)
            left[half].remove(bit)
            mine = (index >> bit) & 1
            own = lax.dynamic_index_in_dim(terms, mine, axis, keepdims=False)
            away = lax.dynamic_index_in_dim(terms, 1 - mine, axis, keepdims=False)
            arrived = flip(away.astype(jnp.bfloat16), size, 1 << bit)
            halves[half] = own + arrived.astype(jnp.float32)
        if 0 < stage < bits - 1:
            halves = list(lax.optimization_barrier(tuple(halves)))
    return halves


def as_rows(value, size):
    count = value.shape[1]
    padded = -(-count // TILE) * TILE
    return jnp.pad(value, ((0, 0), (0, padded - count))).reshape(size, padded // TILE, TILE)


def on_device(
    user_feat, cotangent, gain, item_feat, categories, expert_w, tile_place, tile_level, tile_count
):
    users, width = user_feat.shape
    user_size, item_size = lax.axis_size("user"), lax.axis_size("item")
    item_index = lax.axis_index("item")
    own_items = item_feat.shape[1]
    items = own_items * user_size
    experts_here = expert_w.shape[0]
    first_expert = item_index * experts_here
    own_cats, own_feat = categories[0], item_feat[0]
    rows, half_width = users // ROW_CHUNKS, width // HALVES

    own_halves = own_queries(first_expert, own_cats, own_feat, expert_w)
    order = gather_order(user_size)
    layers = gather_layers(own_halves[0], user_size)
    dense = dense_tiles(
        tile_place[0, 0], tile_count[0], tile_level[0, 0], users, items, earlier=layers
    )
    same = gather_sides(layers, user_size)
    same, dense, own_second = lax.optimization_barrier((same, dense, own_halves[1]))
    queries = (same, flip(same, user_size, 1))
    layers = gather_layers(own_second, user_size)

    product, order = spread_items(order, queries, dense, 0, (ROW_CHUNKS,), rows)
    partials = [[(exchange(product, item_size), 0)], []]
    local_cats = (own_cats - first_expert).astype(jnp.bfloat16)
    local_cats, layers, order = lax.optimization_barrier((local_cats, layers, order))
    same = gather_sides(layers, user_size)
    queries = (same, flip(same, user_size, 1))
    counts = (ROW_CHUNKS - 2, 1, 1)
    *products, order = spread_items(order, queries, dense, 0, counts, rows)
    for number, product in enumerate(products):
        partials[1].append((exchange(product, item_size), sum(counts[:number]) * rows))

    packed = jnp.concatenate(
        [own_feat, jnp.broadcast_to(local_cats[:, None], (own_items, TILE))], axis=1
    )
    packed = gather_layers(packed, user_size)
    arrived = partials[0][0][0]
    packed, order, arrived[-1] = lax.optimization_barrier((packed, order, arrived[-1]))
    packed = gather_sides(packed, user_size)
    own_width = width // user_size
    feats, mask = ordered_items(
        order, (packed, flip(packed, user_size, 1)), experts_here, own_width, width
    )

    grads, gain_term, item_terms = [], 0.0, 0.0
    for chunk in range(ROW_CHUNKS):
        pieces = [
            [piece for piece in partials[half] if piece[1] <= chunk * rows][-1]
            for half in range(HALVES)
        ]
        earlier = [mask] if chunk == ROW_CHUNKS - 2 else []
        grad, term = user_gradient(
            user_feat, cotangent, gain, pieces, chunk * rows, rows, earlier
        )
        grads.append(grad)
        gain_term = gain_term + term[0]
        if chunk < ROW_CHUNKS - 1:
            item_terms = item_terms + lax.dot_general(
                grad,
                dense[chunk * rows : (chunk + 1) * rows],
                (((0,), (0,)), ((), ())),
                preferred_element_type=jnp.float32,
            )
    part_width = own_width // HALVES
    halves = []
    for half in range(HALVES):
        part = slice(half * half_width, (half + 1) * half_width)
        terms = item_terms[part] + lax.dot_general(
            grads[-1][:, part],
            dense[users - rows :],
            (((0,), (0,)), ((), ())),
            preferred_element_type=jnp.float32,
        )
        halves.append(terms.reshape(user_size, part_width, items))
    sums = jnp.concatenate(scatter_sums(halves, user_size), axis=0).astype(jnp.bfloat16)

    col_width = width // item_size
    user_grad = jnp.concatenate(
        [lax.dynamic_slice_in_dim(grad, item_index * col_width, col_width, 1) for grad in grads],
        axis=0,
    )
    gain_own = lax.dynamic_slice_in_dim(gain_term, item_index * col_width, col_width, 0)

    masked = mask * sums[None]
    expert_cols = lax.dot_general(
        feats,
        masked.reshape(experts_here * own_width, items),
        (((0,), (1,)), ((), ())),
        preferred_element_type=jnp.float32,
    ).astype(jnp.bfloat16)
    by_item = sums.reshape(own_width, user_size, own_items).transpose(1, 0, 2)
    gain_sent = jnp.broadcast_to(gain_own.astype(jnp.bfloat16)[None], (user_size, col_width))
    pieces = [
        as_rows(by_item.reshape(user_size, -1), user_size),
        as_rows(expert_cols.reshape(user_size, -1), user_size),
        as_rows(gain_sent, user_size),
    ]
    swapped = lax.all_to_all(jnp.concatenate(pieces, axis=1), "user", 0, 0)
    ends = [pieces[0].shape[1], pieces[0].shape[1] + pieces[1].shape[1]]

    own_sums = (
        swapped[:, : ends[0]]
        .reshape(user_size, HALVES, part_width, own_items)
        .transpose(1, 0, 2, 3)
        .reshape(width, own_items)
    )
    expert_grad = (
        swapped[:, ends[0] : ends[1]]
        .reshape(user_size, own_width, experts_here, HALVES, part_width)
        .transpose(2, 1, 3, 0, 4)
        .reshape(experts_here, own_width, width)
        .astype(jnp.float32)
    )
    gain_grad = jnp.sum(
        swapped[:, ends[1] :].reshape(user_size, -1)[:, :col_width].astype(jnp.float32), axis=0
    )
    item_total = jnp.zeros((own_items, width), jnp.float32)
    for expert in range(experts_here):
        item_total = item_total + jnp.where(
            (own_cats == first_expert + expert)[:, None],
            lax.dot_general(
                own_sums,
                expert_w[expert],
                (((0,), (1,)), ((), ())),
                preferred_element_type=jnp.float32,
            ),
            0.0,
        )
    return (user_grad, item_total.astype(jnp.bfloat16)[None], expert_grad, gain_grad)


def solution(mesh):
    placed = (
        P("user", None),
        P("user", None),
        P(),
        P("item", "user", None),
        P("item", "user"),
        P("item", None, None),
        P("user", "item", None),
        P("user", "item", None, None, None),
        P("user", "item"),
    )
    return jax.shard_map(
        on_device,
        mesh=mesh,
        in_specs=placed,
        out_specs=(P("user", "item"), P("item", "user", None), P("item", "user", None), P("item")),
        check_vma=False,
    )
```

```python
import functools

import jax
import jax.numpy as jnp
from jax import lax
from jax.experimental import pallas as pl
from jax.experimental.pallas import tpu as pltpu
from jax.sharding import PartitionSpec as P

TILE = 128
SLOTS_PER_STEP = 8
HALVES = 2
ROW_CHUNKS = 4
BLOCK_ROWS = 256
MIB = 1024 * 1024


def place_tiles(item_blocks, place_ref, count_ref, order_ref, level_ref, dense_ref, next_ref):
    step = pl.program_id(0)

    @pl.when(step == 0)
    def _():
        dense_ref[...] = jnp.zeros_like(dense_ref)
        for place in range(next_ref.shape[0]):
            next_ref[place] = order_ref[place]

    for offset in range(level_ref.shape[0]):
        slot = step * level_ref.shape[0] + offset

        @pl.when(slot < count_ref[0])
        def _():
            place = place_ref[slot]
            row = pl.multiple_of((place // item_blocks) * TILE, TILE)
            col = pl.multiple_of((place % item_blocks) * TILE, TILE)
            weights = level_ref[offset].astype(jnp.float32) * (1.0 / (2.0 * TILE))
            dense_ref[pl.ds(row, TILE), pl.ds(col, TILE)] = weights.astype(jnp.bfloat16)


def dense_tiles(place, count, level, users, items, order):
    slots = level.shape[0]
    per_step = SLOTS_PER_STEP if slots % SLOTS_PER_STEP == 0 else 1
    return pl.pallas_call(
        functools.partial(place_tiles, items // TILE),
        out_shape=[
            jax.ShapeDtypeStruct((users, items), jnp.bfloat16),
            jax.ShapeDtypeStruct(order.shape, jnp.int32),
        ],
        grid_spec=pltpu.PrefetchScalarGridSpec(
            num_scalar_prefetch=3,
            grid=(slots // per_step,),
            in_specs=[pl.BlockSpec((per_step, TILE, TILE), lambda step, *_: (step, 0, 0))],
            out_specs=[
                pl.BlockSpec((users, items), lambda step, *_: (0, 0)),
                pl.BlockSpec(memory_space=pltpu.SMEM),
            ],
        ),
        compiler_params=pltpu.CompilerParams(
            dimension_semantics=("arbitrary",), vmem_limit_bytes=40 * MIB
        ),
        cost_estimate=pl.CostEstimate(
            flops=slots * TILE * TILE,
            bytes_accessed=slots * TILE * TILE * 4 + users * items * 2,
            transcendentals=0,
        ),
        name="place_tiles",
    )(place, count, order, level)


def project_own(first_ref, cats_ref, feat_ref, weight_ref, *rest):
    out_refs, total_ref = rest[:-1], rest[-1]
    expert = pl.program_id(0)
    own = feat_ref.shape[0]
    on_diagonal = lax.broadcasted_iota(jnp.int32, (own, own), 0) == lax.broadcasted_iota(
        jnp.int32, (own, own), 1
    )
    cats = jnp.sum(
        jnp.where(on_diagonal, cats_ref[...].astype(jnp.float32), 0.0), axis=1, keepdims=True
    )
    chosen = cats == (first_ref[0] + expert).astype(jnp.float32)
    part = jnp.dot(feat_ref[...], weight_ref[0], preferred_element_type=jnp.float32)
    part = jnp.where(chosen, part, 0.0)

    @pl.when(expert == 0)
    def _():
        total_ref[...] = part

    @pl.when(expert > 0)
    def _():
        total_ref[...] += part

    @pl.when(expert == pl.num_programs(0) - 1)
    def _():
        cols = out_refs[0].shape[1]
        for half, out_ref in enumerate(out_refs):
            out_ref[...] = total_ref[:, half * cols : (half + 1) * cols].astype(out_ref.dtype)


def own_queries(first_expert, cats, feat, weights):
    own, width = feat.shape
    experts = weights.shape[0]
    half = jax.ShapeDtypeStruct((own, width // HALVES), jnp.bfloat16)
    half_spec = pl.BlockSpec((own, width // HALVES), lambda expert, first_ref: (0, 0))
    return pl.pallas_call(
        project_own,
        out_shape=[half] * HALVES,
        grid_spec=pltpu.PrefetchScalarGridSpec(
            num_scalar_prefetch=1,
            grid=(experts,),
            in_specs=[
                pl.BlockSpec((1, own), lambda expert, first_ref: (0, 0)),
                pl.BlockSpec((own, width), lambda expert, first_ref: (0, 0)),
                pl.BlockSpec((1, width, width), lambda expert, first_ref: (expert, 0, 0)),
            ],
            out_specs=[half_spec] * HALVES,
            scratch_shapes=[pltpu.VMEM((own, width), jnp.float32)],
        ),
        compiler_params=pltpu.CompilerParams(dimension_semantics=("arbitrary",)),
        cost_estimate=pl.CostEstimate(
            flops=2 * own * width * width * experts,
            bytes_accessed=weights.size * 2 + own * width * 4,
            transcendentals=0,
        ),
        name="own_queries",
    )(first_expert.reshape(1), cats.reshape(1, own), feat, weights)


def fetch_in_order(order_ref, sources, all_ref, sems):
    per_source = len(sems) // len(sources)
    own = sources[0].shape[0] // per_source
    copies = []
    for place in range(len(sems)):
        source = sources[place // per_source].at[pl.ds((place % per_source) * own, own)]
        start = pl.multiple_of(order_ref[place] * own, own)
        copy = pltpu.make_async_copy(source, all_ref.at[pl.ds(start, own)], sems[place])
        copy.start()
        copies.append(copy)
    for copy in copies:
        copy.wait()


def spread(blocks, order_ref, same_ref, other_ref, dense_ref, *rest):
    out_refs, next_ref, all_ref = rest[:-2], rest[-2], rest[-1]
    step = pl.program_id(0)

    @pl.when(step == 0)
    def _():
        for place in range(blocks):
            next_ref[place] = order_ref[place]
        own = all_ref.shape[0] // blocks
        for place in range(blocks):
            source = (same_ref, other_ref)[2 * place // blocks]
            start = pl.multiple_of(order_ref[place] * own, own)
            all_ref[pl.ds(start, own)] = source[pl.ds((place % (blocks // 2)) * own, own)]

    product = jnp.dot(dense_ref[...], all_ref[...], preferred_element_type=jnp.float32)
    rows, first = product.shape[0], 0
    for out_ref in out_refs:
        chunks = out_ref.shape[0] // rows

        @pl.when((step >= first) & (step < first + chunks))
        def _():
            start = pl.multiple_of((step - first) * rows, rows)
            out_ref[pl.ds(start, rows)] = product.astype(out_ref.dtype)

        first += chunks


def spread_items(order, queries, dense, first, counts, rows):
    items = dense.shape[1]
    cols = queries[0].shape[1]
    blocks, chunks = order.shape[0], sum(counts)
    whole = lambda step, order_ref: (0, 0)
    return pl.pallas_call(
        functools.partial(spread, blocks),
        out_shape=[jax.ShapeDtypeStruct((count * rows, cols), jnp.bfloat16) for count in counts]
        + [jax.ShapeDtypeStruct((blocks,), jnp.int32)],
        grid_spec=pltpu.PrefetchScalarGridSpec(
            num_scalar_prefetch=1,
            grid=(chunks,),
            in_specs=[pl.BlockSpec(queries[0].shape, whole)] * 2
            + [pl.BlockSpec((rows, items), lambda step, order_ref: (first + step, 0))],
            out_specs=[pl.BlockSpec((count * rows, cols), whole) for count in counts]
            + [pl.BlockSpec(memory_space=pltpu.SMEM)],
            scratch_shapes=[pltpu.VMEM((items, cols), jnp.bfloat16)],
        ),
        compiler_params=pltpu.CompilerParams(
            dimension_semantics=("arbitrary",), vmem_limit_bytes=24 * MIB
        ),
        cost_estimate=pl.CostEstimate(
            flops=2 * chunks * rows * items * cols,
            bytes_accessed=chunks * rows * (items + cols) * 2 + items * cols * 2,
            transcendentals=0,
        ),
        name="spread_items",
    )(order, *queries, dense)


def order_items(
    blocks, order_ref, same_ref, other_ref, feat_ref, mask_ref, next_ref, all_ref, sems
):
    for place in range(blocks):
        next_ref[place] = order_ref[place]
    fetch_in_order(
        order_ref, (same_ref, other_ref), all_ref, [sems.at[place] for place in range(blocks)]
    )
    width = feat_ref.shape[1]
    experts, own_width = mask_ref.shape[0], mask_ref.shape[1]
    feat_ref[...] = all_ref[:, :width]
    for start in range(0, feat_ref.shape[0], TILE):
        cats = all_ref[pl.ds(start, TILE), pl.ds(width, TILE)].astype(jnp.float32)
        cats = jnp.transpose(cats)[:own_width]
        for expert in range(experts):
            mask_ref[expert, :, pl.ds(start, TILE)] = (cats == expert).astype(mask_ref.dtype)


def ordered_items(order, packed, experts, own_width, width):
    items, blocks = 2 * packed[0].shape[0], order.shape[0]
    return pl.pallas_call(
        functools.partial(order_items, blocks),
        out_shape=[
            jax.ShapeDtypeStruct((items, width), jnp.bfloat16),
            jax.ShapeDtypeStruct((experts, own_width, items), jnp.bfloat16),
            jax.ShapeDtypeStruct((blocks,), jnp.int32),
        ],
        grid_spec=pltpu.PrefetchScalarGridSpec(
            num_scalar_prefetch=1,
            grid=(1,),
            in_specs=[pl.BlockSpec(memory_space=pl.ANY)] * 2,
            out_specs=[
                pl.BlockSpec((items, width), lambda step, order_ref: (0, 0)),
                pl.BlockSpec((experts, own_width, items), lambda step, order_ref: (0, 0, 0)),
                pl.BlockSpec(memory_space=pltpu.SMEM),
            ],
            scratch_shapes=[
                pltpu.VMEM((items, packed[0].shape[1]), jnp.bfloat16),
                pltpu.SemaphoreType.DMA((blocks,)),
            ],
        ),
        compiler_params=pltpu.CompilerParams(
            dimension_semantics=("arbitrary",), vmem_limit_bytes=14 * MIB
        ),
        cost_estimate=pl.CostEstimate(
            flops=0, bytes_accessed=items * width * 6, transcendentals=0
        ),
        name="order_items",
    )(order, *packed)


def norm_backward(pieces, user_ref, grad_ref, gain_ref, *rest):
    piece_refs, out_ref, term_ref = rest[: pieces * HALVES], rest[-2], rest[-1]
    summed = []
    for half in range(HALVES):
        total = piece_refs[half * pieces][...].astype(jnp.float32)
        for piece in range(1, pieces):
            total = total + piece_refs[half * pieces + piece][...].astype(jnp.float32)
        summed.append(total)
    width = out_ref.shape[1]
    pre_norm = user_ref[...].astype(jnp.float32) + jnp.concatenate(summed, axis=1)
    grad = grad_ref[...].astype(jnp.float32)
    scaled_grad = gain_ref[...] * grad
    inv_rms = lax.rsqrt(jnp.sum(pre_norm * pre_norm, axis=1, keepdims=True) / width + 1e-05)
    cross_mean = jnp.sum(scaled_grad * pre_norm, axis=1, keepdims=True) / width
    out_ref[...] = (
        inv_rms * scaled_grad - pre_norm * (inv_rms * inv_rms * inv_rms * cross_mean)
    ).astype(out_ref.dtype)
    term = jnp.sum(grad * pre_norm * inv_rms, axis=0, keepdims=True)

    @pl.when(pl.program_id(0) == 0)
    def _():
        term_ref[...] = term

    @pl.when(pl.program_id(0) > 0)
    def _():
        term_ref[...] += term


def user_gradient(user_feat, cotangent, gain, pieces, first, rows):
    width = user_feat.shape[1]
    block_rows = min(BLOCK_ROWS, rows)
    first_block = first // block_rows
    flat = [piece for half in pieces for piece in half]
    whole = pl.BlockSpec((block_rows, width), lambda step: (first_block + step, 0))
    part = pl.BlockSpec((block_rows, width // HALVES), lambda step: (step, 0))
    return pl.pallas_call(
        functools.partial(norm_backward, len(pieces[0])),
        out_shape=[
            jax.ShapeDtypeStruct((rows, width), jnp.bfloat16),
            jax.ShapeDtypeStruct((1, width), jnp.float32),
        ],
        grid=(rows // block_rows,),
        in_specs=[whole, whole, pl.BlockSpec((1, width), lambda step: (0, 0))] + [part] * len(flat),
        out_specs=[
            pl.BlockSpec((block_rows, width), lambda step: (step, 0)),
            pl.BlockSpec((1, width), lambda step: (0, 0)),
        ],
        compiler_params=pltpu.CompilerParams(
            dimension_semantics=("arbitrary",), vmem_limit_bytes=24 * MIB
        ),
        cost_estimate=pl.CostEstimate(
            flops=16 * rows * width,
            bytes_accessed=rows * width * 2 * (3 + len(pieces[0])),
            transcendentals=rows,
        ),
        name="user_gradient",
    )(user_feat, cotangent, gain.reshape(1, width), *flat)


def flip(value, size, bits):
    return lax.ppermute(value, "user", [(source, source ^ bits) for source in range(size)])


def gather_layers(own, size):
    return jnp.concatenate(
        [own] + [flip(own, size, 4 * layer) for layer in range(1, size // 4)], axis=0
    )


def gather_sides(own, size):
    own = jnp.concatenate([own, flip(own, size, 2)], axis=0)
    return own, flip(own, size, 1)


def gather_order(size):
    layers = size // 4
    place = jnp.arange(size, dtype=jnp.int32)
    core, side, layer = place // (size // 2), (place // layers) % 2, place % layers
    return lax.axis_index("user") ^ (layer * 4 + side * 2 + core)


def scatter_sums(halves, size, beside):
    bits = size.bit_length() - 1
    index = lax.axis_index("user")
    orders = [list(range(bits)), [0, 2, 1] + list(range(3, bits))]
    halves = [terms.reshape((2,) * bits + terms.shape[1:]) for terms in halves]
    left = [list(reversed(range(bits))) for _ in halves]
    for stage in range(bits):
        for half, terms in enumerate(halves):
            bit = orders[half][stage]
            axis = left[half].index(bit)
            left[half].remove(bit)
            mine = (index >> bit) & 1
            own = lax.dynamic_index_in_dim(terms, mine, axis, keepdims=False)
            away = lax.dynamic_index_in_dim(terms, 1 - mine, axis, keepdims=False)
            arrived = flip(away.astype(jnp.bfloat16), size, 1 << bit)
            halves[half] = own + arrived.astype(jnp.float32)
        if stage == 1:
            *halves, beside = lax.optimization_barrier((*halves, beside))
        elif 1 < stage < bits - 1:
            halves = list(lax.optimization_barrier(tuple(halves)))
    return halves, beside


def pack(size, _, feat_ref, mask_ref, first_ref, second_ref, gain_ref, out_ref):
    experts, own_width, items = mask_ref.shape
    own = items // size
    sums = jnp.concatenate([first_ref[...], second_ref[...]], axis=0).astype(jnp.bfloat16)
    masked = jnp.concatenate([mask_ref[expert] * sums for expert in range(experts)], axis=0)
    cols = jnp.dot(masked, feat_ref[...], preferred_element_type=jnp.float32)
    cols = jnp.transpose(cols).astype(jnp.bfloat16)
    gain = gain_ref[...].astype(jnp.bfloat16)
    for place in range(size):
        out_ref[place, :own_width] = sums[:, place * own : (place + 1) * own]
        out_ref[place, own_width : 2 * own_width] = cols[place * own_width : (place + 1) * own_width]
        out_ref[place, 2 * own_width :] = gain


def packed_sums(order, feats, mask, halves, gain):
    size = order.shape[0]
    experts, own_width, items = mask.shape
    own = items // size
    gain = jnp.pad(gain.reshape(-1, own), ((0, 16 - gain.shape[0] // own), (0, 0)))
    operands = (feats, mask, *halves, gain)
    shape = (size, 2 * own_width + gain.shape[0], own)
    specs = [
        pl.BlockSpec(value.shape, lambda step, order_ref, rank=value.ndim: (0,) * rank)
        for value in operands
    ]
    return pl.pallas_call(
        functools.partial(pack, size),
        out_shape=jax.ShapeDtypeStruct(shape, jnp.bfloat16),
        grid_spec=pltpu.PrefetchScalarGridSpec(
            num_scalar_prefetch=1,
            grid=(1,),
            in_specs=specs,
            out_specs=pl.BlockSpec(shape, lambda step, order_ref: (0, 0, 0)),
        ),
        compiler_params=pltpu.CompilerParams(
            dimension_semantics=("arbitrary",), vmem_limit_bytes=16 * MIB
        ),
        cost_estimate=pl.CostEstimate(
            flops=2 * experts * own_width * items * feats.shape[1],
            bytes_accessed=items * feats.shape[1] * 2,
            transcendentals=0,
        ),
        name="packed_sums",
    )(order, *operands)


def unpack(first_ref, swapped_ref, weight_ref, cats_ref, item_ref, expert_ref, gain_ref):
    size, _, own = swapped_ref.shape
    experts, own_width, width = expert_ref.shape
    part_width = own_width // HALVES
    swapped = [swapped_ref[place].astype(jnp.float32) for place in range(size)]
    sums = jnp.concatenate(
        [
            block[half * part_width : (half + 1) * part_width]
            for half in range(HALVES)
            for block in swapped
        ],
        axis=0,
    ).astype(jnp.bfloat16)
    total = jnp.zeros((width, own), jnp.float32)
    for expert in range(experts):
        part = jnp.dot(weight_ref[expert], sums, preferred_element_type=jnp.float32)
        total = total + jnp.where(cats_ref[...] == first_ref[0] + expert, part, 0.0)
    item_ref[...] = jnp.transpose(total).astype(item_ref.dtype)
    cols = [jnp.transpose(block[own_width : 2 * own_width]) for block in swapped]
    for expert in range(experts):
        rows = [
            block[start : start + part_width]
            for start in range(expert * own_width, (expert + 1) * own_width, part_width)
            for block in cols
        ]
        expert_ref[expert] = jnp.transpose(jnp.concatenate(rows, axis=0))
    gain = swapped[0][2 * own_width :]
    for block in swapped[1:]:
        gain = gain + block[2 * own_width :]
    gain_ref[...] = gain[: gain_ref.shape[0]]


def unpacked(swapped, first_expert, weights, cats, own_width, gain_width):
    own, width = swapped.shape[2], weights.shape[1]
    experts = weights.shape[0]
    operands = (swapped, weights, cats.reshape(1, own))
    shapes = [(own, width), (experts, own_width, width), (gain_width // own, own)]
    dtypes = [jnp.bfloat16, jnp.float32, jnp.float32]
    whole = lambda shape: pl.BlockSpec(shape, lambda step, first_ref: (0,) * len(shape))
    return pl.pallas_call(
        unpack,
        out_shape=[jax.ShapeDtypeStruct(*pair) for pair in zip(shapes, dtypes)],
        grid_spec=pltpu.PrefetchScalarGridSpec(
            num_scalar_prefetch=1,
            grid=(1,),
            in_specs=[whole(value.shape) for value in operands],
            out_specs=[whole(shape) for shape in shapes],
        ),
        compiler_params=pltpu.CompilerParams(
            dimension_semantics=("arbitrary",), vmem_limit_bytes=16 * MIB
        ),
        cost_estimate=pl.CostEstimate(
            flops=2 * experts * own * width * width,
            bytes_accessed=weights.size * 2,
            transcendentals=0,
        ),
        name="unpacked",
    )(first_expert.reshape(1), *operands)


def on_device(
    user_feat, cotangent, gain, item_feat, categories, expert_w, tile_place, tile_level, tile_count
):
    users, width = user_feat.shape
    user_size, item_size = lax.axis_size("user"), lax.axis_size("item")
    item_index = lax.axis_index("item")
    own_items = item_feat.shape[1]
    items = own_items * user_size
    experts_here = expert_w.shape[0]
    first_expert = item_index * experts_here
    own_cats, own_feat = categories[0], item_feat[0]
    rows, half_width = users // ROW_CHUNKS, width // HALVES

    own_halves = own_queries(first_expert, own_cats, own_feat, expert_w)
    order = gather_order(user_size)
    dense, order = dense_tiles(
        tile_place[0, 0], tile_count[0], tile_level[0, 0], users, items, order
    )
    layers = [gather_layers(own, user_size) for own in own_halves]
    layers[0], order = lax.optimization_barrier((layers[0], order))
    queries = [gather_sides(part, user_size) for part in layers]

    partials = [[] for _ in range(HALVES)]
    for half in range(HALVES):
        for first, count in ((0, 1), (1, ROW_CHUNKS - 1)):
            *products, last = spread_items(order, queries[half], dense, first, (1,) * count, rows)
            for product in products:
                pieces = [product]
                for shift in range(1, item_size):
                    pairs = [(source, (source + shift) % item_size) for source in range(item_size)]
                    pieces.append(lax.ppermute(product, "item", pairs))
                partials[half].append(pieces)
    local_cats = (own_cats - first_expert).astype(jnp.bfloat16)
    arrived = partials[0][0]
    local_cats, arrived[-1] = lax.optimization_barrier((local_cats, arrived[-1]))
    packed = jnp.concatenate(
        [own_feat, jnp.broadcast_to(local_cats[:, None], (own_items, TILE))], axis=1
    )
    packed = gather_layers(packed, user_size)
    arrived = partials[1][1]
    packed, arrived[-1] = lax.optimization_barrier((packed, arrived[-1]))
    same = jnp.concatenate([packed, flip(packed, user_size, 2)], axis=0)
    arrived = partials[1][3]
    same, arrived[-1] = lax.optimization_barrier((same, arrived[-1]))
    packed = (same, flip(same, user_size, 1))
    own_width = width // user_size
    feats, mask, order = ordered_items(order, packed, experts_here, own_width, width)

    grads, gain_term, item_terms = [], 0.0, 0.0
    for chunk in range(ROW_CHUNKS):
        grad, term = user_gradient(
            user_feat,
            cotangent,
            gain,
            [partials[half][chunk] for half in range(HALVES)],
            chunk * rows,
            rows,
        )
        grads.append(grad)
        gain_term = gain_term + term[0]
        if chunk < ROW_CHUNKS - 1:
            item_terms = item_terms + lax.dot_general(
                grad,
                dense[chunk * rows : (chunk + 1) * rows],
                (((0,), (0,)), ((), ())),
                preferred_element_type=jnp.float32,
            )
    part_width = own_width // HALVES
    halves = []
    for half in range(HALVES):
        part = slice(half * half_width, (half + 1) * half_width)
        terms = item_terms[part] + lax.dot_general(
            grads[-1][:, part],
            dense[users - rows :],
            (((0,), (0,)), ((), ())),
            preferred_element_type=jnp.float32,
        )
        halves.append(terms.reshape(user_size, part_width, items))
    halves, order = scatter_sums(halves, user_size, order)

    col_width = width // item_size
    user_grad = jnp.concatenate(
        [lax.dynamic_slice_in_dim(grad, item_index * col_width, col_width, 1) for grad in grads],
        axis=0,
    )
    gain_own = lax.dynamic_slice_in_dim(gain_term, item_index * col_width, col_width, 0)

    sent = packed_sums(order, feats, mask, halves, gain_own)
    swapped = lax.all_to_all(sent, "user", 0, 0)
    item_grad, expert_grad, gain_grad = unpacked(
        swapped, first_expert, expert_w, own_cats, own_width, col_width
    )
    return (user_grad, item_grad[None], expert_grad, gain_grad.reshape(col_width))


def solution(mesh):
    placed = (
        P("user", None),
        P("user", None),
        P(),
        P("item", "user", None),
        P("item", "user"),
        P("item", None, None),
        P("user", "item", None),
        P("user", "item", None, None, None),
        P("user", "item"),
    )
    return jax.shard_map(
        on_device,
        mesh=mesh,
        in_specs=placed,
        out_specs=(P("user", "item"), P("item", "user", None), P("item", "user", None), P("item")),
        check_vma=False,
    )
```

```python
import functools

import jax
import jax.numpy as jnp
from jax import lax
from jax.experimental import pallas as pl
from jax.experimental.pallas import tpu as pltpu
from jax.sharding import PartitionSpec as P

TILE = 128
SLOTS_PER_STEP = 8
HALVES = 2
ROW_CHUNKS = 4
BLOCK_ROWS = 256
MIB = 1024 * 1024


def place_tiles(item_blocks, place_ref, count_ref, level_ref, dense_ref):
    step = pl.program_id(0)

    @pl.when(step == 0)
    def _():
        dense_ref[...] = jnp.zeros_like(dense_ref)

    for offset in range(level_ref.shape[0]):
        slot = step * level_ref.shape[0] + offset

        @pl.when(slot < count_ref[0])
        def _():
            place = place_ref[slot]
            row = pl.multiple_of((place // item_blocks) * TILE, TILE)
            col = pl.multiple_of((place % item_blocks) * TILE, TILE)
            weights = level_ref[offset].astype(jnp.float32) * (1.0 / (2.0 * TILE))
            dense_ref[pl.ds(row, TILE), pl.ds(col, TILE)] = weights.astype(jnp.bfloat16)


def dense_tiles(place, count, level, users, items):
    slots = level.shape[0]
    per_step = SLOTS_PER_STEP if slots % SLOTS_PER_STEP == 0 else 1
    return pl.pallas_call(
        functools.partial(place_tiles, items // TILE),
        out_shape=jax.ShapeDtypeStruct((users, items), jnp.bfloat16),
        grid_spec=pltpu.PrefetchScalarGridSpec(
            num_scalar_prefetch=2,
            grid=(slots // per_step,),
            in_specs=[
                pl.BlockSpec((per_step, TILE, TILE), lambda step, place_ref, count_ref: (step, 0, 0))
            ],
            out_specs=pl.BlockSpec((users, items), lambda step, place_ref, count_ref: (0, 0)),
        ),
        compiler_params=pltpu.CompilerParams(
            dimension_semantics=("arbitrary",), vmem_limit_bytes=16 * MIB
        ),
        cost_estimate=pl.CostEstimate(
            flops=slots * TILE * TILE,
            bytes_accessed=slots * TILE * TILE * 4 + users * items * 2,
            transcendentals=0,
        ),
        name="place_tiles",
    )(place, count, level)


def project_own(first_ref, cats_ref, feat_ref, weight_ref, *rest):
    out_refs, total_ref = rest[:-1], rest[-1]
    expert = pl.program_id(0)
    own = feat_ref.shape[0]
    on_diagonal = lax.broadcasted_iota(jnp.int32, (own, own), 0) == lax.broadcasted_iota(
        jnp.int32, (own, own), 1
    )
    cats = jnp.sum(
        jnp.where(on_diagonal, cats_ref[...].astype(jnp.float32), 0.0), axis=1, keepdims=True
    )
    chosen = cats == (first_ref[0] + expert).astype(jnp.float32)
    part = jnp.dot(feat_ref[...], weight_ref[0], preferred_element_type=jnp.float32)
    part = jnp.where(chosen, part, 0.0)

    @pl.when(expert == 0)
    def _():
        total_ref[...] = part

    @pl.when(expert > 0)
    def _():
        total_ref[...] += part

    @pl.when(expert == pl.num_programs(0) - 1)
    def _():
        cols = out_refs[0].shape[1]
        for half, out_ref in enumerate(out_refs):
            out_ref[...] = total_ref[:, half * cols : (half + 1) * cols].astype(out_ref.dtype)


def own_queries(first_expert, cats, feat, weights):
    own, width = feat.shape
    experts = weights.shape[0]
    half = jax.ShapeDtypeStruct((own, width // HALVES), jnp.bfloat16)
    half_spec = pl.BlockSpec((own, width // HALVES), lambda expert, first_ref: (0, 0))
    return pl.pallas_call(
        project_own,
        out_shape=[half] * HALVES,
        grid_spec=pltpu.PrefetchScalarGridSpec(
            num_scalar_prefetch=1,
            grid=(experts,),
            in_specs=[
                pl.BlockSpec((1, own), lambda expert, first_ref: (0, 0)),
                pl.BlockSpec((own, width), lambda expert, first_ref: (0, 0)),
                pl.BlockSpec((1, width, width), lambda expert, first_ref: (expert, 0, 0)),
            ],
            out_specs=[half_spec] * HALVES,
            scratch_shapes=[pltpu.VMEM((own, width), jnp.float32)],
        ),
        compiler_params=pltpu.CompilerParams(dimension_semantics=("arbitrary",)),
        cost_estimate=pl.CostEstimate(
            flops=2 * own * width * width * experts,
            bytes_accessed=weights.size * 2 + own * width * 4,
            transcendentals=0,
        ),
        name="own_queries",
    )(first_expert.reshape(1), cats.reshape(1, own), feat, weights)


def spread(blocks, order_ref, same_ref, other_ref, dense_ref, *rest):
    out_refs, next_ref, all_ref = rest[:-2], rest[-2], rest[-1]
    step = pl.program_id(0)

    @pl.when(step == 0)
    def _():
        for place in range(blocks):
            next_ref[place] = order_ref[place]
        own = all_ref.shape[0] // blocks
        for place in range(blocks):
            source = (same_ref, other_ref)[2 * place // blocks]
            start = pl.multiple_of(order_ref[place] * own, own)
            all_ref[pl.ds(start, own)] = source[pl.ds((place % (blocks // 2)) * own, own)]

    product = jnp.dot(dense_ref[...], all_ref[...], preferred_element_type=jnp.float32)
    rows, first = product.shape[0], 0
    for out_ref in out_refs:
        chunks = out_ref.shape[0] // rows

        @pl.when((step >= first) & (step < first + chunks))
        def _():
            start = pl.multiple_of((step - first) * rows, rows)
            out_ref[pl.ds(start, rows)] = product.astype(out_ref.dtype)

        first += chunks


def spread_items(order, queries, dense, first, counts, rows):
    items = dense.shape[1]
    cols = queries[0].shape[1]
    blocks, chunks = order.shape[0], sum(counts)
    whole = lambda step, order_ref: (0, 0)
    return pl.pallas_call(
        functools.partial(spread, blocks),
        out_shape=[jax.ShapeDtypeStruct((count * rows, cols), jnp.bfloat16) for count in counts]
        + [jax.ShapeDtypeStruct((blocks,), jnp.int32)],
        grid_spec=pltpu.PrefetchScalarGridSpec(
            num_scalar_prefetch=1,
            grid=(chunks,),
            in_specs=[pl.BlockSpec(queries[0].shape, whole)] * 2
            + [pl.BlockSpec((rows, items), lambda step, order_ref: (first + step, 0))],
            out_specs=[pl.BlockSpec((count * rows, cols), whole) for count in counts]
            + [pl.BlockSpec(memory_space=pltpu.SMEM)],
            scratch_shapes=[pltpu.VMEM((items, cols), jnp.bfloat16)],
        ),
        compiler_params=pltpu.CompilerParams(
            dimension_semantics=("arbitrary",), vmem_limit_bytes=14 * MIB
        ),
        cost_estimate=pl.CostEstimate(
            flops=2 * chunks * rows * items * cols,
            bytes_accessed=chunks * rows * (items + cols) * 2 + items * cols * 2,
            transcendentals=0,
        ),
        name="spread_items",
    )(order, *queries, dense)


def norm_backward(pieces, user_ref, grad_ref, gain_ref, *rest):
    piece_refs, out_ref, term_ref = rest[: pieces * HALVES], rest[-2], rest[-1]
    summed = []
    for half in range(HALVES):
        total = piece_refs[half * pieces][...].astype(jnp.float32)
        for piece in range(1, pieces):
            total = total + piece_refs[half * pieces + piece][...].astype(jnp.float32)
        summed.append(total)
    width = out_ref.shape[1]
    pre_norm = user_ref[...].astype(jnp.float32) + jnp.concatenate(summed, axis=1)
    grad = grad_ref[...].astype(jnp.float32)
    scaled_grad = gain_ref[...] * grad
    inv_rms = lax.rsqrt(jnp.sum(pre_norm * pre_norm, axis=1, keepdims=True) / width + 1e-05)
    cross_mean = jnp.sum(scaled_grad * pre_norm, axis=1, keepdims=True) / width
    out_ref[...] = (
        inv_rms * scaled_grad - pre_norm * (inv_rms * inv_rms * inv_rms * cross_mean)
    ).astype(out_ref.dtype)
    term = jnp.sum(grad * pre_norm * inv_rms, axis=0, keepdims=True)

    @pl.when(pl.program_id(0) == 0)
    def _():
        term_ref[...] = term

    @pl.when(pl.program_id(0) > 0)
    def _():
        term_ref[...] += term


def user_gradient(user_feat, cotangent, gain, pieces, first, rows):
    width = user_feat.shape[1]
    block_rows = min(BLOCK_ROWS, rows)
    first_block = first // block_rows
    flat = [piece for half in pieces for piece in half]
    whole = pl.BlockSpec((block_rows, width), lambda step: (first_block + step, 0))
    part = pl.BlockSpec((block_rows, width // HALVES), lambda step: (step, 0))
    return pl.pallas_call(
        functools.partial(norm_backward, len(pieces[0])),
        out_shape=[
            jax.ShapeDtypeStruct((rows, width), jnp.bfloat16),
            jax.ShapeDtypeStruct((1, width), jnp.float32),
        ],
        grid=(rows // block_rows,),
        in_specs=[whole, whole, pl.BlockSpec((1, width), lambda step: (0, 0))] + [part] * len(flat),
        out_specs=[
            pl.BlockSpec((block_rows, width), lambda step: (step, 0)),
            pl.BlockSpec((1, width), lambda step: (0, 0)),
        ],
        compiler_params=pltpu.CompilerParams(
            dimension_semantics=("arbitrary",), vmem_limit_bytes=10 * MIB
        ),
        cost_estimate=pl.CostEstimate(
            flops=16 * rows * width,
            bytes_accessed=rows * width * 2 * (3 + len(pieces[0])),
            transcendentals=rows,
        ),
        name="user_gradient",
    )(user_feat, cotangent, gain.reshape(1, width), *flat)


def flip(value, size, bits):
    return lax.ppermute(value, "user", [(source, source ^ bits) for source in range(size)])


def gather_layers(own, size):
    return jnp.concatenate(
        [own] + [flip(own, size, 4 * layer) for layer in range(1, size // 4)], axis=0
    )


def gather_sides(own, size):
    own = jnp.concatenate([own, flip(own, size, 2)], axis=0)
    return own, flip(own, size, 1)


def gather_order(size):
    layers = size // 4
    place = jnp.arange(size, dtype=jnp.int32)
    core, side, layer = place // (size // 2), (place // layers) % 2, place % layers
    return lax.axis_index("user") ^ (layer * 4 + side * 2 + core)


def scatter_sums(halves, size):
    bits = size.bit_length() - 1
    index = lax.axis_index("user")
    orders = [list(range(bits)), [0, 2, 1] + list(range(3, bits))]
    halves = [terms.reshape((2,) * bits + terms.shape[1:]) for terms in halves]
    left = [list(reversed(range(bits))) for _ in halves]
    for stage in range(bits):
        for half, terms in enumerate(halves):
            bit = orders[half][stage]
            axis = left[half].index(bit)
            left[half].remove(bit)
            mine = (index >> bit) & 1
            own = lax.dynamic_index_in_dim(terms, mine, axis, keepdims=False)
            away = lax.dynamic_index_in_dim(terms, 1 - mine, axis, keepdims=False)
            arrived = flip(away.astype(jnp.bfloat16), size, 1 << bit)
            halves[half] = own + arrived.astype(jnp.float32)
        if 0 < stage < bits - 1:
            halves = list(lax.optimization_barrier(tuple(halves)))
    return halves


def on_device(
    user_feat, cotangent, gain, item_feat, categories, expert_w, tile_place, tile_level, tile_count
):
    users, width = user_feat.shape
    user_size, item_size = lax.axis_size("user"), lax.axis_size("item")
    item_index = lax.axis_index("item")
    own_items = item_feat.shape[1]
    items = own_items * user_size
    experts_here = expert_w.shape[0]
    first_expert = item_index * experts_here
    own_cats, own_feat = categories[0], item_feat[0]
    rows, half_width = users // ROW_CHUNKS, width // HALVES

    own_halves = own_queries(first_expert, own_cats, own_feat, expert_w)
    order = gather_order(user_size)
    dense = dense_tiles(tile_place[0, 0], tile_count[0], tile_level[0, 0], users, items)
    layers = [gather_layers(own, user_size) for own in own_halves]
    queries = [gather_sides(part, user_size) for part in layers]

    partials = [[] for _ in range(HALVES)]
    for half in range(HALVES):
        for first, count in ((0, 1), (1, ROW_CHUNKS - 1)):
            *products, last = spread_items(order, queries[half], dense, first, (1,) * count, rows)
            for product in products:
                pieces = [product]
                for shift in range(1, item_size):
                    pairs = [(source, (source + shift) % item_size) for source in range(item_size)]
                    pieces.append(lax.ppermute(product, "item", pairs))
                partials[half].append(pieces)
    grads, gain_term, item_terms = [], 0.0, 0.0
    for chunk in range(ROW_CHUNKS):
        grad, term = user_gradient(
            user_feat,
            cotangent,
            gain,
            [partials[half][chunk] for half in range(HALVES)],
            chunk * rows,
            rows,
        )
        grads.append(grad)
        gain_term = gain_term + term[0]
        if chunk < ROW_CHUNKS - 1:
            item_terms = item_terms + lax.dot_general(
                dense[chunk * rows : (chunk + 1) * rows],
                grad,
                (((0,), (0,)), ((), ())),
                preferred_element_type=jnp.float32,
            )
    col_width = width // item_size
    user_grad = jnp.concatenate(
        [lax.dynamic_slice_in_dim(grad, item_index * col_width, col_width, 1) for grad in grads],
        axis=0,
    )
    gain_grad = lax.dynamic_slice_in_dim(gain_term, item_index * col_width, col_width, 0)
    for bit in range(user_size.bit_length() - 1):
        gain_grad = gain_grad + flip(gain_grad, user_size, 1 << bit)

    halves = []
    for half in range(HALVES):
        part = slice(half * half_width, (half + 1) * half_width)
        terms = item_terms[:, part] + lax.dot_general(
            dense[users - rows :],
            grads[-1][:, part],
            (((0,), (0,)), ((), ())),
            preferred_element_type=jnp.float32,
        )
        halves.append(terms.reshape(user_size, own_items, half_width))
    sums = [half.astype(jnp.bfloat16) for half in scatter_sums(halves, user_size)]

    chosen = own_cats[:, None] == first_expert + jnp.arange(experts_here, dtype=jnp.int32)[None, :]
    own_width = width // user_size
    left = jnp.where(
        chosen[:, None, :, None],
        own_feat.reshape(own_items, user_size, 1, own_width),
        jnp.zeros((), own_feat.dtype),
    ).reshape(own_items, -1)
    halves = [
        lax.dot_general(
            left, half, (((0,), (0,)), ((), ())), preferred_element_type=jnp.float32
        ).reshape(user_size, experts_here * own_width, half_width)
        for half in sums
    ]
    expert_grad = jnp.concatenate(scatter_sums(halves, user_size), axis=1)
    own_sums = jnp.concatenate(sums, axis=1)
    item_total = jnp.zeros((own_items, width), jnp.float32)
    for expert in range(experts_here):
        item_total = item_total + jnp.where(
            chosen[:, expert][:, None],
            lax.dot_general(
                own_sums,
                expert_w[expert],
                (((1,), (1,)), ((), ())),
                preferred_element_type=jnp.float32,
            ),
            0.0,
        )
    return (
        user_grad,
        item_total.astype(jnp.bfloat16)[None],
        expert_grad.reshape(experts_here, own_width, width),
        gain_grad,
    )


def solution(mesh):
    placed = (
        P("user", None),
        P("user", None),
        P(),
        P("item", "user", None),
        P("item", "user"),
        P("item", None, None),
        P("user", "item", None),
        P("user", "item", None, None, None),
        P("user", "item"),
    )
    return jax.shard_map(
        on_device,
        mesh=mesh,
        in_specs=placed,
        out_specs=(P("user", "item"), P("item", "user", None), P("item", "user", None), P("item")),
        check_vma=False,
    )
```

```python
import functools

import jax
import jax.numpy as jnp
from jax import lax
from jax.experimental import pallas as pl
from jax.experimental.pallas import tpu as pltpu
from jax.sharding import PartitionSpec as P

TILE = 128
SLOTS_PER_STEP = 8
HALVES = 2
ROW_CHUNKS = 4
BLOCK_ROWS = 256
MIB = 1024 * 1024


def place_tiles(item_blocks, place_ref, count_ref, weight_ref, dense_ref):
    step = pl.program_id(0)

    @pl.when(step == 0)
    def _():
        dense_ref[...] = jnp.zeros_like(dense_ref)

    for offset in range(weight_ref.shape[0]):
        slot = step * weight_ref.shape[0] + offset

        @pl.when(slot < count_ref[0])
        def _():
            place = place_ref[slot]
            row = pl.multiple_of((place // item_blocks) * TILE, TILE)
            col = pl.multiple_of((place % item_blocks) * TILE, TILE)
            dense_ref[pl.ds(row, TILE), pl.ds(col, TILE)] = weight_ref[offset]


def dense_tiles(place, count, weights, users, items):
    slots = weights.shape[0]
    per_step = SLOTS_PER_STEP if slots % SLOTS_PER_STEP == 0 else 1
    return pl.pallas_call(
        functools.partial(place_tiles, items // TILE),
        out_shape=jax.ShapeDtypeStruct((users, items), jnp.bfloat16),
        grid_spec=pltpu.PrefetchScalarGridSpec(
            num_scalar_prefetch=2,
            grid=(slots // per_step,),
            in_specs=[
                pl.BlockSpec((per_step, TILE, TILE), lambda step, place_ref, count_ref: (step, 0, 0))
            ],
            out_specs=pl.BlockSpec((users, items), lambda step, place_ref, count_ref: (0, 0)),
        ),
        compiler_params=pltpu.CompilerParams(
            dimension_semantics=("arbitrary",), vmem_limit_bytes=16 * MIB
        ),
        cost_estimate=pl.CostEstimate(
            flops=slots * TILE * TILE,
            bytes_accessed=slots * TILE * TILE * 2 + users * items * 2,
            transcendentals=0,
        ),
        name="place_tiles",
    )(place, count, weights)


def project_own(first_ref, cats_ref, feat_ref, weight_ref, *rest):
    out_refs, total_ref = rest[:-1], rest[-1]
    expert = pl.program_id(0)
    own = feat_ref.shape[0]
    on_diagonal = lax.broadcasted_iota(jnp.int32, (own, own), 0) == lax.broadcasted_iota(
        jnp.int32, (own, own), 1
    )
    cats = jnp.sum(
        jnp.where(on_diagonal, cats_ref[...].astype(jnp.float32), 0.0), axis=1, keepdims=True
    )
    chosen = cats == (first_ref[0] + expert).astype(jnp.float32)
    part = jnp.dot(feat_ref[...], weight_ref[0], preferred_element_type=jnp.float32)
    part = jnp.where(chosen, part, 0.0)

    @pl.when(expert == 0)
    def _():
        total_ref[...] = part

    @pl.when(expert > 0)
    def _():
        total_ref[...] += part

    @pl.when(expert == pl.num_programs(0) - 1)
    def _():
        cols = out_refs[0].shape[1]
        for half, out_ref in enumerate(out_refs):
            out_ref[...] = total_ref[:, half * cols : (half + 1) * cols].astype(out_ref.dtype)


def own_queries(first_expert, cats, feat, weights):
    own, width = feat.shape
    experts = weights.shape[0]
    half = jax.ShapeDtypeStruct((own, width // HALVES), jnp.bfloat16)
    half_spec = pl.BlockSpec((own, width // HALVES), lambda expert, first_ref: (0, 0))
    return pl.pallas_call(
        project_own,
        out_shape=[half] * HALVES,
        grid_spec=pltpu.PrefetchScalarGridSpec(
            num_scalar_prefetch=1,
            grid=(experts,),
            in_specs=[
                pl.BlockSpec((1, own), lambda expert, first_ref: (0, 0)),
                pl.BlockSpec((own, width), lambda expert, first_ref: (0, 0)),
                pl.BlockSpec((1, width, width), lambda expert, first_ref: (expert, 0, 0)),
            ],
            out_specs=[half_spec] * HALVES,
            scratch_shapes=[pltpu.VMEM((own, width), jnp.float32)],
        ),
        compiler_params=pltpu.CompilerParams(dimension_semantics=("arbitrary",)),
        cost_estimate=pl.CostEstimate(
            flops=2 * own * width * width * experts,
            bytes_accessed=weights.size * 2 + own * width * 4,
            transcendentals=0,
        ),
        name="own_queries",
    )(first_expert.reshape(1), cats.reshape(1, own), feat, weights)


def spread(blocks, order_ref, same_ref, other_ref, dense_ref, *rest):
    out_refs, next_ref, all_ref = rest[:-2], rest[-2], rest[-1]
    step = pl.program_id(0)

    @pl.when(step == 0)
    def _():
        for place in range(blocks):
            next_ref[place] = order_ref[place]
        own = all_ref.shape[0] // blocks
        for place in range(blocks):
            source = (same_ref, other_ref)[2 * place // blocks]
            start = pl.multiple_of(order_ref[place] * own, own)
            all_ref[pl.ds(start, own)] = source[pl.ds((place % (blocks // 2)) * own, own)]

    product = jnp.dot(dense_ref[...], all_ref[...], preferred_element_type=jnp.float32)
    rows, first = product.shape[0], 0
    for out_ref in out_refs:
        chunks = out_ref.shape[0] // rows

        @pl.when((step >= first) & (step < first + chunks))
        def _():
            start = pl.multiple_of((step - first) * rows, rows)
            out_ref[pl.ds(start, rows)] = product.astype(out_ref.dtype)

        first += chunks


def spread_items(order, queries, dense, first, counts, rows):
    items = dense.shape[1]
    cols = queries[0].shape[1]
    blocks, chunks = order.shape[0], sum(counts)
    whole = lambda step, order_ref: (0, 0)
    return pl.pallas_call(
        functools.partial(spread, blocks),
        out_shape=[jax.ShapeDtypeStruct((count * rows, cols), jnp.bfloat16) for count in counts]
        + [jax.ShapeDtypeStruct((blocks,), jnp.int32)],
        grid_spec=pltpu.PrefetchScalarGridSpec(
            num_scalar_prefetch=1,
            grid=(chunks,),
            in_specs=[pl.BlockSpec(queries[0].shape, whole)] * 2
            + [pl.BlockSpec((rows, items), lambda step, order_ref: (first + step, 0))],
            out_specs=[pl.BlockSpec((count * rows, cols), whole) for count in counts]
            + [pl.BlockSpec(memory_space=pltpu.SMEM)],
            scratch_shapes=[pltpu.VMEM((items, cols), jnp.bfloat16)],
        ),
        compiler_params=pltpu.CompilerParams(
            dimension_semantics=("arbitrary",), vmem_limit_bytes=14 * MIB
        ),
        cost_estimate=pl.CostEstimate(
            flops=2 * chunks * rows * items * cols,
            bytes_accessed=chunks * rows * (items + cols) * 2 + items * cols * 2,
            transcendentals=0,
        ),
        name="spread_items",
    )(order, *queries, dense)


def norm_backward(pieces, user_ref, grad_ref, gain_ref, *rest):
    piece_refs, out_ref, term_ref = rest[: pieces * HALVES], rest[-2], rest[-1]
    summed = []
    for half in range(HALVES):
        total = piece_refs[half * pieces][...].astype(jnp.float32)
        for piece in range(1, pieces):
            total = total + piece_refs[half * pieces + piece][...].astype(jnp.float32)
        summed.append(total)
    width = out_ref.shape[1]
    pre_norm = user_ref[...].astype(jnp.float32) + jnp.concatenate(summed, axis=1)
    grad = grad_ref[...].astype(jnp.float32)
    scaled_grad = gain_ref[...] * grad
    inv_rms = lax.rsqrt(jnp.sum(pre_norm * pre_norm, axis=1, keepdims=True) / width + 1e-05)
    cross_mean = jnp.sum(scaled_grad * pre_norm, axis=1, keepdims=True) / width
    out_ref[...] = (
        inv_rms * scaled_grad - pre_norm * (inv_rms * inv_rms * inv_rms * cross_mean)
    ).astype(out_ref.dtype)
    term = jnp.sum(grad * pre_norm * inv_rms, axis=0, keepdims=True)

    @pl.when(pl.program_id(0) == 0)
    def _():
        term_ref[...] = term

    @pl.when(pl.program_id(0) > 0)
    def _():
        term_ref[...] += term


def user_gradient(user_feat, cotangent, gain, pieces, first, rows):
    width = user_feat.shape[1]
    block_rows = min(BLOCK_ROWS, rows)
    first_block = first // block_rows
    flat = [piece for half in pieces for piece in half]
    whole = pl.BlockSpec((block_rows, width), lambda step: (first_block + step, 0))
    part = pl.BlockSpec((block_rows, width // HALVES), lambda step: (step, 0))
    return pl.pallas_call(
        functools.partial(norm_backward, len(pieces[0])),
        out_shape=[
            jax.ShapeDtypeStruct((rows, width), jnp.bfloat16),
            jax.ShapeDtypeStruct((1, width), jnp.float32),
        ],
        grid=(rows // block_rows,),
        in_specs=[whole, whole, pl.BlockSpec((1, width), lambda step: (0, 0))] + [part] * len(flat),
        out_specs=[
            pl.BlockSpec((block_rows, width), lambda step: (step, 0)),
            pl.BlockSpec((1, width), lambda step: (0, 0)),
        ],
        compiler_params=pltpu.CompilerParams(
            dimension_semantics=("arbitrary",), vmem_limit_bytes=10 * MIB
        ),
        cost_estimate=pl.CostEstimate(
            flops=16 * rows * width,
            bytes_accessed=rows * width * 2 * (3 + len(pieces[0])),
            transcendentals=rows,
        ),
        name="user_gradient",
    )(user_feat, cotangent, gain.reshape(1, width), *flat)


def flip(value, size, bits):
    return lax.ppermute(value, "user", [(source, source ^ bits) for source in range(size)])


def gather_layers(own, size):
    return jnp.concatenate(
        [own] + [flip(own, size, 4 * layer) for layer in range(1, size // 4)], axis=0
    )


def gather_sides(own, size):
    own = jnp.concatenate([own, flip(own, size, 2)], axis=0)
    return own, flip(own, size, 1)


def gather_order(size):
    layers = size // 4
    place = jnp.arange(size, dtype=jnp.int32)
    core, side, layer = place // (size // 2), (place // layers) % 2, place % layers
    return lax.axis_index("user") ^ (layer * 4 + side * 2 + core)


def scatter_sums(halves, size):
    bits = size.bit_length() - 1
    index = lax.axis_index("user")
    orders = [list(range(bits)), [0, 2, 1] + list(range(3, bits))]
    halves = [terms.reshape((2,) * bits + terms.shape[1:]) for terms in halves]
    left = [list(reversed(range(bits))) for _ in halves]
    for stage in range(bits):
        for half, terms in enumerate(halves):
            bit = orders[half][stage]
            axis = left[half].index(bit)
            left[half].remove(bit)
            mine = (index >> bit) & 1
            own = lax.dynamic_index_in_dim(terms, mine, axis, keepdims=False)
            away = lax.dynamic_index_in_dim(terms, 1 - mine, axis, keepdims=False)
            arrived = flip(away.astype(jnp.bfloat16), size, 1 << bit)
            halves[half] = own + arrived.astype(jnp.float32)
        if 0 < stage < bits - 1:
            halves = list(lax.optimization_barrier(tuple(halves)))
    return halves


def on_device(
    user_feat, cotangent, gain, item_feat, categories, expert_w, tile_place, tile_level, tile_count
):
    users, width = user_feat.shape
    user_size, item_size = lax.axis_size("user"), lax.axis_size("item")
    item_index = lax.axis_index("item")
    own_items = item_feat.shape[1]
    items = own_items * user_size
    experts_here = expert_w.shape[0]
    first_expert = item_index * experts_here
    own_cats, own_feat = categories[0], item_feat[0]
    rows, half_width = users // ROW_CHUNKS, width // HALVES

    own_halves = own_queries(first_expert, own_cats, own_feat, expert_w)
    order = gather_order(user_size)
    weights = (tile_level[0, 0].astype(jnp.float32) * (1.0 / (2.0 * TILE))).astype(jnp.bfloat16)
    dense = dense_tiles(tile_place[0, 0], tile_count[0], weights, users, items)
    layers = [gather_layers(own, user_size) for own in own_halves]
    queries = [gather_sides(part, user_size) for part in layers]

    partials = [[] for _ in range(HALVES)]
    for half in range(HALVES):
        last = order
        for first, count in ((0, 1), (1, ROW_CHUNKS - 1)):
            *products, last = spread_items(last, queries[half], dense, first, (1,) * count, rows)
            for product in products:
                pieces = [product]
                for shift in range(1, item_size):
                    pairs = [(source, (source + shift) % item_size) for source in range(item_size)]
                    pieces.append(lax.ppermute(product, "item", pairs))
                partials[half].append(pieces)
    grads, gain_term, item_terms = [], 0.0, 0.0
    for chunk in range(ROW_CHUNKS):
        grad, term = user_gradient(
            user_feat,
            cotangent,
            gain,
            [partials[half][chunk] for half in range(HALVES)],
            chunk * rows,
            rows,
        )
        grads.append(grad)
        gain_term = gain_term + term[0]
        if chunk < ROW_CHUNKS - 1:
            item_terms = item_terms + lax.dot_general(
                dense[chunk * rows : (chunk + 1) * rows],
                grad,
                (((0,), (0,)), ((), ())),
                preferred_element_type=jnp.float32,
            )
    col_width = width // item_size
    user_grad = jnp.concatenate(
        [lax.dynamic_slice_in_dim(grad, item_index * col_width, col_width, 1) for grad in grads],
        axis=0,
    )
    gain_own = lax.dynamic_slice_in_dim(gain_term, item_index * col_width, col_width, 0)

    halves = []
    for half in range(HALVES):
        part = slice(half * half_width, (half + 1) * half_width)
        terms = item_terms[:, part] + lax.dot_general(
            dense[users - rows :],
            grads[-1][:, part],
            (((0,), (0,)), ((), ())),
            preferred_element_type=jnp.float32,
        )
        halves.append(terms.reshape(user_size, own_items, half_width))
    sums = [half.astype(jnp.bfloat16) for half in scatter_sums(halves, user_size)]

    chosen = own_cats[:, None] == first_expert + jnp.arange(experts_here, dtype=jnp.int32)[None, :]
    own_width = width // user_size
    left = jnp.where(
        chosen[:, None, :, None],
        own_feat.reshape(own_items, user_size, 1, own_width),
        jnp.zeros((), own_feat.dtype),
    ).reshape(own_items, -1)
    halves = [
        lax.dot_general(
            left, half, (((0,), (0,)), ((), ())), preferred_element_type=jnp.float32
        ).reshape(user_size, experts_here * own_width, half_width)
        for half in sums
    ]
    gain_rows = jnp.pad(gain_own, (0, 8 * half_width - col_width)).reshape(1, 8, half_width)
    gain_rows = jnp.broadcast_to(gain_rows, (user_size, 8, half_width))
    halves[0] = jnp.concatenate([halves[0], gain_rows], axis=1)
    halves = scatter_sums(halves, user_size)
    gain_grad = halves[0][-8:].reshape(-1)[:col_width]
    expert_grad = jnp.concatenate([halves[0][:-8], halves[1]], axis=1)
    own_sums = jnp.concatenate(sums, axis=1)
    item_total = jnp.zeros((own_items, width), jnp.float32)
    for expert in range(experts_here):
        item_total = item_total + jnp.where(
            chosen[:, expert][:, None],
            lax.dot_general(
                own_sums,
                expert_w[expert],
                (((1,), (1,)), ((), ())),
                preferred_element_type=jnp.float32,
            ),
            0.0,
        )
    return (
        user_grad,
        item_total.astype(jnp.bfloat16)[None],
        expert_grad.reshape(experts_here, own_width, width),
        gain_grad,
    )


def solution(mesh):
    placed = (
        P("user", None),
        P("user", None),
        P(),
        P("item", "user", None),
        P("item", "user"),
        P("item", None, None),
        P("user", "item", None),
        P("user", "item", None, None, None),
        P("user", "item"),
    )
    return jax.shard_map(
        on_device,
        mesh=mesh,
        in_specs=placed,
        out_specs=(P("user", "item"), P("item", "user", None), P("item", "user", None), P("item")),
        check_vma=False,
    )
```

```python
import functools

import jax
import jax.numpy as jnp
from jax import lax
from jax.experimental import pallas as pl
from jax.experimental.pallas import tpu as pltpu
from jax.sharding import PartitionSpec as P

TILE = 128
SLOTS_PER_STEP = 8
HALVES = 2
ROW_CHUNKS = 4
BLOCK_ROWS = 256
MIB = 1024 * 1024


def place_tiles(item_blocks, place_ref, count_ref, level_ref, dense_ref):
    step = pl.program_id(0)

    @pl.when(step == 0)
    def _():
        dense_ref[...] = jnp.zeros_like(dense_ref)

    for offset in range(level_ref.shape[0]):
        slot = step * level_ref.shape[0] + offset

        @pl.when(slot < count_ref[0])
        def _():
            place = place_ref[slot]
            row = pl.multiple_of((place // item_blocks) * TILE, TILE)
            col = pl.multiple_of((place % item_blocks) * TILE, TILE)
            weights = level_ref[offset].astype(jnp.float32) * (1.0 / (2.0 * TILE))
            dense_ref[pl.ds(row, TILE), pl.ds(col, TILE)] = weights.astype(jnp.bfloat16)


def dense_tiles(place, count, level, users, items):
    slots = level.shape[0]
    per_step = SLOTS_PER_STEP if slots % SLOTS_PER_STEP == 0 else 1
    return pl.pallas_call(
        functools.partial(place_tiles, items // TILE),
        out_shape=jax.ShapeDtypeStruct((users, items), jnp.bfloat16),
        grid_spec=pltpu.PrefetchScalarGridSpec(
            num_scalar_prefetch=2,
            grid=(slots // per_step,),
            in_specs=[
                pl.BlockSpec((per_step, TILE, TILE), lambda step, place_ref, count_ref: (step, 0, 0))
            ],
            out_specs=pl.BlockSpec((users, items), lambda step, place_ref, count_ref: (0, 0)),
        ),
        compiler_params=pltpu.CompilerParams(
            dimension_semantics=("arbitrary",), vmem_limit_bytes=16 * MIB
        ),
        cost_estimate=pl.CostEstimate(
            flops=slots * TILE * TILE,
            bytes_accessed=slots * TILE * TILE * 4 + users * items * 2,
            transcendentals=0,
        ),
        name="place_tiles",
    )(place, count, level)


def project_own(first_ref, cats_ref, feat_ref, weight_ref, *rest):
    out_refs, total_ref = rest[:-1], rest[-1]
    expert = pl.program_id(0)
    own = feat_ref.shape[0]
    on_diagonal = lax.broadcasted_iota(jnp.int32, (own, own), 0) == lax.broadcasted_iota(
        jnp.int32, (own, own), 1
    )
    cats = jnp.sum(
        jnp.where(on_diagonal, cats_ref[...].astype(jnp.float32), 0.0), axis=1, keepdims=True
    )
    chosen = cats == (first_ref[0] + expert).astype(jnp.float32)
    part = jnp.dot(feat_ref[...], weight_ref[0], preferred_element_type=jnp.float32)
    part = jnp.where(chosen, part, 0.0)

    @pl.when(expert == 0)
    def _():
        total_ref[...] = part

    @pl.when(expert > 0)
    def _():
        total_ref[...] += part

    @pl.when(expert == pl.num_programs(0) - 1)
    def _():
        cols = out_refs[0].shape[1]
        for half, out_ref in enumerate(out_refs):
            out_ref[...] = total_ref[:, half * cols : (half + 1) * cols].astype(out_ref.dtype)


def own_queries(first_expert, cats, feat, weights):
    own, width = feat.shape
    experts = weights.shape[0]
    half = jax.ShapeDtypeStruct((own, width // HALVES), jnp.bfloat16)
    half_spec = pl.BlockSpec((own, width // HALVES), lambda expert, first_ref: (0, 0))
    return pl.pallas_call(
        project_own,
        out_shape=[half] * HALVES,
        grid_spec=pltpu.PrefetchScalarGridSpec(
            num_scalar_prefetch=1,
            grid=(experts,),
            in_specs=[
                pl.BlockSpec((1, own), lambda expert, first_ref: (0, 0)),
                pl.BlockSpec((own, width), lambda expert, first_ref: (0, 0)),
                pl.BlockSpec((1, width, width), lambda expert, first_ref: (expert, 0, 0)),
            ],
            out_specs=[half_spec] * HALVES,
            scratch_shapes=[pltpu.VMEM((own, width), jnp.float32)],
        ),
        compiler_params=pltpu.CompilerParams(dimension_semantics=("arbitrary",)),
        cost_estimate=pl.CostEstimate(
            flops=2 * own * width * width * experts,
            bytes_accessed=weights.size * 2 + own * width * 4,
            transcendentals=0,
        ),
        name="own_queries",
    )(first_expert.reshape(1), cats.reshape(1, own), feat, weights)


def spread(blocks, order_ref, *rest):
    source_refs, dense_ref, out_refs, next_ref, all_ref = rest[:4], rest[4], rest[5:-2], *rest[-2:]
    step = pl.program_id(0)

    @pl.when(step == 0)
    def _():
        for place in range(blocks):
            next_ref[place] = order_ref[place]
        own = all_ref.shape[0] // blocks
        for place in range(blocks):
            source = source_refs[4 * place // blocks]
            start = pl.multiple_of(order_ref[place] * own, own)
            all_ref[pl.ds(start, own)] = source[pl.ds((place % (blocks // 4)) * own, own)]

    product = jnp.dot(dense_ref[...], all_ref[...], preferred_element_type=jnp.float32)
    rows, first = product.shape[0], 0
    for out_ref in out_refs:
        chunks = out_ref.shape[0] // rows

        @pl.when((step >= first) & (step < first + chunks))
        def _():
            start = pl.multiple_of((step - first) * rows, rows)
            out_ref[pl.ds(start, rows)] = product.astype(out_ref.dtype)

        first += chunks


def spread_items(order, queries, dense, first, counts, rows):
    items = dense.shape[1]
    cols = queries[0].shape[1]
    blocks, chunks = order.shape[0], sum(counts)
    whole = lambda step, order_ref: (0, 0)
    return pl.pallas_call(
        functools.partial(spread, blocks),
        out_shape=[jax.ShapeDtypeStruct((count * rows, cols), jnp.bfloat16) for count in counts]
        + [jax.ShapeDtypeStruct((blocks,), jnp.int32)],
        grid_spec=pltpu.PrefetchScalarGridSpec(
            num_scalar_prefetch=1,
            grid=(chunks,),
            in_specs=[pl.BlockSpec(queries[0].shape, whole)] * 4
            + [pl.BlockSpec((rows, items), lambda step, order_ref: (first + step, 0))],
            out_specs=[pl.BlockSpec((count * rows, cols), whole) for count in counts]
            + [pl.BlockSpec(memory_space=pltpu.SMEM)],
            scratch_shapes=[pltpu.VMEM((items, cols), jnp.bfloat16)],
        ),
        compiler_params=pltpu.CompilerParams(
            dimension_semantics=("arbitrary",), vmem_limit_bytes=14 * MIB
        ),
        cost_estimate=pl.CostEstimate(
            flops=2 * chunks * rows * items * cols,
            bytes_accessed=chunks * rows * (items + cols) * 2 + items * cols * 2,
            transcendentals=0,
        ),
        name="spread_items",
    )(order, *queries, dense)


def norm_backward(pieces, user_ref, grad_ref, gain_ref, *rest):
    piece_refs, out_ref, term_ref = rest[: pieces * HALVES], rest[-2], rest[-1]
    summed = []
    for half in range(HALVES):
        total = piece_refs[half * pieces][...].astype(jnp.float32)
        for piece in range(1, pieces):
            total = total + piece_refs[half * pieces + piece][...].astype(jnp.float32)
        summed.append(total)
    width = out_ref.shape[1]
    pre_norm = user_ref[...].astype(jnp.float32) + jnp.concatenate(summed, axis=1)
    grad = grad_ref[...].astype(jnp.float32)
    scaled_grad = gain_ref[...] * grad
    inv_rms = lax.rsqrt(jnp.sum(pre_norm * pre_norm, axis=1, keepdims=True) / width + 1e-05)
    cross_mean = jnp.sum(scaled_grad * pre_norm, axis=1, keepdims=True) / width
    out_ref[...] = (
        inv_rms * scaled_grad - pre_norm * (inv_rms * inv_rms * inv_rms * cross_mean)
    ).astype(out_ref.dtype)
    term = jnp.sum(grad * pre_norm * inv_rms, axis=0, keepdims=True)

    @pl.when(pl.program_id(0) == 0)
    def _():
        term_ref[...] = term

    @pl.when(pl.program_id(0) > 0)
    def _():
        term_ref[...] += term


def user_gradient(user_feat, cotangent, gain, pieces, first, rows):
    width = user_feat.shape[1]
    block_rows = min(BLOCK_ROWS, rows)
    first_block = first // block_rows
    flat = [piece for half in pieces for piece in half]
    whole = pl.BlockSpec((block_rows, width), lambda step: (first_block + step, 0))
    part = pl.BlockSpec((block_rows, width // HALVES), lambda step: (step, 0))
    return pl.pallas_call(
        functools.partial(norm_backward, len(pieces[0])),
        out_shape=[
            jax.ShapeDtypeStruct((rows, width), jnp.bfloat16),
            jax.ShapeDtypeStruct((1, width), jnp.float32),
        ],
        grid=(rows // block_rows,),
        in_specs=[whole, whole, pl.BlockSpec((1, width), lambda step: (0, 0))] + [part] * len(flat),
        out_specs=[
            pl.BlockSpec((block_rows, width), lambda step: (step, 0)),
            pl.BlockSpec((1, width), lambda step: (0, 0)),
        ],
        compiler_params=pltpu.CompilerParams(
            dimension_semantics=("arbitrary",), vmem_limit_bytes=10 * MIB
        ),
        cost_estimate=pl.CostEstimate(
            flops=16 * rows * width,
            bytes_accessed=rows * width * 2 * (3 + len(pieces[0])),
            transcendentals=rows,
        ),
        name="user_gradient",
    )(user_feat, cotangent, gain.reshape(1, width), *flat)


def flip(value, size, bits):
    return lax.ppermute(value, "user", [(source, source ^ bits) for source in range(size)])


def gather_layers(own, size):
    return jnp.concatenate(
        [own] + [flip(own, size, 4 * layer) for layer in range(1, size // 4)], axis=0
    )


def gather_sides(own, size):
    other = flip(own, size, 2)
    return own, other, flip(own, size, 1), flip(other, size, 1)


def gather_order(size):
    layers = size // 4
    place = jnp.arange(size, dtype=jnp.int32)
    core, side, layer = place // (size // 2), (place // layers) % 2, place % layers
    return lax.axis_index("user") ^ (layer * 4 + side * 2 + core)


def scatter_sums(halves, size):
    bits = size.bit_length() - 1
    index = lax.axis_index("user")
    orders = [list(range(bits)), [0, 2, 1] + list(range(3, bits))]
    halves = [terms.reshape((2,) * bits + terms.shape[1:]) for terms in halves]
    left = [list(reversed(range(bits))) for _ in halves]
    for stage in range(bits):
        for half, terms in enumerate(halves):
            bit = orders[half][stage]
            axis = left[half].index(bit)
            left[half].remove(bit)
            mine = (index >> bit) & 1
            own = lax.dynamic_index_in_dim(terms, mine, axis, keepdims=False)
            away = lax.dynamic_index_in_dim(terms, 1 - mine, axis, keepdims=False)
            arrived = flip(away.astype(jnp.bfloat16), size, 1 << bit)
            halves[half] = own + arrived.astype(jnp.float32)
        if 0 < stage < bits - 1:
            halves = list(lax.optimization_barrier(tuple(halves)))
    return halves


def on_device(
    user_feat, cotangent, gain, item_feat, categories, expert_w, tile_place, tile_level, tile_count
):
    users, width = user_feat.shape
    user_size, item_size = lax.axis_size("user"), lax.axis_size("item")
    item_index = lax.axis_index("item")
    own_items = item_feat.shape[1]
    items = own_items * user_size
    experts_here = expert_w.shape[0]
    first_expert = item_index * experts_here
    own_cats, own_feat = categories[0], item_feat[0]
    rows, half_width = users // ROW_CHUNKS, width // HALVES

    own_halves = own_queries(first_expert, own_cats, own_feat, expert_w)
    order = gather_order(user_size)
    dense = dense_tiles(tile_place[0, 0], tile_count[0], tile_level[0, 0], users, items)
    layers = [gather_layers(own, user_size) for own in own_halves]
    queries = [gather_sides(part, user_size) for part in layers]

    partials = [[] for _ in range(HALVES)]
    for half in range(HALVES):
        for first, count in ((0, 1), (1, ROW_CHUNKS - 1)):
            *products, _ = spread_items(order, queries[half], dense, first, (1,) * count, rows)
            for product in products:
                pieces = [product]
                for shift in range(1, item_size):
                    pairs = [(source, (source + shift) % item_size) for source in range(item_size)]
                    pieces.append(lax.ppermute(product, "item", pairs))
                partials[half].append(pieces)
    grads, gain_term, item_terms = [None] * ROW_CHUNKS, 0.0, 0.0
    chunk_order = [0] + list(range(ROW_CHUNKS - 1, 0, -1))
    for chunk in chunk_order:
        grad, term = user_gradient(
            user_feat,
            cotangent,
            gain,
            [partials[half][chunk] for half in range(HALVES)],
            chunk * rows,
            rows,
        )
        grads[chunk] = grad
        gain_term = gain_term + term[0]
        if chunk != chunk_order[-1]:
            item_terms = item_terms + lax.dot_general(
                dense[chunk * rows : (chunk + 1) * rows],
                grad,
                (((0,), (0,)), ((), ())),
                preferred_element_type=jnp.float32,
            )
    col_width = width // item_size
    user_grad = jnp.concatenate(
        [lax.dynamic_slice_in_dim(grad, item_index * col_width, col_width, 1) for grad in grads],
        axis=0,
    )
    gain_own = lax.dynamic_slice_in_dim(gain_term, item_index * col_width, col_width, 0)

    halves = []
    for half in range(HALVES):
        part = slice(half * half_width, (half + 1) * half_width)
        terms = item_terms[:, part] + lax.dot_general(
            dense[chunk_order[-1] * rows : (chunk_order[-1] + 1) * rows],
            grads[chunk_order[-1]][:, part],
            (((0,), (0,)), ((), ())),
            preferred_element_type=jnp.float32,
        )
        halves.append(terms.reshape(user_size, own_items, half_width))
    sums = [half.astype(jnp.bfloat16) for half in scatter_sums(halves, user_size)]

    chosen = own_cats[:, None] == first_expert + jnp.arange(experts_here, dtype=jnp.int32)[None, :]
    own_width = width // user_size
    left = jnp.where(
        chosen[:, None, :, None],
        own_feat.reshape(own_items, user_size, 1, own_width),
        jnp.zeros((), own_feat.dtype),
    ).reshape(own_items, -1)
    halves = [
        lax.dot_general(
            left, half, (((0,), (0,)), ((), ())), preferred_element_type=jnp.float32
        ).reshape(user_size, experts_here * own_width, half_width)
        for half in sums
    ]
    gain_rows = jnp.pad(gain_own, (0, 8 * half_width - col_width)).reshape(1, 8, half_width)
    gain_rows = jnp.broadcast_to(gain_rows, (user_size, 8, half_width))
    halves[0] = jnp.concatenate([halves[0], gain_rows], axis=1)
    halves = scatter_sums(halves, user_size)
    gain_grad = halves[0][-8:].reshape(-1)[:col_width]
    expert_grad = jnp.concatenate([halves[0][:-8], halves[1]], axis=1)
    own_sums = jnp.concatenate(sums, axis=1)
    item_total = jnp.zeros((own_items, width), jnp.float32)
    for expert in range(experts_here):
        item_total = item_total + jnp.where(
            chosen[:, expert][:, None],
            lax.dot_general(
                own_sums,
                expert_w[expert],
                (((1,), (1,)), ((), ())),
                preferred_element_type=jnp.float32,
            ),
            0.0,
        )
    return (
        user_grad,
        item_total.astype(jnp.bfloat16)[None],
        expert_grad.reshape(experts_here, own_width, width),
        gain_grad,
    )


def solution(mesh):
    placed = (
        P("user", None),
        P("user", None),
        P(),
        P("item", "user", None),
        P("item", "user"),
        P("item", None, None),
        P("user", "item", None),
        P("user", "item", None, None, None),
        P("user", "item"),
    )
    return jax.shard_map(
        on_device,
        mesh=mesh,
        in_specs=placed,
        out_specs=(P("user", "item"), P("item", "user", None), P("item", "user", None), P("item")),
        check_vma=False,
    )
```

```python
import functools

import jax
import jax.numpy as jnp
from jax import lax
from jax.experimental import pallas as pl
from jax.experimental.pallas import tpu as pltpu
from jax.sharding import PartitionSpec as P

TILE = 128
SLOTS_PER_STEP = 8
HALVES = 2
ROW_CHUNKS = 4
BLOCK_ROWS = 256
MIB = 1024 * 1024


def place_tiles(item_blocks, place_ref, count_ref, level_ref, dense_ref):
    step = pl.program_id(0)

    @pl.when(step == 0)
    def _():
        dense_ref[...] = jnp.zeros_like(dense_ref)

    for offset in range(level_ref.shape[0]):
        slot = step * level_ref.shape[0] + offset

        @pl.when(slot < count_ref[0])
        def _():
            place = place_ref[slot]
            row = pl.multiple_of((place // item_blocks) * TILE, TILE)
            col = pl.multiple_of((place % item_blocks) * TILE, TILE)
            weights = level_ref[offset].astype(jnp.float32) * (1.0 / (2.0 * TILE))
            dense_ref[pl.ds(row, TILE), pl.ds(col, TILE)] = weights.astype(jnp.bfloat16)


def dense_tiles(place, count, level, users, items):
    slots = level.shape[0]
    per_step = SLOTS_PER_STEP if slots % SLOTS_PER_STEP == 0 else 1
    return pl.pallas_call(
        functools.partial(place_tiles, items // TILE),
        out_shape=jax.ShapeDtypeStruct((users, items), jnp.bfloat16),
        grid_spec=pltpu.PrefetchScalarGridSpec(
            num_scalar_prefetch=2,
            grid=(slots // per_step,),
            in_specs=[
                pl.BlockSpec((per_step, TILE, TILE), lambda step, place_ref, count_ref: (step, 0, 0))
            ],
            out_specs=pl.BlockSpec((users, items), lambda step, place_ref, count_ref: (0, 0)),
        ),
        compiler_params=pltpu.CompilerParams(
            dimension_semantics=("arbitrary",), vmem_limit_bytes=16 * MIB
        ),
        cost_estimate=pl.CostEstimate(
            flops=slots * TILE * TILE,
            bytes_accessed=slots * TILE * TILE * 4 + users * items * 2,
            transcendentals=0,
        ),
        name="place_tiles",
    )(place, count, level)


def project_own(first_ref, cats_ref, feat_ref, weight_ref, *rest):
    out_refs, total_ref = rest[:-1], rest[-1]
    expert = pl.program_id(0)
    own = feat_ref.shape[0]
    on_diagonal = lax.broadcasted_iota(jnp.int32, (own, own), 0) == lax.broadcasted_iota(
        jnp.int32, (own, own), 1
    )
    cats = jnp.sum(
        jnp.where(on_diagonal, cats_ref[...].astype(jnp.float32), 0.0), axis=1, keepdims=True
    )
    chosen = cats == (first_ref[0] + expert).astype(jnp.float32)
    part = jnp.dot(feat_ref[...], weight_ref[0], preferred_element_type=jnp.float32)
    part = jnp.where(chosen, part, 0.0)

    @pl.when(expert == 0)
    def _():
        total_ref[...] = part

    @pl.when(expert > 0)
    def _():
        total_ref[...] += part

    @pl.when(expert == pl.num_programs(0) - 1)
    def _():
        cols = out_refs[0].shape[1]
        for half, out_ref in enumerate(out_refs):
            out_ref[...] = total_ref[:, half * cols : (half + 1) * cols].astype(out_ref.dtype)


def own_queries(first_expert, cats, feat, weights):
    own, width = feat.shape
    experts = weights.shape[0]
    half = jax.ShapeDtypeStruct((own, width // HALVES), jnp.bfloat16)
    half_spec = pl.BlockSpec((own, width // HALVES), lambda expert, first_ref: (0, 0))
    return pl.pallas_call(
        project_own,
        out_shape=[half] * HALVES,
        grid_spec=pltpu.PrefetchScalarGridSpec(
            num_scalar_prefetch=1,
            grid=(experts,),
            in_specs=[
                pl.BlockSpec((1, own), lambda expert, first_ref: (0, 0)),
                pl.BlockSpec((own, width), lambda expert, first_ref: (0, 0)),
                pl.BlockSpec((1, width, width), lambda expert, first_ref: (expert, 0, 0)),
            ],
            out_specs=[half_spec] * HALVES,
            scratch_shapes=[pltpu.VMEM((own, width), jnp.float32)],
        ),
        compiler_params=pltpu.CompilerParams(dimension_semantics=("arbitrary",)),
        cost_estimate=pl.CostEstimate(
            flops=2 * own * width * width * experts,
            bytes_accessed=weights.size * 2 + own * width * 4,
            transcendentals=0,
        ),
        name="own_queries",
    )(first_expert.reshape(1), cats.reshape(1, own), feat, weights)


def spread(blocks, order_ref, *rest):
    source_refs, dense_ref, out_refs, next_ref, all_ref = rest[:4], rest[4], rest[5:-2], *rest[-2:]
    step = pl.program_id(0)

    @pl.when(step == 0)
    def _():
        for place in range(blocks):
            next_ref[place] = order_ref[place]
        own = all_ref.shape[0] // blocks
        for place in range(blocks):
            source = source_refs[4 * place // blocks]
            start = pl.multiple_of(order_ref[place] * own, own)
            all_ref[pl.ds(start, own)] = source[pl.ds((place % (blocks // 4)) * own, own)]

    product = jnp.dot(dense_ref[...], all_ref[...], preferred_element_type=jnp.float32)
    rows, first = product.shape[0], 0
    for out_ref in out_refs:
        chunks = out_ref.shape[0] // rows

        @pl.when((step >= first) & (step < first + chunks))
        def _():
            start = pl.multiple_of((step - first) * rows, rows)
            out_ref[pl.ds(start, rows)] = product.astype(out_ref.dtype)

        first += chunks


def spread_items(order, queries, dense, first, counts, rows):
    items = dense.shape[1]
    cols = queries[0].shape[1]
    blocks, chunks = order.shape[0], sum(counts)
    whole = lambda step, order_ref: (0, 0)
    return pl.pallas_call(
        functools.partial(spread, blocks),
        out_shape=[jax.ShapeDtypeStruct((count * rows, cols), jnp.bfloat16) for count in counts]
        + [jax.ShapeDtypeStruct((blocks,), jnp.int32)],
        grid_spec=pltpu.PrefetchScalarGridSpec(
            num_scalar_prefetch=1,
            grid=(chunks,),
            in_specs=[pl.BlockSpec(queries[0].shape, whole)] * 4
            + [pl.BlockSpec((rows, items), lambda step, order_ref: (first + step, 0))],
            out_specs=[pl.BlockSpec((count * rows, cols), whole) for count in counts]
            + [pl.BlockSpec(memory_space=pltpu.SMEM)],
            scratch_shapes=[pltpu.VMEM((items, cols), jnp.bfloat16)],
        ),
        compiler_params=pltpu.CompilerParams(
            dimension_semantics=("arbitrary",), vmem_limit_bytes=14 * MIB
        ),
        cost_estimate=pl.CostEstimate(
            flops=2 * chunks * rows * items * cols,
            bytes_accessed=chunks * rows * (items + cols) * 2 + items * cols * 2,
            transcendentals=0,
        ),
        name="spread_items",
    )(order, *queries, dense)


def norm_backward(pieces, user_ref, grad_ref, gain_ref, *rest):
    piece_refs, out_ref, term_ref = rest[: pieces * HALVES], rest[-2], rest[-1]
    summed = []
    for half in range(HALVES):
        total = piece_refs[half * pieces][...].astype(jnp.float32)
        for piece in range(1, pieces):
            total = total + piece_refs[half * pieces + piece][...].astype(jnp.float32)
        summed.append(total)
    width = out_ref.shape[1]
    pre_norm = user_ref[...].astype(jnp.float32) + jnp.concatenate(summed, axis=1)
    grad = grad_ref[...].astype(jnp.float32)
    scaled_grad = gain_ref[...] * grad
    inv_rms = lax.rsqrt(jnp.sum(pre_norm * pre_norm, axis=1, keepdims=True) / width + 1e-05)
    cross_mean = jnp.sum(scaled_grad * pre_norm, axis=1, keepdims=True) / width
    out_ref[...] = (
        inv_rms * scaled_grad - pre_norm * (inv_rms * inv_rms * inv_rms * cross_mean)
    ).astype(out_ref.dtype)
    term = jnp.sum(grad * pre_norm * inv_rms, axis=0, keepdims=True)

    @pl.when(pl.program_id(0) == 0)
    def _():
        term_ref[...] = term

    @pl.when(pl.program_id(0) > 0)
    def _():
        term_ref[...] += term


def user_gradient(user_feat, cotangent, gain, pieces, first, rows):
    width = user_feat.shape[1]
    block_rows = min(BLOCK_ROWS, rows)
    first_block = first // block_rows
    flat = [piece for half in pieces for piece in half]
    whole = pl.BlockSpec((block_rows, width), lambda step: (first_block + step, 0))
    part = pl.BlockSpec((block_rows, width // HALVES), lambda step: (step, 0))
    return pl.pallas_call(
        functools.partial(norm_backward, len(pieces[0])),
        out_shape=[
            jax.ShapeDtypeStruct((rows, width), jnp.bfloat16),
            jax.ShapeDtypeStruct((1, width), jnp.float32),
        ],
        grid=(rows // block_rows,),
        in_specs=[whole, whole, pl.BlockSpec((1, width), lambda step: (0, 0))] + [part] * len(flat),
        out_specs=[
            pl.BlockSpec((block_rows, width), lambda step: (step, 0)),
            pl.BlockSpec((1, width), lambda step: (0, 0)),
        ],
        compiler_params=pltpu.CompilerParams(
            dimension_semantics=("arbitrary",), vmem_limit_bytes=10 * MIB
        ),
        cost_estimate=pl.CostEstimate(
            flops=16 * rows * width,
            bytes_accessed=rows * width * 2 * (3 + len(pieces[0])),
            transcendentals=rows,
        ),
        name="user_gradient",
    )(user_feat, cotangent, gain.reshape(1, width), *flat)


def flip(value, size, bits):
    return lax.ppermute(value, "user", [(source, source ^ bits) for source in range(size)])


def gather_layers(own, size):
    return jnp.concatenate(
        [own] + [flip(own, size, 4 * layer) for layer in range(1, size // 4)], axis=0
    )


def gather_sides(own, size):
    other = flip(own, size, 2)
    return own, other, flip(own, size, 1), flip(other, size, 1)


def gather_order(size):
    layers = size // 4
    place = jnp.arange(size, dtype=jnp.int32)
    core, side, layer = place // (size // 2), (place // layers) % 2, place % layers
    return lax.axis_index("user") ^ (layer * 4 + side * 2 + core)


def scatter_sum(terms, size, order):
    bits = size.bit_length() - 1
    index = lax.axis_index("user")
    left = list(reversed(range(bits)))
    terms = terms.reshape((2,) * bits + terms.shape[1:])
    for bit in order:
        axis = left.index(bit)
        left.remove(bit)
        mine = (index >> bit) & 1
        own = lax.dynamic_index_in_dim(terms, mine, axis, keepdims=False)
        away = lax.dynamic_index_in_dim(terms, 1 - mine, axis, keepdims=False)
        terms = own + flip(away.astype(jnp.bfloat16), size, 1 << bit).astype(jnp.float32)
    return terms


def scatter_sums(halves, size):
    bits = size.bit_length() - 1
    orders = [list(range(bits)), [0, 2, 1] + list(range(3, bits))]
    return [scatter_sum(terms, size, order) for terms, order in zip(halves, orders)]


def on_device(
    user_feat, cotangent, gain, item_feat, categories, expert_w, tile_place, tile_level, tile_count
):
    users, width = user_feat.shape
    user_size, item_size = lax.axis_size("user"), lax.axis_size("item")
    item_index = lax.axis_index("item")
    own_items = item_feat.shape[1]
    items = own_items * user_size
    experts_here = expert_w.shape[0]
    first_expert = item_index * experts_here
    own_cats, own_feat = categories[0], item_feat[0]
    rows, half_width = users // ROW_CHUNKS, width // HALVES

    own_halves = own_queries(first_expert, own_cats, own_feat, expert_w)
    order = gather_order(user_size)
    dense = dense_tiles(tile_place[0, 0], tile_count[0], tile_level[0, 0], users, items)
    layers = [gather_layers(own, user_size) for own in own_halves]
    queries = [gather_sides(part, user_size) for part in layers]

    partials = [[] for _ in range(HALVES)]
    for half in range(HALVES):
        for first, count in ((0, 1), (1, ROW_CHUNKS - 1)):
            *products, _ = spread_items(order, queries[half], dense, first, (1,) * count, rows)
            for product in products:
                pieces = [product]
                for shift in range(1, item_size):
                    pairs = [(source, (source + shift) % item_size) for source in range(item_size)]
                    pieces.append(lax.ppermute(product, "item", pairs))
                partials[half].append(pieces)
    grads, gain_term, item_terms = [None] * ROW_CHUNKS, 0.0, 0.0
    chunk_order = [0] + list(range(ROW_CHUNKS - 1, 0, -1))
    for chunk in chunk_order:
        grad, term = user_gradient(
            user_feat,
            cotangent,
            gain,
            [partials[half][chunk] for half in range(HALVES)],
            chunk * rows,
            rows,
        )
        grads[chunk] = grad
        gain_term = gain_term + term[0]
        if chunk != chunk_order[-1]:
            item_terms = item_terms + lax.dot_general(
                dense[chunk * rows : (chunk + 1) * rows],
                grad,
                (((0,), (0,)), ((), ())),
                preferred_element_type=jnp.float32,
            )
    col_width = width // item_size
    user_grad = jnp.concatenate(
        [lax.dynamic_slice_in_dim(grad, item_index * col_width, col_width, 1) for grad in grads],
        axis=0,
    )
    gain_own = lax.dynamic_slice_in_dim(gain_term, item_index * col_width, col_width, 0)

    halves = []
    for half in range(HALVES):
        part = slice(half * half_width, (half + 1) * half_width)
        terms = item_terms[:, part] + lax.dot_general(
            dense[chunk_order[-1] * rows : (chunk_order[-1] + 1) * rows],
            grads[chunk_order[-1]][:, part],
            (((0,), (0,)), ((), ())),
            preferred_element_type=jnp.float32,
        )
        halves.append(terms.reshape(user_size, own_items, half_width))
    sums = [half.astype(jnp.bfloat16) for half in scatter_sums(halves, user_size)]

    chosen = own_cats[:, None] == first_expert + jnp.arange(experts_here, dtype=jnp.int32)[None, :]
    own_width = width // user_size
    left = jnp.where(
        chosen[:, None, :, None],
        own_feat.reshape(own_items, user_size, 1, own_width),
        jnp.zeros((), own_feat.dtype),
    ).reshape(own_items, -1)
    halves = [
        lax.dot_general(
            left, half, (((0,), (0,)), ((), ())), preferred_element_type=jnp.float32
        ).reshape(user_size, experts_here * own_width, half_width)
        for half in sums
    ]
    gain_rows = jnp.pad(gain_own, (0, 8 * half_width - col_width)).reshape(1, 8, half_width)
    gain_rows = jnp.broadcast_to(gain_rows, (user_size, 8, half_width))
    halves[0] = jnp.concatenate([halves[0], gain_rows], axis=1)
    halves = scatter_sums(halves, user_size)
    gain_grad = halves[0][-8:].reshape(-1)[:col_width]
    expert_grad = jnp.concatenate([halves[0][:-8], halves[1]], axis=1)
    own_sums = jnp.concatenate(sums, axis=1)
    item_total = jnp.zeros((own_items, width), jnp.float32)
    for expert in range(experts_here):
        item_total = item_total + jnp.where(
            chosen[:, expert][:, None],
            lax.dot_general(
                own_sums,
                expert_w[expert],
                (((1,), (1,)), ((), ())),
                preferred_element_type=jnp.float32,
            ),
            0.0,
        )
    return (
        user_grad,
        item_total.astype(jnp.bfloat16)[None],
        expert_grad.reshape(experts_here, own_width, width),
        gain_grad,
    )


def solution(mesh):
    placed = (
        P("user", None),
        P("user", None),
        P(),
        P("item", "user", None),
        P("item", "user"),
        P("item", None, None),
        P("user", "item", None),
        P("user", "item", None, None, None),
        P("user", "item"),
    )
    return jax.shard_map(
        on_device,
        mesh=mesh,
        in_specs=placed,
        out_specs=(P("user", "item"), P("item", "user", None), P("item", "user", None), P("item")),
        check_vma=False,
    )
```

```python
import functools

import jax
import jax.numpy as jnp
from jax import lax
from jax.experimental import pallas as pl
from jax.experimental.pallas import tpu as pltpu
from jax.sharding import PartitionSpec as P

TILE = 128
SLOTS_PER_STEP = 8
HALVES = 2
ROW_CHUNKS = 4
BLOCK_ROWS = 256
MIB = 1024 * 1024


def place_tiles(item_blocks, place_ref, count_ref, level_ref, dense_ref):
    step = pl.program_id(0)

    @pl.when(step == 0)
    def _():
        dense_ref[...] = jnp.zeros_like(dense_ref)

    for offset in range(level_ref.shape[0]):
        slot = step * level_ref.shape[0] + offset

        @pl.when(slot < count_ref[0])
        def _():
            place = place_ref[slot]
            row = pl.multiple_of((place // item_blocks) * TILE, TILE)
            col = pl.multiple_of((place % item_blocks) * TILE, TILE)
            weights = level_ref[offset].astype(jnp.float32) * (1.0 / (2.0 * TILE))
            dense_ref[pl.ds(row, TILE), pl.ds(col, TILE)] = weights.astype(jnp.bfloat16)


def dense_tiles(place, count, level, users, items):
    slots = level.shape[0]
    per_step = SLOTS_PER_STEP if slots % SLOTS_PER_STEP == 0 else 1
    return pl.pallas_call(
        functools.partial(place_tiles, items // TILE),
        out_shape=jax.ShapeDtypeStruct((users, items), jnp.bfloat16),
        grid_spec=pltpu.PrefetchScalarGridSpec(
            num_scalar_prefetch=2,
            grid=(slots // per_step,),
            in_specs=[
                pl.BlockSpec((per_step, TILE, TILE), lambda step, place_ref, count_ref: (step, 0, 0))
            ],
            out_specs=pl.BlockSpec((users, items), lambda step, place_ref, count_ref: (0, 0)),
        ),
        compiler_params=pltpu.CompilerParams(
            dimension_semantics=("arbitrary",), vmem_limit_bytes=16 * MIB
        ),
        cost_estimate=pl.CostEstimate(
            flops=slots * TILE * TILE,
            bytes_accessed=slots * TILE * TILE * 4 + users * items * 2,
            transcendentals=0,
        ),
        name="place_tiles",
    )(place, count, level)


def project_own(first_ref, cats_ref, feat_ref, weight_ref, *rest):
    out_refs, total_ref = rest[:-1], rest[-1]
    expert = pl.program_id(0)
    own = feat_ref.shape[0]
    on_diagonal = lax.broadcasted_iota(jnp.int32, (own, own), 0) == lax.broadcasted_iota(
        jnp.int32, (own, own), 1
    )
    cats = jnp.sum(
        jnp.where(on_diagonal, cats_ref[...].astype(jnp.float32), 0.0), axis=1, keepdims=True
    )
    chosen = cats == (first_ref[0] + expert).astype(jnp.float32)
    part = jnp.dot(feat_ref[...], weight_ref[0], preferred_element_type=jnp.float32)
    part = jnp.where(chosen, part, 0.0)

    @pl.when(expert == 0)
    def _():
        total_ref[...] = part

    @pl.when(expert > 0)
    def _():
        total_ref[...] += part

    @pl.when(expert == pl.num_programs(0) - 1)
    def _():
        cols = out_refs[0].shape[1]
        for half, out_ref in enumerate(out_refs):
            out_ref[...] = total_ref[:, half * cols : (half + 1) * cols].astype(out_ref.dtype)


def own_queries(first_expert, cats, feat, weights):
    own, width = feat.shape
    experts = weights.shape[0]
    half = jax.ShapeDtypeStruct((own, width // HALVES), jnp.bfloat16)
    half_spec = pl.BlockSpec((own, width // HALVES), lambda expert, first_ref: (0, 0))
    return pl.pallas_call(
        project_own,
        out_shape=[half] * HALVES,
        grid_spec=pltpu.PrefetchScalarGridSpec(
            num_scalar_prefetch=1,
            grid=(experts,),
            in_specs=[
                pl.BlockSpec((1, own), lambda expert, first_ref: (0, 0)),
                pl.BlockSpec((own, width), lambda expert, first_ref: (0, 0)),
                pl.BlockSpec((1, width, width), lambda expert, first_ref: (expert, 0, 0)),
            ],
            out_specs=[half_spec] * HALVES,
            scratch_shapes=[pltpu.VMEM((own, width), jnp.float32)],
        ),
        compiler_params=pltpu.CompilerParams(dimension_semantics=("arbitrary",)),
        cost_estimate=pl.CostEstimate(
            flops=2 * own * width * width * experts,
            bytes_accessed=weights.size * 2 + own * width * 4,
            transcendentals=0,
        ),
        name="own_queries",
    )(first_expert.reshape(1), cats.reshape(1, own), feat, weights)


def spread(blocks, order_ref, *rest):
    source_refs, dense_ref, out_refs, next_ref, all_ref = rest[:4], rest[4], rest[5:-2], *rest[-2:]
    step = pl.program_id(0)

    @pl.when(step == 0)
    def _():
        for place in range(blocks):
            next_ref[place] = order_ref[place]
        own = all_ref.shape[0] // blocks
        for place in range(blocks):
            source = source_refs[4 * place // blocks]
            start = pl.multiple_of(order_ref[place] * own, own)
            all_ref[pl.ds(start, own)] = source[pl.ds((place % (blocks // 4)) * own, own)]

    product = jnp.dot(dense_ref[...], all_ref[...], preferred_element_type=jnp.float32)
    rows, first = product.shape[0], 0
    for out_ref in out_refs:
        chunks = out_ref.shape[0] // rows

        @pl.when((step >= first) & (step < first + chunks))
        def _():
            start = pl.multiple_of((step - first) * rows, rows)
            out_ref[pl.ds(start, rows)] = product.astype(out_ref.dtype)

        first += chunks


def spread_items(order, queries, dense, first, counts, rows):
    items = dense.shape[1]
    cols = queries[0].shape[1]
    blocks, chunks = order.shape[0], sum(counts)
    whole = lambda step, order_ref: (0, 0)
    return pl.pallas_call(
        functools.partial(spread, blocks),
        out_shape=[jax.ShapeDtypeStruct((count * rows, cols), jnp.bfloat16) for count in counts]
        + [jax.ShapeDtypeStruct((blocks,), jnp.int32)],
        grid_spec=pltpu.PrefetchScalarGridSpec(
            num_scalar_prefetch=1,
            grid=(chunks,),
            in_specs=[pl.BlockSpec(queries[0].shape, whole)] * 4
            + [pl.BlockSpec((rows, items), lambda step, order_ref: (first + step, 0))],
            out_specs=[pl.BlockSpec((count * rows, cols), whole) for count in counts]
            + [pl.BlockSpec(memory_space=pltpu.SMEM)],
            scratch_shapes=[pltpu.VMEM((items, cols), jnp.bfloat16)],
        ),
        compiler_params=pltpu.CompilerParams(
            dimension_semantics=("arbitrary",), vmem_limit_bytes=14 * MIB
        ),
        cost_estimate=pl.CostEstimate(
            flops=2 * chunks * rows * items * cols,
            bytes_accessed=chunks * rows * (items + cols) * 2 + items * cols * 2,
            transcendentals=0,
        ),
        name="spread_items",
    )(order, *queries, dense)


def norm_backward(pieces, user_ref, grad_ref, gain_ref, *rest):
    piece_refs, out_ref, term_ref = rest[: pieces * HALVES], rest[-2], rest[-1]
    summed = []
    for half in range(HALVES):
        total = piece_refs[half * pieces][...].astype(jnp.float32)
        for piece in range(1, pieces):
            total = total + piece_refs[half * pieces + piece][...].astype(jnp.float32)
        summed.append(total)
    width = out_ref.shape[1]
    pre_norm = user_ref[...].astype(jnp.float32) + jnp.concatenate(summed, axis=1)
    grad = grad_ref[...].astype(jnp.float32)
    scaled_grad = gain_ref[...] * grad
    inv_rms = lax.rsqrt(jnp.sum(pre_norm * pre_norm, axis=1, keepdims=True) / width + 1e-05)
    cross_mean = jnp.sum(scaled_grad * pre_norm, axis=1, keepdims=True) / width
    out_ref[...] = (
        inv_rms * scaled_grad - pre_norm * (inv_rms * inv_rms * inv_rms * cross_mean)
    ).astype(out_ref.dtype)
    term = jnp.sum(grad * pre_norm * inv_rms, axis=0, keepdims=True)

    @pl.when(pl.program_id(0) == 0)
    def _():
        term_ref[...] = term

    @pl.when(pl.program_id(0) > 0)
    def _():
        term_ref[...] += term


def user_gradient(user_feat, cotangent, gain, pieces, first, rows):
    width = user_feat.shape[1]
    block_rows = min(BLOCK_ROWS, rows)
    first_block = first // block_rows
    flat = [piece for half in pieces for piece in half]
    whole = pl.BlockSpec((block_rows, width), lambda step: (first_block + step, 0))
    part = pl.BlockSpec((block_rows, width // HALVES), lambda step: (step, 0))
    return pl.pallas_call(
        functools.partial(norm_backward, len(pieces[0])),
        out_shape=[
            jax.ShapeDtypeStruct((rows, width), jnp.bfloat16),
            jax.ShapeDtypeStruct((1, width), jnp.float32),
        ],
        grid=(rows // block_rows,),
        in_specs=[whole, whole, pl.BlockSpec((1, width), lambda step: (0, 0))] + [part] * len(flat),
        out_specs=[
            pl.BlockSpec((block_rows, width), lambda step: (step, 0)),
            pl.BlockSpec((1, width), lambda step: (0, 0)),
        ],
        compiler_params=pltpu.CompilerParams(
            dimension_semantics=("arbitrary",), vmem_limit_bytes=10 * MIB
        ),
        cost_estimate=pl.CostEstimate(
            flops=16 * rows * width,
            bytes_accessed=rows * width * 2 * (3 + len(pieces[0])),
            transcendentals=rows,
        ),
        name="user_gradient",
    )(user_feat, cotangent, gain.reshape(1, width), *flat)


def flip(value, size, bits):
    return lax.ppermute(value, "user", [(source, source ^ bits) for source in range(size)])


def gather_layers(own, size):
    return jnp.concatenate(
        [own] + [flip(own, size, 4 * layer) for layer in range(1, size // 4)], axis=0
    )


def gather_sides(own, size):
    other = flip(own, size, 2)
    return own, other, flip(own, size, 1), flip(other, size, 1)


def gather_order(size):
    layers = size // 4
    place = jnp.arange(size, dtype=jnp.int32)
    core, side, layer = place // (size // 2), (place // layers) % 2, place % layers
    return lax.axis_index("user") ^ (layer * 4 + side * 2 + core)


def scatter_sum(terms, size, order, beside=None):
    bits = size.bit_length() - 1
    index = lax.axis_index("user")
    left = list(reversed(range(bits)))
    terms = terms.reshape((2,) * bits + terms.shape[1:])
    for bit in order:
        axis = left.index(bit)
        left.remove(bit)
        mine = (index >> bit) & 1
        own = lax.dynamic_index_in_dim(terms, mine, axis, keepdims=False)
        away = lax.dynamic_index_in_dim(terms, 1 - mine, axis, keepdims=False)
        terms = own + flip(away.astype(jnp.bfloat16), size, 1 << bit).astype(jnp.float32)
        if beside is not None and len(left) == 2:
            terms, beside = lax.optimization_barrier((terms, beside))
    return terms, beside


def scatter_sums(halves, size, beside=None):
    bits = size.bit_length() - 1
    orders = [list(range(bits)), [0, 2, 1] + list(range(3, bits))]
    first, _ = scatter_sum(halves[0], size, orders[0])
    second, beside = scatter_sum(halves[1], size, orders[1], beside)
    return [first, second], beside


def on_device(
    user_feat, cotangent, gain, item_feat, categories, expert_w, tile_place, tile_level, tile_count
):
    users, width = user_feat.shape
    user_size, item_size = lax.axis_size("user"), lax.axis_size("item")
    item_index = lax.axis_index("item")
    own_items = item_feat.shape[1]
    items = own_items * user_size
    experts_here = expert_w.shape[0]
    first_expert = item_index * experts_here
    own_cats, own_feat = categories[0], item_feat[0]
    rows, half_width = users // ROW_CHUNKS, width // HALVES

    own_halves = own_queries(first_expert, own_cats, own_feat, expert_w)
    order = gather_order(user_size)
    dense = dense_tiles(tile_place[0, 0], tile_count[0], tile_level[0, 0], users, items)
    layers = [gather_layers(own, user_size) for own in own_halves]
    queries = [gather_sides(part, user_size) for part in layers]

    partials = [[] for _ in range(HALVES)]
    for half in range(HALVES):
        for first, count in ((0, 1), (1, ROW_CHUNKS - 1)):
            *products, _ = spread_items(order, queries[half], dense, first, (1,) * count, rows)
            for product in products:
                pieces = [product]
                for shift in range(1, item_size):
                    pairs = [(source, (source + shift) % item_size) for source in range(item_size)]
                    pieces.append(lax.ppermute(product, "item", pairs))
                partials[half].append(pieces)
    grads, gain_term, item_terms = [None] * ROW_CHUNKS, 0.0, 0.0
    chunk_order = [0] + list(range(ROW_CHUNKS - 1, 0, -1))
    for chunk in chunk_order:
        grad, term = user_gradient(
            user_feat,
            cotangent,
            gain,
            [partials[half][chunk] for half in range(HALVES)],
            chunk * rows,
            rows,
        )
        grads[chunk] = grad
        gain_term = gain_term + term[0]
        if chunk != chunk_order[-1]:
            item_terms = item_terms + lax.dot_general(
                dense[chunk * rows : (chunk + 1) * rows],
                grad,
                (((0,), (0,)), ((), ())),
                preferred_element_type=jnp.float32,
            )
    col_width = width // item_size
    user_grad = jnp.concatenate(
        [lax.dynamic_slice_in_dim(grad, item_index * col_width, col_width, 1) for grad in grads],
        axis=0,
    )
    gain_own = lax.dynamic_slice_in_dim(gain_term, item_index * col_width, col_width, 0)

    halves = []
    for half in range(HALVES):
        part = slice(half * half_width, (half + 1) * half_width)
        terms = item_terms[:, part] + lax.dot_general(
            dense[chunk_order[-1] * rows : (chunk_order[-1] + 1) * rows],
            grads[chunk_order[-1]][:, part],
            (((0,), (0,)), ((), ())),
            preferred_element_type=jnp.float32,
        )
        halves.append(terms.reshape(user_size, own_items, half_width))
    sums = [half.astype(jnp.bfloat16) for half in scatter_sums(halves, user_size)[0]]
    own_sums = jnp.concatenate(sums, axis=1)

    chosen = own_cats[:, None] == first_expert + jnp.arange(experts_here, dtype=jnp.int32)[None, :]
    own_width = width // user_size
    left = jnp.where(
        chosen[:, None, :, None],
        own_feat.reshape(own_items, user_size, 1, own_width),
        jnp.zeros((), own_feat.dtype),
    ).reshape(own_items, -1)
    halves = [
        lax.dot_general(
            left, half, (((0,), (0,)), ((), ())), preferred_element_type=jnp.float32
        ).reshape(user_size, experts_here * own_width, half_width)
        for half in sums
    ]
    gain_rows = jnp.pad(gain_own, (0, 8 * half_width - col_width)).reshape(1, 8, half_width)
    gain_rows = jnp.broadcast_to(gain_rows, (user_size, 8, half_width))
    halves[0] = jnp.concatenate([halves[0], gain_rows], axis=1)
    halves, own_sums = scatter_sums(halves, user_size, own_sums)
    gain_grad = halves[0][-8:].reshape(-1)[:col_width]
    expert_grad = jnp.concatenate([halves[0][:-8], halves[1]], axis=1)
    item_total = jnp.zeros((own_items, width), jnp.float32)
    for expert in range(experts_here):
        item_total = item_total + jnp.where(
            chosen[:, expert][:, None],
            lax.dot_general(
                own_sums,
                expert_w[expert],
                (((1,), (1,)), ((), ())),
                preferred_element_type=jnp.float32,
            ),
            0.0,
        )
    return (
        user_grad,
        item_total.astype(jnp.bfloat16)[None],
        expert_grad.reshape(experts_here, own_width, width),
        gain_grad,
    )


def solution(mesh):
    placed = (
        P("user", None),
        P("user", None),
        P(),
        P("item", "user", None),
        P("item", "user"),
        P("item", None, None),
        P("user", "item", None),
        P("user", "item", None, None, None),
        P("user", "item"),
    )
    return jax.shard_map(
        on_device,
        mesh=mesh,
        in_specs=placed,
        out_specs=(P("user", "item"), P("item", "user", None), P("item", "user", None), P("item")),
        check_vma=False,
    )
```

```python
import functools

import jax
import jax.numpy as jnp
from jax import lax
from jax.experimental import pallas as pl
from jax.experimental.pallas import tpu as pltpu
from jax.sharding import PartitionSpec as P

TILE = 128
SLOTS_PER_STEP = 8
HALVES = 2
ROW_CHUNKS = 4
BLOCK_ROWS = 256
MIB = 1024 * 1024


def place_tiles(item_blocks, place_ref, count_ref, level_ref, dense_ref):
    step = pl.program_id(0)

    @pl.when(step == 0)
    def _():
        dense_ref[...] = jnp.zeros_like(dense_ref)

    for offset in range(level_ref.shape[0]):
        slot = step * level_ref.shape[0] + offset

        @pl.when(slot < count_ref[0])
        def _():
            place = place_ref[slot]
            row = pl.multiple_of((place // item_blocks) * TILE, TILE)
            col = pl.multiple_of((place % item_blocks) * TILE, TILE)
            weights = level_ref[offset].astype(jnp.float32) * (1.0 / (2.0 * TILE))
            dense_ref[pl.ds(row, TILE), pl.ds(col, TILE)] = weights.astype(jnp.bfloat16)


def dense_tiles(place, count, level, users, items):
    slots = level.shape[0]
    per_step = SLOTS_PER_STEP if slots % SLOTS_PER_STEP == 0 else 1
    return pl.pallas_call(
        functools.partial(place_tiles, items // TILE),
        out_shape=jax.ShapeDtypeStruct((users, items), jnp.bfloat16),
        grid_spec=pltpu.PrefetchScalarGridSpec(
            num_scalar_prefetch=2,
            grid=(slots // per_step,),
            in_specs=[
                pl.BlockSpec((per_step, TILE, TILE), lambda step, place_ref, count_ref: (step, 0, 0))
            ],
            out_specs=pl.BlockSpec((users, items), lambda step, place_ref, count_ref: (0, 0)),
        ),
        compiler_params=pltpu.CompilerParams(
            dimension_semantics=("arbitrary",), vmem_limit_bytes=16 * MIB
        ),
        cost_estimate=pl.CostEstimate(
            flops=slots * TILE * TILE,
            bytes_accessed=slots * TILE * TILE * 4 + users * items * 2,
            transcendentals=0,
        ),
        name="place_tiles",
    )(place, count, level)


def project_own(first_ref, cats_ref, feat_ref, weight_ref, *rest):
    out_refs, total_ref = rest[:-1], rest[-1]
    expert = pl.program_id(0)
    own = feat_ref.shape[0]
    on_diagonal = lax.broadcasted_iota(jnp.int32, (own, own), 0) == lax.broadcasted_iota(
        jnp.int32, (own, own), 1
    )
    cats = jnp.sum(
        jnp.where(on_diagonal, cats_ref[...].astype(jnp.float32), 0.0), axis=1, keepdims=True
    )
    chosen = cats == (first_ref[0] + expert).astype(jnp.float32)
    part = jnp.dot(feat_ref[...], weight_ref[0], preferred_element_type=jnp.float32)
    part = jnp.where(chosen, part, 0.0)

    @pl.when(expert == 0)
    def _():
        total_ref[...] = part

    @pl.when(expert > 0)
    def _():
        total_ref[...] += part

    @pl.when(expert == pl.num_programs(0) - 1)
    def _():
        cols = out_refs[0].shape[1]
        for half, out_ref in enumerate(out_refs):
            out_ref[...] = total_ref[:, half * cols : (half + 1) * cols].astype(out_ref.dtype)


def own_queries(first_expert, cats, feat, weights):
    own, width = feat.shape
    experts = weights.shape[0]
    half = jax.ShapeDtypeStruct((own, width // HALVES), jnp.bfloat16)
    half_spec = pl.BlockSpec((own, width // HALVES), lambda expert, first_ref: (0, 0))
    return pl.pallas_call(
        project_own,
        out_shape=[half] * HALVES,
        grid_spec=pltpu.PrefetchScalarGridSpec(
            num_scalar_prefetch=1,
            grid=(experts,),
            in_specs=[
                pl.BlockSpec((1, own), lambda expert, first_ref: (0, 0)),
                pl.BlockSpec((own, width), lambda expert, first_ref: (0, 0)),
                pl.BlockSpec((1, width, width), lambda expert, first_ref: (expert, 0, 0)),
            ],
            out_specs=[half_spec] * HALVES,
            scratch_shapes=[pltpu.VMEM((own, width), jnp.float32)],
        ),
        compiler_params=pltpu.CompilerParams(dimension_semantics=("arbitrary",)),
        cost_estimate=pl.CostEstimate(
            flops=2 * own * width * width * experts,
            bytes_accessed=weights.size * 2 + own * width * 4,
            transcendentals=0,
        ),
        name="own_queries",
    )(first_expert.reshape(1), cats.reshape(1, own), feat, weights)


def spread(blocks, order_ref, *rest):
    source_refs, dense_ref, out_refs, next_ref, all_ref = rest[:4], rest[4], rest[5:-2], *rest[-2:]
    step = pl.program_id(0)

    @pl.when(step == 0)
    def _():
        for place in range(blocks):
            next_ref[place] = order_ref[place]
        own = all_ref.shape[0] // blocks
        for place in range(blocks):
            source = source_refs[4 * place // blocks]
            start = pl.multiple_of(order_ref[place] * own, own)
            all_ref[pl.ds(start, own)] = source[pl.ds((place % (blocks // 4)) * own, own)]

    product = jnp.dot(dense_ref[...], all_ref[...], preferred_element_type=jnp.float32)
    rows, first = product.shape[0], 0
    for out_ref in out_refs:
        chunks = out_ref.shape[0] // rows

        @pl.when((step >= first) & (step < first + chunks))
        def _():
            start = pl.multiple_of((step - first) * rows, rows)
            out_ref[pl.ds(start, rows)] = product.astype(out_ref.dtype)

        first += chunks


def spread_items(order, queries, dense, first, counts, rows):
    items = dense.shape[1]
    cols = queries[0].shape[1]
    blocks, chunks = order.shape[0], sum(counts)
    whole = lambda step, order_ref: (0, 0)
    return pl.pallas_call(
        functools.partial(spread, blocks),
        out_shape=[jax.ShapeDtypeStruct((count * rows, cols), jnp.bfloat16) for count in counts]
        + [jax.ShapeDtypeStruct((blocks,), jnp.int32)],
        grid_spec=pltpu.PrefetchScalarGridSpec(
            num_scalar_prefetch=1,
            grid=(chunks,),
            in_specs=[pl.BlockSpec(queries[0].shape, whole)] * 4
            + [pl.BlockSpec((rows, items), lambda step, order_ref: (first + step, 0))],
            out_specs=[pl.BlockSpec((count * rows, cols), whole) for count in counts]
            + [pl.BlockSpec(memory_space=pltpu.SMEM)],
            scratch_shapes=[pltpu.VMEM((items, cols), jnp.bfloat16)],
        ),
        compiler_params=pltpu.CompilerParams(
            dimension_semantics=("arbitrary",), vmem_limit_bytes=14 * MIB
        ),
        cost_estimate=pl.CostEstimate(
            flops=2 * chunks * rows * items * cols,
            bytes_accessed=chunks * rows * (items + cols) * 2 + items * cols * 2,
            transcendentals=0,
        ),
        name="spread_items",
    )(order, *queries, dense)


def norm_backward(pieces, user_ref, grad_ref, gain_ref, *rest):
    piece_refs, out_ref, term_ref = rest[: pieces * HALVES], rest[-2], rest[-1]
    summed = []
    for half in range(HALVES):
        total = piece_refs[half * pieces][...].astype(jnp.float32)
        for piece in range(1, pieces):
            total = total + piece_refs[half * pieces + piece][...].astype(jnp.float32)
        summed.append(total)
    width = out_ref.shape[1]
    pre_norm = user_ref[...].astype(jnp.float32) + jnp.concatenate(summed, axis=1)
    grad = grad_ref[...].astype(jnp.float32)
    scaled_grad = gain_ref[...] * grad
    inv_rms = lax.rsqrt(jnp.sum(pre_norm * pre_norm, axis=1, keepdims=True) / width + 1e-05)
    cross_mean = jnp.sum(scaled_grad * pre_norm, axis=1, keepdims=True) / width
    out_ref[...] = (
        inv_rms * scaled_grad - pre_norm * (inv_rms * inv_rms * inv_rms * cross_mean)
    ).astype(out_ref.dtype)
    term = jnp.sum(grad * pre_norm * inv_rms, axis=0, keepdims=True)

    @pl.when(pl.program_id(0) == 0)
    def _():
        term_ref[...] = term

    @pl.when(pl.program_id(0) > 0)
    def _():
        term_ref[...] += term


def user_gradient(user_feat, cotangent, gain, pieces, first, rows):
    width = user_feat.shape[1]
    block_rows = min(BLOCK_ROWS, rows)
    first_block = first // block_rows
    flat = [piece for half in pieces for piece in half]
    whole = pl.BlockSpec((block_rows, width), lambda step: (first_block + step, 0))
    part = pl.BlockSpec((block_rows, width // HALVES), lambda step: (step, 0))
    return pl.pallas_call(
        functools.partial(norm_backward, len(pieces[0])),
        out_shape=[
            jax.ShapeDtypeStruct((rows, width), jnp.bfloat16),
            jax.ShapeDtypeStruct((1, width), jnp.float32),
        ],
        grid=(rows // block_rows,),
        in_specs=[whole, whole, pl.BlockSpec((1, width), lambda step: (0, 0))] + [part] * len(flat),
        out_specs=[
            pl.BlockSpec((block_rows, width), lambda step: (step, 0)),
            pl.BlockSpec((1, width), lambda step: (0, 0)),
        ],
        compiler_params=pltpu.CompilerParams(
            dimension_semantics=("arbitrary",), vmem_limit_bytes=10 * MIB
        ),
        cost_estimate=pl.CostEstimate(
            flops=16 * rows * width,
            bytes_accessed=rows * width * 2 * (3 + len(pieces[0])),
            transcendentals=rows,
        ),
        name="user_gradient",
    )(user_feat, cotangent, gain.reshape(1, width), *flat)


def flip(value, size, bits):
    return lax.ppermute(value, "user", [(source, source ^ bits) for source in range(size)])


def gather_layers(own, size):
    return jnp.concatenate(
        [own] + [flip(own, size, 4 * layer) for layer in range(1, size // 4)], axis=0
    )


def gather_sides(own, size):
    other = flip(own, size, 2)
    return own, other, flip(own, size, 1), flip(other, size, 1)


def gather_order(size):
    layers = size // 4
    place = jnp.arange(size, dtype=jnp.int32)
    core, side, layer = place // (size // 2), (place // layers) % 2, place % layers
    return lax.axis_index("user") ^ (layer * 4 + side * 2 + core)


def scatter_sum(terms, size, order, beside=None):
    bits = size.bit_length() - 1
    index = lax.axis_index("user")
    left = list(reversed(range(bits)))
    terms = terms.reshape((2,) * bits + terms.shape[1:])
    for bit in order:
        axis = left.index(bit)
        left.remove(bit)
        mine = (index >> bit) & 1
        own = lax.dynamic_index_in_dim(terms, mine, axis, keepdims=False)
        away = lax.dynamic_index_in_dim(terms, 1 - mine, axis, keepdims=False)
        terms = own + flip(away.astype(jnp.bfloat16), size, 1 << bit).astype(jnp.float32)
        if beside is not None and len(left) == 2:
            terms, beside = lax.optimization_barrier((terms, beside))
    return terms, beside


def scatter_sums(halves, size, beside=None):
    bits = size.bit_length() - 1
    orders = [list(range(bits)), [0, 2, 1] + list(range(3, bits))]
    first, _ = scatter_sum(halves[0], size, orders[0])
    second, beside = scatter_sum(halves[1], size, orders[1], beside)
    return [first, second], beside


def on_device(
    user_feat, cotangent, gain, item_feat, categories, expert_w, tile_place, tile_level, tile_count
):
    users, width = user_feat.shape
    user_size, item_size = lax.axis_size("user"), lax.axis_size("item")
    item_index = lax.axis_index("item")
    own_items = item_feat.shape[1]
    items = own_items * user_size
    experts_here = expert_w.shape[0]
    first_expert = item_index * experts_here
    own_cats, own_feat = categories[0], item_feat[0]
    rows, half_width = users // ROW_CHUNKS, width // HALVES

    own_halves = own_queries(first_expert, own_cats, own_feat, expert_w)
    order = gather_order(user_size)
    dense = dense_tiles(tile_place[0, 0], tile_count[0], tile_level[0, 0], users, items)
    layers = [gather_layers(own, user_size) for own in own_halves]
    queries = [gather_sides(part, user_size) for part in layers]

    partials = [[] for _ in range(HALVES)]
    for half in range(HALVES):
        for first, count in ((0, ROW_CHUNKS - 1), (ROW_CHUNKS - 1, 1)):
            *products, _ = spread_items(order, queries[half], dense, first, (1,) * count, rows)
            for product in products:
                pieces = [product]
                for shift in range(1, item_size):
                    pairs = [(source, (source + shift) % item_size) for source in range(item_size)]
                    pieces.append(lax.ppermute(product, "item", pairs))
                partials[half].append(pieces)
    grads, gain_term, item_terms = [None] * ROW_CHUNKS, 0.0, 0.0
    chunk_order = [0] + list(range(ROW_CHUNKS - 1, 0, -1))
    for chunk in chunk_order:
        grad, term = user_gradient(
            user_feat,
            cotangent,
            gain,
            [partials[half][chunk] for half in range(HALVES)],
            chunk * rows,
            rows,
        )
        grads[chunk] = grad
        gain_term = gain_term + term[0]
        if chunk != chunk_order[-1]:
            item_terms = item_terms + lax.dot_general(
                dense[chunk * rows : (chunk + 1) * rows],
                grad,
                (((0,), (0,)), ((), ())),
                preferred_element_type=jnp.float32,
            )
    col_width = width // item_size
    user_grad = jnp.concatenate(
        [lax.dynamic_slice_in_dim(grad, item_index * col_width, col_width, 1) for grad in grads],
        axis=0,
    )
    gain_own = lax.dynamic_slice_in_dim(gain_term, item_index * col_width, col_width, 0)

    halves = []
    for half in range(HALVES):
        part = slice(half * half_width, (half + 1) * half_width)
        terms = item_terms[:, part] + lax.dot_general(
            dense[chunk_order[-1] * rows : (chunk_order[-1] + 1) * rows],
            grads[chunk_order[-1]][:, part],
            (((0,), (0,)), ((), ())),
            preferred_element_type=jnp.float32,
        )
        halves.append(terms.reshape(user_size, own_items, half_width))
    sums = [half.astype(jnp.bfloat16) for half in scatter_sums(halves, user_size)[0]]
    own_sums = jnp.concatenate(sums, axis=1)

    chosen = own_cats[:, None] == first_expert + jnp.arange(experts_here, dtype=jnp.int32)[None, :]
    own_width = width // user_size
    left = jnp.where(
        chosen[:, None, :, None],
        own_feat.reshape(own_items, user_size, 1, own_width),
        jnp.zeros((), own_feat.dtype),
    ).reshape(own_items, -1)
    halves = [
        lax.dot_general(
            left, half, (((0,), (0,)), ((), ())), preferred_element_type=jnp.float32
        ).reshape(user_size, experts_here * own_width, half_width)
        for half in sums
    ]
    gain_rows = jnp.pad(gain_own, (0, 8 * half_width - col_width)).reshape(1, 8, half_width)
    gain_rows = jnp.broadcast_to(gain_rows, (user_size, 8, half_width))
    halves[0] = jnp.concatenate([halves[0], gain_rows], axis=1)
    halves, own_sums = scatter_sums(halves, user_size, own_sums)
    gain_grad = halves[0][-8:].reshape(-1)[:col_width]
    expert_grad = jnp.concatenate([halves[0][:-8], halves[1]], axis=1)
    item_total = jnp.zeros((own_items, width), jnp.float32)
    for expert in range(experts_here):
        item_total = item_total + jnp.where(
            chosen[:, expert][:, None],
            lax.dot_general(
                own_sums,
                expert_w[expert],
                (((1,), (1,)), ((), ())),
                preferred_element_type=jnp.float32,
            ),
            0.0,
        )
    return (
        user_grad,
        item_total.astype(jnp.bfloat16)[None],
        expert_grad.reshape(experts_here, own_width, width),
        gain_grad,
    )


def solution(mesh):
    placed = (
        P("user", None),
        P("user", None),
        P(),
        P("item", "user", None),
        P("item", "user"),
        P("item", None, None),
        P("user", "item", None),
        P("user", "item", None, None, None),
        P("user", "item"),
    )
    return jax.shard_map(
        on_device,
        mesh=mesh,
        in_specs=placed,
        out_specs=(P("user", "item"), P("item", "user", None), P("item", "user", None), P("item")),
        check_vma=False,
    )
```

```python
import functools

import jax
import jax.numpy as jnp
from jax import lax
from jax.experimental import pallas as pl
from jax.experimental.pallas import tpu as pltpu
from jax.sharding import PartitionSpec as P

TILE = 128
SLOTS_PER_STEP = 8
HALVES = 2
ROW_CHUNKS = 4
BLOCK_ROWS = 256
MIB = 1024 * 1024


def place_tiles(item_blocks, place_ref, count_ref, level_ref, dense_ref):
    step = pl.program_id(0)

    @pl.when(step == 0)
    def _():
        dense_ref[...] = jnp.zeros_like(dense_ref)

    for offset in range(level_ref.shape[0]):
        slot = step * level_ref.shape[0] + offset

        @pl.when(slot < count_ref[0])
        def _():
            place = place_ref[slot]
            row = pl.multiple_of((place // item_blocks) * TILE, TILE)
            col = pl.multiple_of((place % item_blocks) * TILE, TILE)
            weights = level_ref[offset].astype(jnp.float32) * (1.0 / (2.0 * TILE))
            dense_ref[pl.ds(row, TILE), pl.ds(col, TILE)] = weights.astype(jnp.bfloat16)


def dense_tiles(place, count, level, users, items):
    slots = level.shape[0]
    per_step = SLOTS_PER_STEP if slots % SLOTS_PER_STEP == 0 else 1
    return pl.pallas_call(
        functools.partial(place_tiles, items // TILE),
        out_shape=jax.ShapeDtypeStruct((users, items), jnp.bfloat16),
        grid_spec=pltpu.PrefetchScalarGridSpec(
            num_scalar_prefetch=2,
            grid=(slots // per_step,),
            in_specs=[
                pl.BlockSpec((per_step, TILE, TILE), lambda step, place_ref, count_ref: (step, 0, 0))
            ],
            out_specs=pl.BlockSpec((users, items), lambda step, place_ref, count_ref: (0, 0)),
        ),
        compiler_params=pltpu.CompilerParams(
            dimension_semantics=("arbitrary",), vmem_limit_bytes=16 * MIB
        ),
        cost_estimate=pl.CostEstimate(
            flops=slots * TILE * TILE,
            bytes_accessed=slots * TILE * TILE * 4 + users * items * 2,
            transcendentals=0,
        ),
        name="place_tiles",
    )(place, count, level)


def project_own(first_ref, cats_ref, feat_ref, weight_ref, *rest):
    out_refs, total_ref = rest[:-1], rest[-1]
    expert = pl.program_id(0)
    own = feat_ref.shape[0]
    on_diagonal = lax.broadcasted_iota(jnp.int32, (own, own), 0) == lax.broadcasted_iota(
        jnp.int32, (own, own), 1
    )
    cats = jnp.sum(
        jnp.where(on_diagonal, cats_ref[...].astype(jnp.float32), 0.0), axis=1, keepdims=True
    )
    chosen = cats == (first_ref[0] + expert).astype(jnp.float32)
    part = jnp.dot(feat_ref[...], weight_ref[0], preferred_element_type=jnp.float32)
    part = jnp.where(chosen, part, 0.0)

    @pl.when(expert == 0)
    def _():
        total_ref[...] = part

    @pl.when(expert > 0)
    def _():
        total_ref[...] += part

    @pl.when(expert == pl.num_programs(0) - 1)
    def _():
        cols = out_refs[0].shape[1]
        for half, out_ref in enumerate(out_refs):
            out_ref[...] = total_ref[:, half * cols : (half + 1) * cols].astype(out_ref.dtype)


def own_queries(first_expert, cats, feat, weights):
    own, width = feat.shape
    experts = weights.shape[0]
    half = jax.ShapeDtypeStruct((own, width // HALVES), jnp.bfloat16)
    half_spec = pl.BlockSpec((own, width // HALVES), lambda expert, first_ref: (0, 0))
    return pl.pallas_call(
        project_own,
        out_shape=[half] * HALVES,
        grid_spec=pltpu.PrefetchScalarGridSpec(
            num_scalar_prefetch=1,
            grid=(experts,),
            in_specs=[
                pl.BlockSpec((1, own), lambda expert, first_ref: (0, 0)),
                pl.BlockSpec((own, width), lambda expert, first_ref: (0, 0)),
                pl.BlockSpec((1, width, width), lambda expert, first_ref: (expert, 0, 0)),
            ],
            out_specs=[half_spec] * HALVES,
            scratch_shapes=[pltpu.VMEM((own, width), jnp.float32)],
        ),
        compiler_params=pltpu.CompilerParams(dimension_semantics=("arbitrary",)),
        cost_estimate=pl.CostEstimate(
            flops=2 * own * width * width * experts,
            bytes_accessed=weights.size * 2 + own * width * 4,
            transcendentals=0,
        ),
        name="own_queries",
    )(first_expert.reshape(1), cats.reshape(1, own), feat, weights)


def spread(blocks, order_ref, *rest):
    source_refs, dense_ref, out_refs, next_ref, all_ref = rest[:4], rest[4], rest[5:-2], *rest[-2:]
    step = pl.program_id(0)

    @pl.when(step == 0)
    def _():
        for place in range(blocks):
            next_ref[place] = order_ref[place]
        own = all_ref.shape[0] // blocks
        for place in range(blocks):
            source = source_refs[4 * place // blocks]
            start = pl.multiple_of(order_ref[place] * own, own)
            all_ref[pl.ds(start, own)] = source[pl.ds((place % (blocks // 4)) * own, own)]

    product = jnp.dot(dense_ref[...], all_ref[...], preferred_element_type=jnp.float32)
    rows, first = product.shape[0], 0
    for out_ref in out_refs:
        chunks = out_ref.shape[0] // rows

        @pl.when((step >= first) & (step < first + chunks))
        def _():
            start = pl.multiple_of((step - first) * rows, rows)
            out_ref[pl.ds(start, rows)] = product.astype(out_ref.dtype)

        first += chunks


def spread_items(order, queries, dense, first, counts, rows):
    items = dense.shape[1]
    cols = queries[0].shape[1]
    blocks, chunks = order.shape[0], sum(counts)
    whole = lambda step, order_ref: (0, 0)
    return pl.pallas_call(
        functools.partial(spread, blocks),
        out_shape=[jax.ShapeDtypeStruct((count * rows, cols), jnp.bfloat16) for count in counts]
        + [jax.ShapeDtypeStruct((blocks,), jnp.int32)],
        grid_spec=pltpu.PrefetchScalarGridSpec(
            num_scalar_prefetch=1,
            grid=(chunks,),
            in_specs=[pl.BlockSpec(queries[0].shape, whole)] * 4
            + [pl.BlockSpec((rows, items), lambda step, order_ref: (first + step, 0))],
            out_specs=[pl.BlockSpec((count * rows, cols), whole) for count in counts]
            + [pl.BlockSpec(memory_space=pltpu.SMEM)],
            scratch_shapes=[pltpu.VMEM((items, cols), jnp.bfloat16)],
        ),
        compiler_params=pltpu.CompilerParams(
            dimension_semantics=("arbitrary",), vmem_limit_bytes=14 * MIB
        ),
        cost_estimate=pl.CostEstimate(
            flops=2 * chunks * rows * items * cols,
            bytes_accessed=chunks * rows * (items + cols) * 2 + items * cols * 2,
            transcendentals=0,
        ),
        name="spread_items",
    )(order, *queries, dense)


def norm_backward(pieces, user_ref, grad_ref, gain_ref, *rest):
    piece_refs, out_ref, term_ref = rest[: pieces * HALVES], rest[-2], rest[-1]
    summed = []
    for half in range(HALVES):
        total = piece_refs[half * pieces][...].astype(jnp.float32)
        for piece in range(1, pieces):
            total = total + piece_refs[half * pieces + piece][...].astype(jnp.float32)
        summed.append(total)
    width = out_ref.shape[1]
    pre_norm = user_ref[...].astype(jnp.float32) + jnp.concatenate(summed, axis=1)
    grad = grad_ref[...].astype(jnp.float32)
    scaled_grad = gain_ref[...] * grad
    inv_rms = lax.rsqrt(jnp.sum(pre_norm * pre_norm, axis=1, keepdims=True) / width + 1e-05)
    cross_mean = jnp.sum(scaled_grad * pre_norm, axis=1, keepdims=True) / width
    out_ref[...] = (
        inv_rms * scaled_grad - pre_norm * (inv_rms * inv_rms * inv_rms * cross_mean)
    ).astype(out_ref.dtype)
    term = jnp.sum(grad * pre_norm * inv_rms, axis=0, keepdims=True)

    @pl.when(pl.program_id(0) == 0)
    def _():
        term_ref[...] = term

    @pl.when(pl.program_id(0) > 0)
    def _():
        term_ref[...] += term


def user_gradient(user_feat, cotangent, gain, pieces, first, rows):
    width = user_feat.shape[1]
    block_rows = min(BLOCK_ROWS, rows)
    first_block = first // block_rows
    flat = [piece for half in pieces for piece in half]
    whole = pl.BlockSpec((block_rows, width), lambda step: (first_block + step, 0))
    part = pl.BlockSpec((block_rows, width // HALVES), lambda step: (step, 0))
    return pl.pallas_call(
        functools.partial(norm_backward, len(pieces[0])),
        out_shape=[
            jax.ShapeDtypeStruct((rows, width), jnp.bfloat16),
            jax.ShapeDtypeStruct((1, width), jnp.float32),
        ],
        grid=(rows // block_rows,),
        in_specs=[whole, whole, pl.BlockSpec((1, width), lambda step: (0, 0))] + [part] * len(flat),
        out_specs=[
            pl.BlockSpec((block_rows, width), lambda step: (step, 0)),
            pl.BlockSpec((1, width), lambda step: (0, 0)),
        ],
        compiler_params=pltpu.CompilerParams(
            dimension_semantics=("arbitrary",), vmem_limit_bytes=10 * MIB
        ),
        cost_estimate=pl.CostEstimate(
            flops=16 * rows * width,
            bytes_accessed=rows * width * 2 * (3 + len(pieces[0])),
            transcendentals=rows,
        ),
        name="user_gradient",
    )(user_feat, cotangent, gain.reshape(1, width), *flat)


def flip(value, size, bits):
    return lax.ppermute(value, "user", [(source, source ^ bits) for source in range(size)])


def gather_layers(own, size):
    return jnp.concatenate(
        [own] + [flip(own, size, 4 * layer) for layer in range(1, size // 4)], axis=0
    )


def gather_sides(own, size):
    other = flip(own, size, 2)
    return own, other, flip(own, size, 1), flip(other, size, 1)


def gather_order(size):
    layers = size // 4
    place = jnp.arange(size, dtype=jnp.int32)
    core, side, layer = place // (size // 2), (place // layers) % 2, place % layers
    return lax.axis_index("user") ^ (layer * 4 + side * 2 + core)


def scatter_sum(terms, size, order, beside=None):
    bits = size.bit_length() - 1
    index = lax.axis_index("user")
    left = list(reversed(range(bits)))
    if 0 in order:
        terms = terms.reshape((2,) * bits + terms.shape[1:])
    else:
        left.remove(0)
    for bit in order:
        axis = left.index(bit)
        left.remove(bit)
        mine = (index >> bit) & 1
        own = lax.dynamic_index_in_dim(terms, mine, axis, keepdims=False)
        away = lax.dynamic_index_in_dim(terms, 1 - mine, axis, keepdims=False)
        terms = own + flip(away.astype(jnp.bfloat16), size, 1 << bit).astype(jnp.float32)
        if beside is not None and len(left) == 2:
            terms, beside = lax.optimization_barrier((terms, beside))
    return terms, beside


def scatter_sums(halves, size, beside=None):
    bits = size.bit_length() - 1
    orders = [list(range(bits)), [0, 2, 1] + list(range(3, bits))]
    if beside is None:
        halves = [scatter_sum(terms, size, [0])[0] for terms in halves]
        halves = lax.optimization_barrier(tuple(halves))
        orders = [order[1:] for order in orders]
    first, _ = scatter_sum(halves[0], size, orders[0])
    second, beside = scatter_sum(halves[1], size, orders[1], beside)
    return [first, second], beside


def on_device(
    user_feat, cotangent, gain, item_feat, categories, expert_w, tile_place, tile_level, tile_count
):
    users, width = user_feat.shape
    user_size, item_size = lax.axis_size("user"), lax.axis_size("item")
    item_index = lax.axis_index("item")
    own_items = item_feat.shape[1]
    items = own_items * user_size
    experts_here = expert_w.shape[0]
    first_expert = item_index * experts_here
    own_cats, own_feat = categories[0], item_feat[0]
    rows, half_width = users // ROW_CHUNKS, width // HALVES

    own_halves = own_queries(first_expert, own_cats, own_feat, expert_w)
    order = gather_order(user_size)
    dense = dense_tiles(tile_place[0, 0], tile_count[0], tile_level[0, 0], users, items)
    layers = [gather_layers(own, user_size) for own in own_halves]
    queries = [gather_sides(part, user_size) for part in layers]

    partials = [[] for _ in range(HALVES)]
    for half in range(HALVES):
        for first, count in ((0, ROW_CHUNKS - 1), (ROW_CHUNKS - 1, 1)):
            *products, _ = spread_items(order, queries[half], dense, first, (1,) * count, rows)
            for product in products:
                pieces = [product]
                for shift in range(1, item_size):
                    pairs = [(source, (source + shift) % item_size) for source in range(item_size)]
                    pieces.append(lax.ppermute(product, "item", pairs))
                partials[half].append(pieces)
    grads, gain_term, item_terms = [None] * ROW_CHUNKS, 0.0, 0.0
    chunk_order = [0] + list(range(ROW_CHUNKS - 1, 0, -1))
    for chunk in chunk_order:
        grad, term = user_gradient(
            user_feat,
            cotangent,
            gain,
            [partials[half][chunk] for half in range(HALVES)],
            chunk * rows,
            rows,
        )
        grads[chunk] = grad
        gain_term = gain_term + term[0]
        if chunk != chunk_order[-1]:
            item_terms = item_terms + lax.dot_general(
                dense[chunk * rows : (chunk + 1) * rows],
                grad,
                (((0,), (0,)), ((), ())),
                preferred_element_type=jnp.float32,
            )
    col_width = width // item_size
    user_grad = jnp.concatenate(
        [lax.dynamic_slice_in_dim(grad, item_index * col_width, col_width, 1) for grad in grads],
        axis=0,
    )
    gain_own = lax.dynamic_slice_in_dim(gain_term, item_index * col_width, col_width, 0)

    halves = []
    for half in range(HALVES):
        part = slice(half * half_width, (half + 1) * half_width)
        terms = item_terms[:, part] + lax.dot_general(
            dense[chunk_order[-1] * rows : (chunk_order[-1] + 1) * rows],
            grads[chunk_order[-1]][:, part],
            (((0,), (0,)), ((), ())),
            preferred_element_type=jnp.float32,
        )
        halves.append(terms.reshape(user_size, own_items, half_width))
    sums = [half.astype(jnp.bfloat16) for half in scatter_sums(halves, user_size)[0]]
    own_sums = jnp.concatenate(sums, axis=1)

    chosen = own_cats[:, None] == first_expert + jnp.arange(experts_here, dtype=jnp.int32)[None, :]
    own_width = width // user_size
    left = jnp.where(
        chosen[:, None, :, None],
        own_feat.reshape(own_items, user_size, 1, own_width),
        jnp.zeros((), own_feat.dtype),
    ).reshape(own_items, -1)
    halves = [
        lax.dot_general(
            left, half, (((0,), (0,)), ((), ())), preferred_element_type=jnp.float32
        ).reshape(user_size, experts_here * own_width, half_width)
        for half in sums
    ]
    gain_rows = jnp.pad(gain_own, (0, 8 * half_width - col_width)).reshape(1, 8, half_width)
    gain_rows = jnp.broadcast_to(gain_rows, (user_size, 8, half_width))
    halves[0] = jnp.concatenate([halves[0], gain_rows], axis=1)
    halves, own_sums = scatter_sums(halves, user_size, own_sums)
    gain_grad = halves[0][-8:].reshape(-1)[:col_width]
    expert_grad = jnp.concatenate([halves[0][:-8], halves[1]], axis=1)
    item_total = jnp.zeros((own_items, width), jnp.float32)
    for expert in range(experts_here):
        item_total = item_total + jnp.where(
            chosen[:, expert][:, None],
            lax.dot_general(
                own_sums,
                expert_w[expert],
                (((1,), (1,)), ((), ())),
                preferred_element_type=jnp.float32,
            ),
            0.0,
        )
    return (
        user_grad,
        item_total.astype(jnp.bfloat16)[None],
        expert_grad.reshape(experts_here, own_width, width),
        gain_grad,
    )


def solution(mesh):
    placed = (
        P("user", None),
        P("user", None),
        P(),
        P("item", "user", None),
        P("item", "user"),
        P("item", None, None),
        P("user", "item", None),
        P("user", "item", None, None, None),
        P("user", "item"),
    )
    return jax.shard_map(
        on_device,
        mesh=mesh,
        in_specs=placed,
        out_specs=(P("user", "item"), P("item", "user", None), P("item", "user", None), P("item")),
        check_vma=False,
    )
```

```python
import functools

import jax
import jax.numpy as jnp
from jax import lax
from jax.experimental import pallas as pl
from jax.experimental.pallas import tpu as pltpu
from jax.sharding import PartitionSpec as P

TILE = 128
SLOTS_PER_STEP = 8
HALVES = 2
ROW_CHUNKS = 4
BLOCK_ROWS = 256
MIB = 1024 * 1024


def place_tiles(item_blocks, place_ref, count_ref, level_ref, dense_ref):
    step = pl.program_id(0)

    @pl.when(step == 0)
    def _():
        dense_ref[...] = jnp.zeros_like(dense_ref)

    for offset in range(level_ref.shape[0]):
        slot = step * level_ref.shape[0] + offset

        @pl.when(slot < count_ref[0])
        def _():
            place = place_ref[slot]
            row = pl.multiple_of((place // item_blocks) * TILE, TILE)
            col = pl.multiple_of((place % item_blocks) * TILE, TILE)
            weights = level_ref[offset].astype(jnp.float32) * (1.0 / (2.0 * TILE))
            dense_ref[pl.ds(row, TILE), pl.ds(col, TILE)] = weights.astype(jnp.bfloat16)


def dense_tiles(place, count, level, users, items):
    slots = level.shape[0]
    per_step = SLOTS_PER_STEP if slots % SLOTS_PER_STEP == 0 else 1
    return pl.pallas_call(
        functools.partial(place_tiles, items // TILE),
        out_shape=jax.ShapeDtypeStruct((users, items), jnp.bfloat16),
        grid_spec=pltpu.PrefetchScalarGridSpec(
            num_scalar_prefetch=2,
            grid=(slots // per_step,),
            in_specs=[
                pl.BlockSpec((per_step, TILE, TILE), lambda step, place_ref, count_ref: (step, 0, 0))
            ],
            out_specs=pl.BlockSpec((users, items), lambda step, place_ref, count_ref: (0, 0)),
        ),
        compiler_params=pltpu.CompilerParams(
            dimension_semantics=("arbitrary",), vmem_limit_bytes=16 * MIB
        ),
        cost_estimate=pl.CostEstimate(
            flops=slots * TILE * TILE,
            bytes_accessed=slots * TILE * TILE * 4 + users * items * 2,
            transcendentals=0,
        ),
        name="place_tiles",
    )(place, count, level)


def project_own(first_ref, cats_ref, feat_ref, weight_ref, *rest):
    out_refs, total_ref = rest[:-1], rest[-1]
    expert = pl.program_id(0)
    own = feat_ref.shape[0]
    on_diagonal = lax.broadcasted_iota(jnp.int32, (own, own), 0) == lax.broadcasted_iota(
        jnp.int32, (own, own), 1
    )
    cats = jnp.sum(
        jnp.where(on_diagonal, cats_ref[...].astype(jnp.float32), 0.0), axis=1, keepdims=True
    )
    chosen = cats == (first_ref[0] + expert).astype(jnp.float32)
    part = jnp.dot(feat_ref[...], weight_ref[0], preferred_element_type=jnp.float32)
    part = jnp.where(chosen, part, 0.0)

    @pl.when(expert == 0)
    def _():
        total_ref[...] = part

    @pl.when(expert > 0)
    def _():
        total_ref[...] += part

    @pl.when(expert == pl.num_programs(0) - 1)
    def _():
        cols = out_refs[0].shape[1]
        for half, out_ref in enumerate(out_refs):
            out_ref[...] = total_ref[:, half * cols : (half + 1) * cols].astype(out_ref.dtype)


def own_queries(first_expert, cats, feat, weights):
    own, width = feat.shape
    experts = weights.shape[0]
    half = jax.ShapeDtypeStruct((own, width // HALVES), jnp.bfloat16)
    half_spec = pl.BlockSpec((own, width // HALVES), lambda expert, first_ref: (0, 0))
    return pl.pallas_call(
        project_own,
        out_shape=[half] * HALVES,
        grid_spec=pltpu.PrefetchScalarGridSpec(
            num_scalar_prefetch=1,
            grid=(experts,),
            in_specs=[
                pl.BlockSpec((1, own), lambda expert, first_ref: (0, 0)),
                pl.BlockSpec((own, width), lambda expert, first_ref: (0, 0)),
                pl.BlockSpec((1, width, width), lambda expert, first_ref: (expert, 0, 0)),
            ],
            out_specs=[half_spec] * HALVES,
            scratch_shapes=[pltpu.VMEM((own, width), jnp.float32)],
        ),
        compiler_params=pltpu.CompilerParams(dimension_semantics=("arbitrary",)),
        cost_estimate=pl.CostEstimate(
            flops=2 * own * width * width * experts,
            bytes_accessed=weights.size * 2 + own * width * 4,
            transcendentals=0,
        ),
        name="own_queries",
    )(first_expert.reshape(1), cats.reshape(1, own), feat, weights)


def spread(blocks, order_ref, *rest):
    source_refs, dense_ref, out_refs, next_ref, all_ref = rest[:4], rest[4], rest[5:-2], *rest[-2:]
    step = pl.program_id(0)

    @pl.when(step == 0)
    def _():
        for place in range(blocks):
            next_ref[place] = order_ref[place]
        own = all_ref.shape[0] // blocks
        for place in range(blocks):
            source = source_refs[4 * place // blocks]
            start = pl.multiple_of(order_ref[place] * own, own)
            all_ref[pl.ds(start, own)] = source[pl.ds((place % (blocks // 4)) * own, own)]

    product = jnp.dot(dense_ref[...], all_ref[...], preferred_element_type=jnp.float32)
    rows, first = product.shape[0], 0
    for out_ref in out_refs:
        chunks = out_ref.shape[0] // rows

        @pl.when((step >= first) & (step < first + chunks))
        def _():
            start = pl.multiple_of((step - first) * rows, rows)
            out_ref[pl.ds(start, rows)] = product.astype(out_ref.dtype)

        first += chunks


def spread_items(order, queries, dense, first, counts, rows):
    items = dense.shape[1]
    cols = queries[0].shape[1]
    blocks, chunks = order.shape[0], sum(counts)
    whole = lambda step, order_ref: (0, 0)
    return pl.pallas_call(
        functools.partial(spread, blocks),
        out_shape=[jax.ShapeDtypeStruct((count * rows, cols), jnp.bfloat16) for count in counts]
        + [jax.ShapeDtypeStruct((blocks,), jnp.int32)],
        grid_spec=pltpu.PrefetchScalarGridSpec(
            num_scalar_prefetch=1,
            grid=(chunks,),
            in_specs=[pl.BlockSpec(queries[0].shape, whole)] * 4
            + [pl.BlockSpec((rows, items), lambda step, order_ref: (first + step, 0))],
            out_specs=[pl.BlockSpec((count * rows, cols), whole) for count in counts]
            + [pl.BlockSpec(memory_space=pltpu.SMEM)],
            scratch_shapes=[pltpu.VMEM((items, cols), jnp.bfloat16)],
        ),
        compiler_params=pltpu.CompilerParams(
            dimension_semantics=("arbitrary",), vmem_limit_bytes=14 * MIB
        ),
        cost_estimate=pl.CostEstimate(
            flops=2 * chunks * rows * items * cols,
            bytes_accessed=chunks * rows * (items + cols) * 2 + items * cols * 2,
            transcendentals=0,
        ),
        name="spread_items",
    )(order, *queries, dense)


def norm_backward(pieces, user_ref, grad_ref, gain_ref, *rest):
    piece_refs, out_ref, term_ref = rest[: pieces * HALVES], rest[-2], rest[-1]
    summed = []
    for half in range(HALVES):
        total = piece_refs[half * pieces][...].astype(jnp.float32)
        for piece in range(1, pieces):
            total = total + piece_refs[half * pieces + piece][...].astype(jnp.float32)
        summed.append(total)
    width = out_ref.shape[1]
    pre_norm = user_ref[...].astype(jnp.float32) + jnp.concatenate(summed, axis=1)
    grad = grad_ref[...].astype(jnp.float32)
    scaled_grad = gain_ref[...] * grad
    inv_rms = lax.rsqrt(jnp.sum(pre_norm * pre_norm, axis=1, keepdims=True) / width + 1e-05)
    cross_mean = jnp.sum(scaled_grad * pre_norm, axis=1, keepdims=True) / width
    out_ref[...] = (
        inv_rms * scaled_grad - pre_norm * (inv_rms * inv_rms * inv_rms * cross_mean)
    ).astype(out_ref.dtype)
    term = jnp.sum(grad * pre_norm * inv_rms, axis=0, keepdims=True)

    @pl.when(pl.program_id(0) == 0)
    def _():
        term_ref[...] = term

    @pl.when(pl.program_id(0) > 0)
    def _():
        term_ref[...] += term


def user_gradient(user_feat, cotangent, gain, pieces, first, rows):
    width = user_feat.shape[1]
    block_rows = min(BLOCK_ROWS, rows)
    first_block = first // block_rows
    flat = [piece for half in pieces for piece in half]
    whole = pl.BlockSpec((block_rows, width), lambda step: (first_block + step, 0))
    part = pl.BlockSpec((block_rows, width // HALVES), lambda step: (step, 0))
    return pl.pallas_call(
        functools.partial(norm_backward, len(pieces[0])),
        out_shape=[
            jax.ShapeDtypeStruct((rows, width), jnp.bfloat16),
            jax.ShapeDtypeStruct((1, width), jnp.float32),
        ],
        grid=(rows // block_rows,),
        in_specs=[whole, whole, pl.BlockSpec((1, width), lambda step: (0, 0))] + [part] * len(flat),
        out_specs=[
            pl.BlockSpec((block_rows, width), lambda step: (step, 0)),
            pl.BlockSpec((1, width), lambda step: (0, 0)),
        ],
        compiler_params=pltpu.CompilerParams(
            dimension_semantics=("arbitrary",), vmem_limit_bytes=10 * MIB
        ),
        cost_estimate=pl.CostEstimate(
            flops=16 * rows * width,
            bytes_accessed=rows * width * 2 * (3 + len(pieces[0])),
            transcendentals=rows,
        ),
        name="user_gradient",
    )(user_feat, cotangent, gain.reshape(1, width), *flat)


def flip(value, size, bits):
    return lax.ppermute(value, "user", [(source, source ^ bits) for source in range(size)])


def gather_layers(own, size):
    return jnp.concatenate(
        [own] + [flip(own, size, 4 * layer) for layer in range(1, size // 4)], axis=0
    )


def gather_sides(own, size):
    other = flip(own, size, 2)
    return own, other, flip(own, size, 1), flip(other, size, 1)


def gather_order(size):
    layers = size // 4
    place = jnp.arange(size, dtype=jnp.int32)
    core, side, layer = place // (size // 2), (place // layers) % 2, place % layers
    return lax.axis_index("user") ^ (layer * 4 + side * 2 + core)


def scatter_sum(terms, size, order, beside=None):
    bits = size.bit_length() - 1
    index = lax.axis_index("user")
    left = list(reversed(range(bits)))
    if 0 in order:
        terms = terms.reshape((2,) * bits + terms.shape[1:])
    else:
        left.remove(0)
    for bit in order:
        axis = left.index(bit)
        left.remove(bit)
        mine = (index >> bit) & 1
        own = lax.dynamic_index_in_dim(terms, mine, axis, keepdims=False)
        away = lax.dynamic_index_in_dim(terms, 1 - mine, axis, keepdims=False)
        terms = own + flip(away.astype(jnp.bfloat16), size, 1 << bit).astype(jnp.float32)
        if beside is not None and len(left) == 2:
            terms, beside = lax.optimization_barrier((terms, beside))
    return terms, beside


def scatter_sums(halves, size, beside=None):
    bits = size.bit_length() - 1
    orders = [list(range(bits)), [0, 2, 1] + list(range(3, bits))]
    if beside is None:
        halves = [scatter_sum(terms, size, [0])[0] for terms in halves]
        halves = lax.optimization_barrier(tuple(halves))
        orders = [order[1:] for order in orders]
    first, _ = scatter_sum(halves[0], size, orders[0])
    second, beside = scatter_sum(halves[1], size, orders[1], beside)
    return [first, second], beside


def on_device(
    user_feat, cotangent, gain, item_feat, categories, expert_w, tile_place, tile_level, tile_count
):
    users, width = user_feat.shape
    user_size, item_size = lax.axis_size("user"), lax.axis_size("item")
    item_index = lax.axis_index("item")
    own_items = item_feat.shape[1]
    items = own_items * user_size
    experts_here = expert_w.shape[0]
    first_expert = item_index * experts_here
    own_cats, own_feat = categories[0], item_feat[0]
    rows, half_width = users // ROW_CHUNKS, width // HALVES

    own_halves = own_queries(first_expert, own_cats, own_feat, expert_w)
    order = gather_order(user_size)
    dense = dense_tiles(tile_place[0, 0], tile_count[0], tile_level[0, 0], users, items)
    layers = [gather_layers(own, user_size) for own in own_halves]
    queries = [gather_sides(part, user_size) for part in layers]

    partials = [[] for _ in range(HALVES)]
    for half in range(HALVES):
        for first, count in ((0, 1), (1, ROW_CHUNKS - 1)):
            *products, _ = spread_items(order, queries[half], dense, first, (1,) * count, rows)
            for product in products:
                pieces = [product]
                for shift in range(1, item_size):
                    pairs = [(source, (source + shift) % item_size) for source in range(item_size)]
                    pieces.append(lax.ppermute(product, "item", pairs))
                partials[half].append(pieces)
    grads, gain_term, item_terms = [None] * ROW_CHUNKS, 0.0, 0.0
    chunk_order = [0] + list(range(ROW_CHUNKS - 1, 0, -1))
    for chunk in chunk_order:
        grad, term = user_gradient(
            user_feat,
            cotangent,
            gain,
            [partials[half][chunk] for half in range(HALVES)],
            chunk * rows,
            rows,
        )
        grads[chunk] = grad
        gain_term = gain_term + term[0]
        if chunk != chunk_order[-1]:
            item_terms = item_terms + lax.dot_general(
                dense[chunk * rows : (chunk + 1) * rows],
                grad,
                (((0,), (0,)), ((), ())),
                preferred_element_type=jnp.float32,
            )
    col_width = width // item_size
    user_grad = jnp.concatenate(
        [lax.dynamic_slice_in_dim(grad, item_index * col_width, col_width, 1) for grad in grads],
        axis=0,
    )
    gain_own = lax.dynamic_slice_in_dim(gain_term, item_index * col_width, col_width, 0)

    halves = []
    for half in range(HALVES):
        part = slice(half * half_width, (half + 1) * half_width)
        terms = item_terms[:, part] + lax.dot_general(
            dense[chunk_order[-1] * rows : (chunk_order[-1] + 1) * rows],
            grads[chunk_order[-1]][:, part],
            (((0,), (0,)), ((), ())),
            preferred_element_type=jnp.float32,
        )
        halves.append(terms.reshape(user_size, own_items, half_width))
    sums = [half.astype(jnp.bfloat16) for half in scatter_sums(halves, user_size)[0]]
    own_sums = jnp.concatenate(sums, axis=1)

    chosen = own_cats[:, None] == first_expert + jnp.arange(experts_here, dtype=jnp.int32)[None, :]
    own_width = width // user_size
    left = jnp.where(
        chosen[:, None, :, None],
        own_feat.reshape(own_items, user_size, 1, own_width),
        jnp.zeros((), own_feat.dtype),
    ).reshape(own_items, -1)
    halves = [
        lax.dot_general(
            left, half, (((0,), (0,)), ((), ())), preferred_element_type=jnp.float32
        ).reshape(user_size, experts_here * own_width, half_width)
        for half in sums
    ]
    gain_rows = jnp.pad(gain_own, (0, 8 * half_width - col_width)).reshape(1, 8, half_width)
    gain_rows = jnp.broadcast_to(gain_rows, (user_size, 8, half_width))
    halves[0] = jnp.concatenate([halves[0], gain_rows], axis=1)
    halves, own_sums = scatter_sums(halves, user_size, own_sums)
    gain_grad = halves[0][-8:].reshape(-1)[:col_width]
    expert_grad = jnp.concatenate([halves[0][:-8], halves[1]], axis=1)
    item_total = jnp.zeros((own_items, width), jnp.float32)
    for expert in range(experts_here):
        item_total = item_total + jnp.where(
            chosen[:, expert][:, None],
            lax.dot_general(
                own_sums,
                expert_w[expert],
                (((1,), (1,)), ((), ())),
                preferred_element_type=jnp.float32,
            ),
            0.0,
        )
    return (
        user_grad,
        item_total.astype(jnp.bfloat16)[None],
        expert_grad.reshape(experts_here, own_width, width),
        gain_grad,
    )


def solution(mesh):
    placed = (
        P("user", None),
        P("user", None),
        P(),
        P("item", "user", None),
        P("item", "user"),
        P("item", None, None),
        P("user", "item", None),
        P("user", "item", None, None, None),
        P("user", "item"),
    )
    return jax.shard_map(
        on_device,
        mesh=mesh,
        in_specs=placed,
        out_specs=(P("user", "item"), P("item", "user", None), P("item", "user", None), P("item")),
        check_vma=False,
    )
```
